32 devices in a mesh: sensor: 16 (over z, y, core), tm: 2 (over x).
Axes of the slice: x: 2, y: 2, z: 4, core: 2. Of those that a mesh axis runs over, the one named last changes fastest.
Arguments:
- tokens: bfloat16 [2048, 32, 256], P(('sensor', 'tm')), may hold values from -6 to 6
- gain_time: float32 [256], replicated, may hold values from 0.1 to 1.9
- wq_time: bfloat16 [256, 256], replicated
- wkv_time: bfloat16 [256, 512], replicated
- wo_time: bfloat16 [256, 256], replicated, may hold values from -0.375 to 0.375
- gain_graph: float32 [256], replicated, may hold values from 0.1 to 1.9
- wq_graph: bfloat16 [256, 256], replicated
- wkv_graph: bfloat16 [256, 512], replicated
- wo_graph: bfloat16 [256, 256], replicated, may hold values from -0.375 to 0.375
- gain_ffn: float32 [256], replicated, may hold values from 0.1 to 1.9
- w_in: bfloat16 [256, 1024], replicated, may hold values from -0.375 to 0.375
- w_out: bfloat16 [1024, 256], replicated, may hold values from -0.1875 to 0.1875
- neighbour_blocks: int32 [16, 8], replicated, may hold values from 0 to 15, all different within a row
- slot_used_mask: int32 [16, 8], P('sensor'), may hold values 0 or 1
- neighbour_rows: int32 [16, 8, 4], replicated, may hold values from 0 to 127
Outputs:
- layer_out: bfloat16 [2048, 32, 256], P('sensor', 'tm')
The draws below stay inside these ranges and needn't reach their ends.
Inputs may be any that keep to these rules, and one draw needn't show every extreme that they name: `neighbour_blocks`: each row names 8 different sensor blocks, and every block is named by some row.
All inputs are finite; a program needn't handle non-finite values. No bound on the sum of `slot_used_mask` on one device may be relied on, other than what follows from the above.
Results may differ from the reference program's by a relative error of at most 0.0075.
Values may be sent and summed in bfloat16 or wider, within the bound.
No kernel may reach another device: no remote copies, remote signals or barrier semaphores. Data moves between devices by JAX's collectives and lax.ppermute only.
A program may use at most 64 MiB of HBM per device.

```python
import math
from functools import partial
import jax
import jax.numpy as jnp
from jax import lax

MODEL_DIMENSION = 256
H = 8
FF = 1024
SENSORS_PER_BLOCK = 128
REMOTE_SENSORS = 4
TIME_STEPS = 32
SENSOR_BLOCKS = 16
NEIGHBOUR_SLOTS = 8
SENSORS = 2048


def shared_keys(key, salt):
    return jax.random.normal(jax.random.fold_in(key, salt), (MODEL_DIMENSION, MODEL_DIMENSION), jnp.float32) * MODEL_DIMENSION ** (-0.5)


def query_weights(key, salt):
    noise = jax.random.normal(jax.random.fold_in(key, salt + 1), (MODEL_DIMENSION, MODEL_DIMENSION), jnp.float32) * MODEL_DIMENSION ** (-0.5)
    return noise.astype(jnp.bfloat16)


def key_value_weights(key, salt):
    base = shared_keys(key, salt)
    other = jax.random.normal(jax.random.fold_in(key, salt + 2), (MODEL_DIMENSION, MODEL_DIMENSION), jnp.float32) * MODEL_DIMENSION ** (-0.5)
    return jnp.concatenate([base, other], axis=1).astype(jnp.bfloat16)


def draw_wq_time(key, part):
    return query_weights(key, 1)


def draw_wkv_time(key, part):
    return key_value_weights(key, 1)


def draw_wq_graph(key, part):
    return query_weights(key, 11)


def draw_wkv_graph(key, part):
    return key_value_weights(key, 11)


def place_ends(drawn, rng, low, largest):
    longest = drawn.shape.index(max(drawn.shape))
    spots = []
    for shift in (0, 1):
        where = [jax.random.randint(jax.random.fold_in(rng, axis), (), 0, length) for axis, length in enumerate(drawn.shape)]
        where[longest] = (where[longest] + shift) % drawn.shape[longest]
        spots.append(tuple(where))
    return drawn.at[spots[0]].set(low).at[spots[1]].set(largest)


def block_scale(stream_key, dims, pieces, low, top_value):
    def one(axis_at, blocks):
        heights = jax.random.uniform(jax.random.fold_in(jax.random.fold_in(stream_key, 6), axis_at), (blocks,), jnp.float32, low / len(pieces), top_value / len(pieces))
        return jnp.repeat(jnp.exp(heights), dims[axis_at] // blocks).reshape((-1,) + (1,) * (len(dims) - axis_at - 1))

    factor_of = one(*pieces[0])
    for cut in pieces[1:]:
        factor_of = factor_of * one(*cut)
    return factor_of


def different_ones(rng, rows, count, top, lift):
    sequence = jax.random.permutation(jax.random.fold_in(rng, 1), count)
    favour = sequence
    for power in range(3):
        favour = favour * favour // count
    favour = favour * lift // count
    tickets = jax.random.randint(jax.random.fold_in(rng, 2), (rows, count), 0, 4096) + favour
    sure = jax.random.permutation(jax.random.fold_in(rng, 3), rows)[jnp.arange(count) % rows]
    tickets = jnp.where(jnp.arange(rows)[:, None] == sure[None, :], 1 << 14, tickets)
    priority = tickets * count + jnp.arange(count)
    return lax.top_k(priority.astype(jnp.int32), top)[1].astype(jnp.int32)


def gaussian(stream_key, shape, width, most, pieces=(), dtype=jnp.bfloat16):
    values = width * jax.random.normal(stream_key, shape, jnp.float32)
    if pieces:
        values = values * block_scale(stream_key, shape, pieces, -0.22, 0.18)
    return jnp.clip(values, -most, most).astype(dtype)


def setup_inputs(seed: int = 0) -> dict:
    key_list = jax.random.split(jax.random.key(seed), 16)
    tokens = gaussian(key_list[0], (SENSORS, TIME_STEPS, MODEL_DIMENSION), 1.0, 6.0, ((0, 32),))
    gain_time = jnp.clip(1.0 + 0.18 * jax.random.normal(key_list[1], (MODEL_DIMENSION,), jnp.float32), 0.1, 1.9)
    wq_time = draw_wq_time(jax.random.fold_in(key_list[15], 71), 0)
    wkv_time = draw_wkv_time(jax.random.fold_in(key_list[15], 71), 0)
    wo_time = gaussian(key_list[4], (MODEL_DIMENSION, MODEL_DIMENSION), MODEL_DIMENSION ** -0.5, 0.375)
    gain_graph = jnp.clip(1.0 + 0.18 * jax.random.normal(key_list[5], (MODEL_DIMENSION,), jnp.float32), 0.1, 1.9)
    wq_graph = draw_wq_graph(jax.random.fold_in(key_list[15], 71), 0)
    wkv_graph = draw_wkv_graph(jax.random.fold_in(key_list[15], 71), 0)
    wo_graph = gaussian(key_list[8], (MODEL_DIMENSION, MODEL_DIMENSION), MODEL_DIMENSION ** -0.5, 0.375)
    gain_ffn = jnp.clip(1.0 + 0.18 * jax.random.normal(key_list[9], (MODEL_DIMENSION,), jnp.float32), 0.1, 1.9)
    w_in = gaussian(key_list[10], (MODEL_DIMENSION, FF), MODEL_DIMENSION ** -0.5, 0.375)
    w_out = gaussian(key_list[11], (FF, MODEL_DIMENSION), FF ** -0.5, 0.1875)
    neighbour_blocks = different_ones(key_list[12], SENSOR_BLOCKS, SENSOR_BLOCKS, NEIGHBOUR_SLOTS, 8192)
    slot_used_mask = place_ends((jax.random.randint(key_list[13], (SENSOR_BLOCKS, NEIGHBOUR_SLOTS), 0, 8) < 7).astype(jnp.int32), jax.random.fold_in(key_list[13], 1), 0, 1)
    neighbour_rows = place_ends(jax.random.randint(key_list[14], (SENSOR_BLOCKS, NEIGHBOUR_SLOTS, REMOTE_SENSORS), 0, SENSORS_PER_BLOCK), jax.random.fold_in(key_list[14], 1), 0, SENSORS_PER_BLOCK - 1).astype(jnp.int32)
    return dict(tokens=tokens, gain_time=gain_time, wq_time=wq_time, wkv_time=wkv_time, wo_time=wo_time, gain_graph=gain_graph, wq_graph=wq_graph, wkv_graph=wkv_graph, wo_graph=wo_graph, gain_ffn=gain_ffn, w_in=w_in, w_out=w_out, neighbour_blocks=neighbour_blocks, slot_used_mask=slot_used_mask, neighbour_rows=neighbour_rows)


EPSILON = 1e-06

def rms_norm(values, gain_vec):
    widened = values.astype(jnp.float32)
    inverse = lax.rsqrt(lax.optimization_barrier(jnp.mean(widened * widened, axis=-1, keepdims=True)) + EPSILON)
    return (widened * inverse * gain_vec).astype(jnp.bfloat16)

def project(row_data, weight):
    flattened = row_data.reshape(-1, row_data.shape[-1])
    result = jnp.dot(flattened, weight, preferred_element_type=jnp.float32).astype(jnp.bfloat16)
    return result.reshape(row_data.shape[:-1] + (weight.shape[1],))

def softmax_bf16(scores, allowed):
    masked = jnp.where(allowed, scores, jnp.float32(-1e+30))
    highest = lax.optimization_barrier(jnp.max(masked, axis=-1, keepdims=True))
    exponent = jnp.exp(masked - highest)
    return (exponent / lax.optimization_barrier(jnp.sum(exponent, axis=-1, keepdims=True))).astype(jnp.bfloat16)

def time_block(sensor_rows, gain_time, wq_time, wkv_time, wo_time):
    sensors, time_len, model_width = sensor_rows.shape
    head_size = model_width // H
    normed = rms_norm(sensor_rows, gain_time)
    queries = project(normed, wq_time).reshape(sensors, time_len, H, head_size).astype(jnp.float32)
    key_val = project(normed, wkv_time)
    keys_all = key_val[..., :model_width].reshape(sensors, time_len, H, head_size).astype(jnp.float32)
    vals_all = key_val[..., model_width:].reshape(sensors, time_len, H, head_size).astype(jnp.float32)
    scores = jnp.einsum('stha,suha->shtu', queries, keys_all) / math.sqrt(head_size)
    positions = jnp.arange(time_len)
    causal = positions[None, :] <= positions[:, None]
    weights = softmax_bf16(scores, causal)
    context = jnp.einsum('shtu,suha->stha', weights.astype(jnp.float32), vals_all).astype(jnp.bfloat16)
    context = context.reshape(sensors * time_len, model_width)
    mixed_out = jnp.dot(context, wo_time, preferred_element_type=jnp.float32).reshape(sensor_rows.shape)
    return (sensor_rows.astype(jnp.float32) + mixed_out).astype(jnp.bfloat16)

def graph_block(h_rows, gathered_remote_rows, live_row, gain_graph, wq_graph, wkv_graph, wo_graph, gain_ffn, w_in, w_out):
    block_len, time_len, model_width = h_rows.shape
    head_size = model_width // H
    b_rows = rms_norm(h_rows, gain_graph)
    remote_normed = rms_norm(gathered_remote_rows, gain_graph)
    queries = project(b_rows, wq_graph).reshape(block_len, time_len, H, head_size).astype(jnp.float32)
    local_kv = project(b_rows, wkv_graph)
    remote_kv = project(remote_normed, wkv_graph)
    all_kv = jnp.concatenate([local_kv, remote_kv], axis=0)
    key_count = all_kv.shape[0]
    keys_all = all_kv[..., :model_width].reshape(key_count, time_len, H, head_size).astype(jnp.float32)
    vals_all = all_kv[..., model_width:].reshape(key_count, time_len, H, head_size).astype(jnp.float32)
    allowed = jnp.concatenate([jnp.ones((block_len,), jnp.bool_), jnp.repeat(live_row > 0, REMOTE_SENSORS)])
    scores = jnp.einsum('stha,utha->thsu', queries, keys_all) / math.sqrt(head_size)
    weights = softmax_bf16(scores, allowed)
    context = jnp.einsum('thsu,utha->stha', weights.astype(jnp.float32), vals_all).astype(jnp.bfloat16)
    context = context.reshape(block_len * time_len, model_width)
    after_graph = h_rows.astype(jnp.float32) + jnp.dot(context, wo_graph, preferred_element_type=jnp.float32).reshape(h_rows.shape)
    normed_ffn = rms_norm(after_graph, gain_ffn).reshape(-1, model_width)
    hidden = jax.nn.gelu(jnp.dot(normed_ffn, w_in, preferred_element_type=jnp.float32)).astype(jnp.bfloat16)
    return (after_graph + jnp.dot(hidden, w_out, preferred_element_type=jnp.float32).reshape(h_rows.shape)).astype(jnp.bfloat16)

def reference(tokens, gain_time, wq_time, wkv_time, wo_time, gain_graph, wq_graph, wkv_graph, wo_graph, gain_ffn, w_in, w_out, neighbour_blocks, slot_used_mask, neighbour_rows):
    blocked = tokens.reshape(SENSOR_BLOCKS, SENSORS_PER_BLOCK, TIME_STEPS, MODEL_DIMENSION)
    temporal_output = lax.map(partial(time_block, gain_time=gain_time, wq_time=wq_time, wkv_time=wkv_time, wo_time=wo_time), blocked)

    def one_block(carried):
        h_rows, neighbour_block_ids, live_row, neighbour_row_ids = carried
        gathered_remote_rows = temporal_output[neighbour_block_ids[:, None], neighbour_row_ids].reshape(NEIGHBOUR_SLOTS * REMOTE_SENSORS, TIME_STEPS, MODEL_DIMENSION)
        return graph_block(h_rows, gathered_remote_rows, live_row, gain_graph, wq_graph, wkv_graph, wo_graph, gain_ffn, w_in, w_out)
    result = lax.map(one_block, (temporal_output, neighbour_blocks, slot_used_mask, neighbour_rows))
    return result.reshape(SENSORS, TIME_STEPS, MODEL_DIMENSION)
```

```python
import functools
import math

import jax
import jax.numpy as jnp
from jax import lax
from jax.experimental import pallas as pl
from jax.experimental.pallas import tpu as pltpu
from jax.sharding import PartitionSpec as P

H = 8
HEAD = 32
REMOTE_SENSORS = 4
EPSILON = 1e-06
NEG = -1e30
SCALE = math.log2(math.e) / math.sqrt(HEAD)
F32 = jnp.float32
BF16 = jnp.bfloat16
VMEM_LIMIT = 48 * 1024 * 1024


def dot(a, b):
    return jnp.dot(a, b, preferred_element_type=F32)


def dot_nt(a, b):
    return lax.dot_general(a, b, (((1,), (1,)), ((), ())), preferred_element_type=F32)


def dot_tn(a, b):
    return lax.dot_general(a, b, (((0,), (0,)), ((), ())), preferred_element_type=F32)


def rms(x, gain):
    inverse = lax.rsqrt(jnp.mean(x * x, axis=-1, keepdims=True) + EPSILON)
    return (x * inverse * gain).astype(BF16)


def swap16():
    row = lax.broadcasted_iota(jnp.int32, (256, 256), 0)
    col = lax.broadcasted_iota(jnp.int32, (256, 256), 1)
    return (col == ((row & 15) << 4) + (row >> 4)).astype(BF16)


def head_rows(rows, lanes, head_of_row, first_head):
    row = lax.broadcasted_iota(jnp.int32, (rows, lanes), 0)
    lane = lax.broadcasted_iota(jnp.int32, (rows, lanes), 1)
    return (lane // HEAD + first_head == row // head_of_row).astype(BF16)


def time_kernel(split, my_ref, x_ref, gain_ref, wq_ref, wkv_ref, wo_ref, *refs):
    if split:
        keep_ref, send_ref, q_s, k_s, v_s, c_s, after_s = refs
    else:
        out_ref, q_s, k_s, v_s, c_s = refs
    sensors, steps, width = x_ref.shape
    rows = sensors * steps
    x = x_ref[...].reshape(rows, width).astype(F32)
    normed = rms(x, gain_ref[...])
    q_s[...] = dot(normed, wq_ref[...]).astype(BF16)
    kv = dot(normed, wkv_ref[...]).astype(BF16)
    k_s[...] = kv[:, :width]
    v_s[...] = kv[:, width:]
    lanes = H * steps
    mask = head_rows(lanes, width, steps, 0)
    key_t = lax.broadcasted_iota(jnp.int32, (steps, lanes), 0)
    query_t = lax.broadcasted_iota(jnp.int32, (steps, lanes), 1) & (steps - 1)
    causal = key_t <= query_t
    half_heads = 128 // HEAD
    lane_head = lax.broadcasted_iota(jnp.int32, (steps, 128), 1) // HEAD
    for s in range(sensors):
        here = slice(s * steps, (s + 1) * steps)
        spread = jnp.concatenate([q_s[here, :]] * H, axis=0) * mask
        scores = dot_nt(k_s[here, :], spread)
        scores = jnp.where(causal, scores, NEG)
        top = jnp.max(scores, axis=0, keepdims=True)
        e = jnp.exp2((scores - top) * SCALE)
        attn = (e * (1.0 / jnp.sum(e, axis=0, keepdims=True))).astype(BF16)
        for half in range(width // 128):
            cols = slice(half * 128, (half + 1) * 128)
            span = half_heads * steps
            wide = dot_tn(attn[:, half * span : (half + 1) * span], v_s[here, cols])
            ctx = wide[:steps]
            for h in range(1, half_heads):
                ctx = jnp.where(lane_head == h, wide[h * steps : (h + 1) * steps], ctx)
            c_s[here, cols] = ctx.astype(BF16)
    after = (x + dot(c_s[...], wo_ref[...])).astype(BF16)
    if not split:
        out_ref[...] = after.reshape(sensors, steps, width)
        return
    after_s[...] = after.reshape(sensors, steps, width)
    order = swap16()
    mine = my_ref[0]
    for ref, part in ((keep_ref, mine), (send_ref, 1 - mine)):
        rows16 = after_s[:, pl.ds(pl.multiple_of(part * 16, 16), 16), :]
        for b in range(sensors // 16):
            block = rows16[b * 16 : (b + 1) * 16].reshape(256, width)
            ref[:, b * 16 : (b + 1) * 16, :] = dot(order, block).astype(BF16).reshape(16, 16, width)


def time_block(tokens, my, gain, wq, wkv, wo, first, count, split):
    steps, width = tokens.shape[1:]
    sb = min(16, count)
    rows = sb * steps
    full = lambda a: pl.BlockSpec(a.shape, lambda i, *_: (0,) * a.ndim)
    if split:
        out_shape = [jax.ShapeDtypeStruct((16, count, width), BF16)] * 2
        out_specs = [pl.BlockSpec((16, sb, width), lambda i, *_: (0, i, 0))] * 2
        extra = [pltpu.VMEM((sb, steps, width), BF16)]
    else:
        out_shape = jax.ShapeDtypeStruct((count, steps, width), BF16)
        out_specs = pl.BlockSpec((sb, steps, width), lambda i, *_: (i, 0, 0))
        extra = []
    return pl.pallas_call(
        functools.partial(time_kernel, split),
        out_shape=out_shape,
        grid_spec=pltpu.PrefetchScalarGridSpec(
            num_scalar_prefetch=1,
            grid=(count // sb,),
            in_specs=[
                pl.BlockSpec((sb, steps, width), lambda i, *_: (first // sb + i, 0, 0)),
                full(gain),
                full(wq),
                full(wkv),
                full(wo),
            ],
            out_specs=out_specs,
            scratch_shapes=[pltpu.VMEM((rows, width), BF16)] * 4 + extra,
        ),
        compiler_params=pltpu.CompilerParams(vmem_limit_bytes=VMEM_LIMIT),
        cost_estimate=pl.CostEstimate(
            flops=count * steps * width * width * 12, bytes_accessed=count * steps * width * 4, transcendentals=0
        ),
        name="time_block",
    )(my, tokens, gain, wq, wkv, wo)


def pick_kernel(n, pick_ref, *refs):
    pieces, (out_ref, o_s) = refs[:n], refs[n:]
    steps = out_ref.shape[1]
    wanted = out_ref.shape[0]
    order = swap16()
    pick = pick_ref[...]
    for t in range(steps):
        rows = jnp.concatenate([p[t] for p in pieces], axis=0)
        o_s[t] = dot(pick, rows).astype(BF16)
    for b in range(wanted // 16):
        block = o_s[:, b * 16 : (b + 1) * 16, :].reshape(256, 256)
        out_ref[b * 16 : (b + 1) * 16] = dot(order, block).astype(BF16).reshape(16, 16, 256)


def pick_rows(pick, pieces):
    steps, _, width = pieces[0].shape
    wanted = pick.shape[0]
    return pl.pallas_call(
        functools.partial(pick_kernel, len(pieces)),
        out_shape=jax.ShapeDtypeStruct((wanted, steps, width), BF16),
        scratch_shapes=[pltpu.VMEM((steps, wanted, width), BF16)],
        compiler_params=pltpu.CompilerParams(vmem_limit_bytes=VMEM_LIMIT),
        name="pick_rows",
    )(pick, *pieces)


def local_kernel(n, *refs):
    pieces = refs[:n]
    gain_ref, wq_ref, wkv_ref, q_ref, ctx_ref, top_ref, sum_ref, wvt_ref = refs[n:]
    tb, block, width = q_ref.shape

    @pl.when(pl.program_id(0) == 0)
    def _():
        wvt_ref[...] = wkv_ref[:, width:].astype(F32).T.astype(BF16)

    x = jnp.concatenate([p[t] for t in range(tb) for p in pieces], axis=0).astype(F32)
    normed = rms(x, gain_ref[...])
    q = dot(normed, wq_ref[...]).astype(BF16)
    k = dot(normed, wkv_ref[:, :width]).astype(BF16)
    q_ref[...] = q.reshape(tb, block, width)
    masks = [head_rows(2 * block, 128, block, -2 * p) for p in range(2)]
    for t in range(tb):
        here = slice(t * block, (t + 1) * block)
        vt = dot_nt(wvt_ref[...], normed[here]).astype(BF16)
        for pair in range(H // 2):
            cols = slice(pair // 2 * 128, pair // 2 * 128 + 128)
            qh = q[here, cols]
            spread = jnp.concatenate([qh, qh], axis=0) * masks[pair % 2]
            scores = dot_nt(k[here, cols], spread)
            top = jnp.max(scores, axis=0, keepdims=True)
            e = jnp.exp2((scores - top) * SCALE)
            total = jnp.sum(e, axis=0, keepdims=True)
            lo = pair * 2 * HEAD
            both = dot(vt[lo : lo + 2 * HEAD], e.astype(BF16))
            for i in range(2):
                lanes = slice(i * block, (i + 1) * block)
                ctx_ref[t, lo + i * HEAD : lo + (i + 1) * HEAD, :] = both[i * HEAD : (i + 1) * HEAD, lanes]
                top_ref[t, 2 * pair + i : 2 * pair + i + 1, :] = top[:, lanes]
                sum_ref[t, 2 * pair + i : 2 * pair + i + 1, :] = total[:, lanes]


def local_part(pieces, gain, wq, wkv):
    steps, _, width = pieces[0].shape
    block = sum(p.shape[1] for p in pieces)
    tb = 2
    full = lambda a: pl.BlockSpec(a.shape, lambda i: (0,) * a.ndim)
    per_t = lambda *shape: pl.BlockSpec((tb,) + shape, lambda i: (i, 0, 0))
    return pl.pallas_call(
        functools.partial(local_kernel, len(pieces)),
        out_shape=[
            jax.ShapeDtypeStruct((steps, block, width), BF16),
            jax.ShapeDtypeStruct((steps, width, block), F32),
            jax.ShapeDtypeStruct((steps, H, block), F32),
            jax.ShapeDtypeStruct((steps, H, block), F32),
            jax.ShapeDtypeStruct((width, width), BF16),
        ],
        grid=(steps // tb,),
        in_specs=[per_t(p.shape[1], width) for p in pieces] + [full(gain), full(wq), full(wkv)],
        out_specs=[
            per_t(block, width),
            per_t(width, block),
            per_t(H, block),
            per_t(H, block),
            pl.BlockSpec((width, width), lambda i: (0, 0)),
        ],
        compiler_params=pltpu.CompilerParams(vmem_limit_bytes=VMEM_LIMIT),
        cost_estimate=pl.CostEstimate(
            flops=steps * block * width * width * 12, bytes_accessed=steps * block * width * 10, transcendentals=0
        ),
        name="local_keys",
    )(*pieces, gain, wq, wkv)


def gelu(x):
    inner = x * (0.7978845608028654 + 0.035677408136300125 * (x * x))
    half = 0.5 * x
    return half + half * jnp.tanh(inner)


def finish_kernel(n, split, own_ref, *refs):
    pieces = refs[:n]
    (in_ref, live_ref, q_ref, lctx_ref, ltop_ref, lsum_ref, gain_ref, wk_ref, wvt_ref, wo_ref, gain_ffn_ref,
     w_in_ref, w_out_ref, out_ref, rn_s, rk_s, ctx_s, y_s, pick_s) = refs[n:]
    tb, block, width = q_ref.shape
    steps, remote = rn_s.shape[:2]
    step = pl.program_id(0)

    @pl.when(step == 0)
    def _():
        if split:
            order = swap16()
            for j in range(remote // REMOTE_SENSORS):
                pick_s[j * REMOTE_SENSORS : (j + 1) * REMOTE_SENSORS] = in_ref[own_ref[j]]
            for b in range(remote // 16):
                rows = pick_s[b * 16 : (b + 1) * 16].reshape(256, width)
                rn_s[:, b * 16 : (b + 1) * 16, :] = dot(order, rows).astype(BF16).reshape(16, 16, width)
            raw = rn_s[...]
        else:
            raw = in_ref[...]
        normed = rms(raw.reshape(steps * remote, width).astype(F32), gain_ref[...])
        rn_s[...] = normed.reshape(steps, remote, width)
        rk_s[...] = dot(normed, wk_ref[...]).astype(BF16).reshape(steps, remote, width)

    live = live_ref[...] > 0
    masks = [head_rows(2 * block, 128, block, -2 * p) for p in range(2)]
    rows = []
    for t in range(tb):
        at = step * tb + t
        rk = rk_s[at]
        vt = dot_nt(wvt_ref[...], rn_s[at]).astype(BF16)
        for pair in range(H // 2):
            cols = slice(pair // 2 * 128, pair // 2 * 128 + 128)
            qh = q_ref[t, :, cols]
            spread = jnp.concatenate([qh, qh], axis=0) * masks[pair % 2]
            scores = jnp.where(live, dot_nt(rk[:, cols], spread), NEG)
            pick = lambda ref: jnp.concatenate(
                [ref[t, 2 * pair : 2 * pair + 1, :], ref[t, 2 * pair + 1 : 2 * pair + 2, :]], axis=1
            )
            ltop = pick(ltop_ref)
            top = jnp.maximum(jnp.max(scores, axis=0, keepdims=True), ltop)
            e = jnp.exp2((scores - top) * SCALE)
            keep = jnp.exp2((ltop - top) * SCALE)
            inverse = 1.0 / (jnp.sum(e, axis=0, keepdims=True) + pick(lsum_ref) * keep)
            keep = keep * inverse
            lo = pair * 2 * HEAD
            both = dot(vt[lo : lo + 2 * HEAD], (e * inverse).astype(BF16))
            for i in range(2):
                lanes = slice(i * block, (i + 1) * block)
                dims = slice(lo + i * HEAD, lo + (i + 1) * HEAD)
                merged = lctx_ref[t, dims, :] * keep[:, lanes] + both[i * HEAD : (i + 1) * HEAD, lanes]
                ctx_s[dims, t * block : (t + 1) * block] = merged.astype(BF16)
        rows += [p[t] for p in pieces]
    after = jnp.concatenate(rows, axis=0).astype(F32) + dot_tn(ctx_s[...], wo_ref[...])
    normed = rms(after, gain_ffn_ref[...])
    hidden = gelu(dot(normed, w_in_ref[...])).astype(BF16)
    y = (after + dot(hidden, w_out_ref[...])).astype(BF16).reshape(tb, block, width)
    if not split:
        out_ref[...] = y
        return
    y_s[pl.ds(step * tb, tb)] = y

    @pl.when(step == pl.num_programs(0) - 1)
    def _():
        order = swap16()
        mine = own_ref[own_ref.shape[0] - 1]
        half = block // 2
        for b in range(block // 16):
            first = b * 16
            owner = mine if first < half else 1 - mine
            rows = y_s[:, first : first + 16, :].reshape(256, width)
            at = owner * half + first % half
            out_ref[pl.ds(at, 16)] = dot(order, rows).astype(BF16).reshape(16, 16, width)


def finish(own, pieces, incoming, live, local, gain, wkv, wo, gain_ffn, w_in, w_out, split):
    q, lctx, ltop, lsum, wvt = local
    steps, block, width = q.shape
    remote = live.shape[0]
    tb = 2
    full = lambda a: pl.BlockSpec(a.shape, lambda i, *_: (0,) * a.ndim)
    per_t = lambda *shape: pl.BlockSpec((tb,) + shape, lambda i, *_: (i, 0, 0))
    if split:
        out_shape = jax.ShapeDtypeStruct((block, steps, width), BF16)
        out_specs = pl.BlockSpec((block, steps, width), lambda i, *_: (0, 0, 0))
    else:
        out_shape = jax.ShapeDtypeStruct((steps, block, width), BF16)
        out_specs = per_t(block, width)
    return pl.pallas_call(
        functools.partial(finish_kernel, len(pieces), split),
        out_shape=out_shape,
        grid_spec=pltpu.PrefetchScalarGridSpec(
            num_scalar_prefetch=1,
            grid=(steps // tb,),
            in_specs=[per_t(p.shape[1], width) for p in pieces]
            + [
                full(incoming),
                full(live),
                per_t(block, width),
                per_t(width, block),
                per_t(H, block),
                per_t(H, block),
                full(gain),
                pl.BlockSpec((width, width), lambda i, *_: (0, 0)),
                full(wvt),
                full(wo),
                full(gain_ffn),
                full(w_in),
                full(w_out),
            ],
            out_specs=out_specs,
            scratch_shapes=[
                pltpu.VMEM((steps, remote, width), BF16),
                pltpu.VMEM((steps, remote, width), BF16),
                pltpu.VMEM((width, tb * block), BF16),
                pltpu.VMEM((steps, block, width), BF16),
                pltpu.VMEM((remote, steps, width), BF16),
            ],
        ),
        compiler_params=pltpu.CompilerParams(vmem_limit_bytes=VMEM_LIMIT),
        cost_estimate=pl.CostEstimate(
            flops=steps * block * width * width * 18, bytes_accessed=steps * block * width * 12, transcendentals=0
        ),
        name="remote_keys_and_feed_forward",
    )(own, *pieces, incoming, live, q, lctx, ltop, lsum, gain, wkv, wvt, wo, gain_ffn, w_in, w_out)


def local(
    tm,
    tokens,
    gain_time,
    wq_time,
    wkv_time,
    wo_time,
    gain_graph,
    wq_graph,
    wkv_graph,
    wo_graph,
    gain_ffn,
    w_in,
    w_out,
    neighbour_blocks,
    slot_used_mask,
    neighbour_rows,
):
    sensors_here, steps, width = tokens.shape
    block = sensors_here * tm
    group = steps // tm
    block_count, slots = neighbour_blocks.shape
    split = tm == 2 and group == 16 and sensors_here % 32 == 0
    gain_time, gain_graph, gain_ffn = (g.reshape(1, width) for g in (gain_time, gain_graph, gain_ffn))
    mine = lax.axis_index("tm").astype(jnp.int32)
    block_index = lax.axis_index("sensor")
    time = functools.partial(time_block, tokens, mine.reshape(1), gain_time, wq_time, wkv_time, wo_time)
    if split:
        chunks = 2
        size = sensors_here // chunks
        kept, got = [], []
        for c in range(chunks):
            keep, send = time(c * size, size, True)
            kept.append(keep)
            got.append(lax.ppermute(send, "tm", [(0, 1), (1, 0)]))
        pieces = kept + got
    else:
        whole = lax.all_to_all(time(0, sensors_here, False), "tm", split_axis=1, concat_axis=0, tiled=True)
        pieces = [whole.transpose(1, 0, 2)]
    matches = (neighbour_blocks == block_index).astype(jnp.int32)
    wanted = jnp.sum(matches[:, :, None] * neighbour_rows, axis=1).reshape(-1)
    own = lax.dynamic_index_in_dim(neighbour_blocks, block_index, 0, keepdims=False)
    live = jnp.broadcast_to(jnp.repeat(slot_used_mask[0], REMOTE_SENSORS)[:, None], (slots * REMOTE_SENSORS, 2 * block))
    if split:
        place = (jnp.arange(block) + mine * sensors_here) % block
        pick = (wanted[:, None] == place[None, :]).astype(BF16)
        outgoing = pick_rows(pick, pieces)
    else:
        outgoing = jnp.take(whole, wanted, axis=0)
    outgoing = outgoing.reshape(block_count, REMOTE_SENSORS, group, width)
    incoming = lax.all_to_all(outgoing, "sensor", split_axis=0, concat_axis=0, tiled=True)
    if not split:
        incoming = jnp.take(incoming, own, axis=0).reshape(-1, group, width).transpose(1, 0, 2)
    near = local_part(pieces, gain_graph, wq_graph, wkv_graph)
    numbers = jnp.concatenate([own.astype(jnp.int32), mine.reshape(1)])
    out = finish(numbers, pieces, incoming, live, near, gain_graph, wkv_graph, wo_graph, gain_ffn, w_in, w_out, split)
    return out if split else out.transpose(1, 0, 2)


def solution(mesh):
    in_specs = (
        P(("sensor", "tm"), None, None),
        P(),
        P(),
        P(),
        P(),
        P(),
        P(),
        P(),
        P(),
        P(),
        P(),
        P(),
        P(),
        P("sensor", None),
        P(),
    )
    out_specs = P("sensor", "tm", None)
    body = functools.partial(local, mesh.shape["tm"])
    return jax.shard_map(body, mesh=mesh, in_specs=in_specs, out_specs=out_specs, check_vma=False)
```

```python
import functools
import math

import jax
import jax.numpy as jnp
from jax import lax
from jax.experimental import pallas as pl
from jax.experimental.pallas import tpu as pltpu
from jax.sharding import PartitionSpec as P

H = 8
HEAD = 32
REMOTE_SENSORS = 4
EPSILON = 1e-06
NEG = -1e30
SCALE = math.log2(math.e) / math.sqrt(HEAD)
F32 = jnp.float32
BF16 = jnp.bfloat16
VMEM_LIMIT = 60 * 1024 * 1024


def dot(a, b):
    return jnp.dot(a, b, preferred_element_type=F32)


def dot_nt(a, b):
    return lax.dot_general(a, b, (((1,), (1,)), ((), ())), preferred_element_type=F32)


def dot_tn(a, b):
    return lax.dot_general(a, b, (((0,), (0,)), ((), ())), preferred_element_type=F32)


def rms(x, gain):
    inverse = lax.rsqrt(jnp.mean(x * x, axis=-1, keepdims=True) + EPSILON)
    return (x * inverse * gain).astype(BF16)


def swap16():
    row = lax.broadcasted_iota(jnp.int32, (256, 256), 0)
    col = lax.broadcasted_iota(jnp.int32, (256, 256), 1)
    return (col == ((row & 15) << 4) + (row >> 4)).astype(BF16)


def head_rows(rows, lanes, head_of_row, first_head):
    row = lax.broadcasted_iota(jnp.int32, (rows, lanes), 0)
    lane = lax.broadcasted_iota(jnp.int32, (rows, lanes), 1)
    return (lane // HEAD + first_head == row // head_of_row).astype(BF16)


def time_kernel(split, my_ref, x_ref, gain_ref, wq_ref, wkv_ref, wo_ref, *refs):
    if split:
        keep_ref, send_ref, q_s, k_s, v_s, a_s, c_s, after_s = refs
    else:
        out_ref, q_s, k_s, v_s, a_s, c_s = refs
    sensors, steps, width = x_ref.shape
    rows = sensors * steps
    x = x_ref[...].reshape(rows, width).astype(F32)
    normed = rms(x, gain_ref[...])
    q_s[...] = dot(normed, wq_ref[...]).astype(BF16)
    kv = dot(normed, wkv_ref[...]).astype(BF16)
    k_s[...] = kv[:, :width]
    v_s[...] = kv[:, width:]
    lanes = H * steps
    near = 128 // HEAD
    span = near * steps
    mask = head_rows(span, 128, steps, 0)
    none = jnp.zeros((span, 128), BF16)
    key_t = lax.broadcasted_iota(jnp.int32, (steps, lanes), 0)
    query_t = lax.broadcasted_iota(jnp.int32, (steps, lanes), 1) & (steps - 1)
    causal = key_t <= query_t
    for s in range(sensors):
        here = slice(s * steps, (s + 1) * steps)
        first, second = (jnp.concatenate([q_s[here, c : c + 128]] * near, axis=0) * mask for c in (0, 128))
        spread = jnp.concatenate(
            [jnp.concatenate([first, none], axis=1), jnp.concatenate([none, second], axis=1)], axis=0
        )
        scores = jnp.where(causal, dot_nt(k_s[here, :], spread), NEG)
        top = jnp.max(scores, axis=0, keepdims=True)
        e = jnp.exp2((scores - top) * SCALE)
        a_s[here, :] = (e * (1.0 / jnp.sum(e, axis=0, keepdims=True))).astype(BF16)
    lane_head = lax.broadcasted_iota(jnp.int32, (steps, 128), 1) // HEAD
    for g in range(rows // 128):
        turned = a_s[g * 128 : (g + 1) * 128, :].T
        for half in range(2):
            cols = slice(half * 128, (half + 1) * 128)
            for s in range(0, 128 // steps, 2):
                columns = []
                for r in (s, s + 1):
                    v = v_s[g * 128 + r * steps : g * 128 + (r + 1) * steps, cols]
                    parts = [jnp.zeros((r * steps, 128), BF16), v, jnp.zeros((128 - (r + 1) * steps, 128), BF16)]
                    columns.append(jnp.concatenate([p for p in parts if p.shape[0]], axis=0))
                wide = dot(turned[half * span : (half + 1) * span], jnp.concatenate(columns, axis=1))
                for i in range(2):
                    ctx = wide[:steps, i * 128 : (i + 1) * 128]
                    for h in range(1, near):
                        ctx = jnp.where(lane_head == h, wide[h * steps : (h + 1) * steps, i * 128 : (i + 1) * 128], ctx)
                    at = g * 128 + (s + i) * steps
                    c_s[at : at + steps, cols] = ctx.astype(BF16)
    after = (x + dot(c_s[...], wo_ref[...])).astype(BF16)
    if not split:
        out_ref[...] = after.reshape(sensors, steps, width)
        return
    after_s[...] = after.reshape(sensors, steps, width)
    order = swap16()
    mine = my_ref[0]
    for ref, part in ((keep_ref, mine), (send_ref, 1 - mine)):
        rows16 = after_s[:, pl.ds(pl.multiple_of(part * 16, 16), 16), :]
        for b in range(sensors // 16):
            block = rows16[b * 16 : (b + 1) * 16].reshape(256, width)
            ref[:, b * 16 : (b + 1) * 16, :] = dot(order, block).astype(BF16).reshape(16, 16, width)


def time_block(tokens, my, gain, wq, wkv, wo, first, count, split):
    steps, width = tokens.shape[1:]
    sb = min(16, count)
    rows = sb * steps
    full = lambda a: pl.BlockSpec(a.shape, lambda i, *_: (0,) * a.ndim)
    if split:
        out_shape = [jax.ShapeDtypeStruct((16, count, width), BF16)] * 2
        out_specs = [pl.BlockSpec((16, sb, width), lambda i, *_: (0, i, 0))] * 2
        extra = [pltpu.VMEM((sb, steps, width), BF16)]
    else:
        out_shape = jax.ShapeDtypeStruct((count, steps, width), BF16)
        out_specs = pl.BlockSpec((sb, steps, width), lambda i, *_: (i, 0, 0))
        extra = []
    return pl.pallas_call(
        functools.partial(time_kernel, split),
        out_shape=out_shape,
        grid_spec=pltpu.PrefetchScalarGridSpec(
            num_scalar_prefetch=1,
            grid=(count // sb,),
            in_specs=[
                pl.BlockSpec((sb, steps, width), lambda i, *_: (first // sb + i, 0, 0)),
                full(gain),
                full(wq),
                full(wkv),
                full(wo),
            ],
            out_specs=out_specs,
            scratch_shapes=[pltpu.VMEM((rows, width), BF16)] * 5 + extra,
        ),
        compiler_params=pltpu.CompilerParams(vmem_limit_bytes=VMEM_LIMIT),
        cost_estimate=pl.CostEstimate(
            flops=count * steps * width * width * 12, bytes_accessed=count * steps * width * 4, transcendentals=0
        ),
        name="time_block",
    )(my, tokens, gain, wq, wkv, wo)


def pick_kernel(n, pick_ref, *refs):
    pieces, (out_ref, o_s) = refs[:n], refs[n:]
    steps = out_ref.shape[1]
    wanted = out_ref.shape[0]
    order = swap16()
    pick = pick_ref[...]
    for t in range(steps):
        rows = jnp.concatenate([p[t] for p in pieces], axis=0)
        o_s[t] = dot(pick, rows).astype(BF16)
    for b in range(wanted // 16):
        block = o_s[:, b * 16 : (b + 1) * 16, :].reshape(256, 256)
        out_ref[b * 16 : (b + 1) * 16] = dot(order, block).astype(BF16).reshape(16, 16, 256)


def pick_rows(pick, pieces):
    steps, _, width = pieces[0].shape
    wanted = pick.shape[0]
    return pl.pallas_call(
        functools.partial(pick_kernel, len(pieces)),
        out_shape=jax.ShapeDtypeStruct((wanted, steps, width), BF16),
        scratch_shapes=[pltpu.VMEM((steps, wanted, width), BF16)],
        compiler_params=pltpu.CompilerParams(vmem_limit_bytes=VMEM_LIMIT),
        name="pick_rows",
    )(pick, *pieces)


def pair_scores(q, k, masks, pair):
    cols = slice(pair // 2 * 128, pair // 2 * 128 + 128)
    spread = jnp.concatenate([q[:, cols]] * 2, axis=0) * masks[pair % 2]
    return dot_nt(k[:, cols], spread)


def local_kernel(n, *refs):
    pieces = refs[:n]
    gain_ref, wq_ref, wkv_ref, q_ref, ctx_ref, top_ref, sum_ref, wvt_ref = refs[n:]
    tb, block, width = q_ref.shape

    @pl.when(pl.program_id(0) == 0)
    def _():
        wvt_ref[...] = wkv_ref[:, width:].astype(F32).T.astype(BF16)

    x = jnp.concatenate([p[t] for t in range(tb) for p in pieces], axis=0).astype(F32)
    normed = rms(x, gain_ref[...])
    q = dot(normed, wq_ref[...]).astype(BF16)
    k = dot(normed, wkv_ref[:, :width]).astype(BF16)
    q_ref[...] = q.reshape(tb, block, width)
    masks = [head_rows(2 * block, 128, block, -2 * p) for p in range(2)]
    for t in range(tb):
        here = slice(t * block, (t + 1) * block)
        vt = dot_nt(wvt_ref[...], normed[here]).astype(BF16)
        scores = [pair_scores(q[here], k[here], masks, pair) for pair in range(H // 2)]
        tops = [jnp.max(x, axis=0, keepdims=True) for x in scores]
        es = [jnp.exp2((x - top) * SCALE) for x, top in zip(scores, tops)]
        top_ref[t] = jnp.concatenate(tops, axis=1)
        sum_ref[t] = jnp.concatenate([jnp.sum(e, axis=0, keepdims=True) for e in es], axis=1)
        for pair, e in enumerate(es):
            lo = pair * 2 * HEAD
            both = dot(vt[lo : lo + 2 * HEAD], e.astype(BF16))
            for i in range(2):
                lanes = slice(i * block, (i + 1) * block)
                ctx_ref[t, lo + i * HEAD : lo + (i + 1) * HEAD, :] = both[i * HEAD : (i + 1) * HEAD, lanes]


def local_part(pieces, gain, wq, wkv):
    steps, _, width = pieces[0].shape
    block = sum(p.shape[1] for p in pieces)
    tb = 4
    full = lambda a: pl.BlockSpec(a.shape, lambda i: (0,) * a.ndim)
    per_t = lambda *shape: pl.BlockSpec((tb,) + shape, lambda i: (i, 0, 0))
    return pl.pallas_call(
        functools.partial(local_kernel, len(pieces)),
        out_shape=[
            jax.ShapeDtypeStruct((steps, block, width), BF16),
            jax.ShapeDtypeStruct((steps, width, block), F32),
            jax.ShapeDtypeStruct((steps, 1, H * block), F32),
            jax.ShapeDtypeStruct((steps, 1, H * block), F32),
            jax.ShapeDtypeStruct((width, width), BF16),
        ],
        grid=(steps // tb,),
        in_specs=[per_t(p.shape[1], width) for p in pieces] + [full(gain), full(wq), full(wkv)],
        out_specs=[
            per_t(block, width),
            per_t(width, block),
            per_t(1, H * block),
            per_t(1, H * block),
            pl.BlockSpec((width, width), lambda i: (0, 0)),
        ],
        compiler_params=pltpu.CompilerParams(vmem_limit_bytes=VMEM_LIMIT),
        cost_estimate=pl.CostEstimate(
            flops=steps * block * width * width * 12, bytes_accessed=steps * block * width * 10, transcendentals=0
        ),
        name="local_keys",
    )(*pieces, gain, wq, wkv)


def gelu(x):
    inner = x * (0.7978845608028654 + 0.035677408136300125 * (x * x))
    half = 0.5 * x
    return half + half * jnp.tanh(inner)


def finish_kernel(n, split, own_ref, *refs):
    pieces = refs[:n]
    (in_ref, live_ref, q_ref, lctx_ref, ltop_ref, lsum_ref, gain_ref, wk_ref, wvt_ref, wo_ref, gain_ffn_ref,
     w_in_ref, w_out_ref, out_ref, rn_s, rk_s, ctx_s, y_s, pick_s) = refs[n:]
    tb, block, width = q_ref.shape
    steps, remote = rn_s.shape[:2]
    step = pl.program_id(0)

    @pl.when(step == 0)
    def _():
        if split:
            order = swap16()
            for j in range(remote // REMOTE_SENSORS):
                pick_s[j * REMOTE_SENSORS : (j + 1) * REMOTE_SENSORS] = in_ref[own_ref[j]]
            for b in range(remote // 16):
                rows = pick_s[b * 16 : (b + 1) * 16].reshape(256, width)
                rn_s[:, b * 16 : (b + 1) * 16, :] = dot(order, rows).astype(BF16).reshape(16, 16, width)
            raw = rn_s[...]
        else:
            raw = in_ref[...]
        normed = rms(raw.reshape(steps * remote, width).astype(F32), gain_ref[...])
        rn_s[...] = normed.reshape(steps, remote, width)
        rk_s[...] = dot(normed, wk_ref[...]).astype(BF16).reshape(steps, remote, width)

    live = live_ref[...] > 0
    masks = [head_rows(2 * block, 128, block, -2 * p) for p in range(2)]
    rows = []
    for t in range(tb):
        at = step * tb + t
        rk = rk_s[at]
        vt = dot_nt(wvt_ref[...], rn_s[at]).astype(BF16)
        q = q_ref[t]
        scores = jnp.concatenate([pair_scores(q, rk, masks, pair) for pair in range(H // 2)], axis=1)
        scores = jnp.where(live, scores, NEG)
        ltop = ltop_ref[t]
        top = jnp.maximum(jnp.max(scores, axis=0, keepdims=True), ltop)
        e = jnp.exp2((scores - top) * SCALE)
        keep = jnp.exp2((ltop - top) * SCALE)
        inverse = 1.0 / (jnp.sum(e, axis=0, keepdims=True) + lsum_ref[t] * keep)
        keep = keep * inverse
        e = (e * inverse).astype(BF16)
        for pair in range(H // 2):
            lo = pair * 2 * HEAD
            both = dot(vt[lo : lo + 2 * HEAD], e[:, pair * 2 * block : (pair + 1) * 2 * block])
            for i in range(2):
                lanes = slice(i * block, (i + 1) * block)
                dims = slice(lo + i * HEAD, lo + (i + 1) * HEAD)
                head = 2 * pair + i
                far = both[i * HEAD : (i + 1) * HEAD, lanes]
                merged = lctx_ref[t, dims, :] * keep[:, head * block : (head + 1) * block] + far
                ctx_s[dims, t * block : (t + 1) * block] = merged.astype(BF16)
        rows += [p[t] for p in pieces]
    after = jnp.concatenate(rows, axis=0).astype(F32) + dot(ctx_s[...].T, wo_ref[...])
    normed = rms(after, gain_ffn_ref[...])
    hidden = gelu(dot(normed, w_in_ref[...])).astype(BF16)
    y = (after + dot(hidden, w_out_ref[...])).astype(BF16).reshape(tb, block, width)
    if not split:
        out_ref[...] = y
        return
    y_s[pl.ds(step * tb, tb)] = y

    @pl.when(step == pl.num_programs(0) - 1)
    def _():
        order = swap16()
        mine = own_ref[own_ref.shape[0] - 1]
        half = block // 2
        for b in range(block // 16):
            first = b * 16
            owner = mine if first < half else 1 - mine
            rows = y_s[:, first : first + 16, :].reshape(256, width)
            at = owner * half + first % half
            out_ref[pl.ds(at, 16)] = dot(order, rows).astype(BF16).reshape(16, 16, width)


def finish(own, pieces, incoming, live, local, gain, wkv, wo, gain_ffn, w_in, w_out, split):
    q, lctx, ltop, lsum, wvt = local
    steps, block, width = q.shape
    remote = live.shape[0]
    tb = 4
    full = lambda a: pl.BlockSpec(a.shape, lambda i, *_: (0,) * a.ndim)
    per_t = lambda *shape: pl.BlockSpec((tb,) + shape, lambda i, *_: (i, 0, 0))
    if split:
        out_shape = jax.ShapeDtypeStruct((block, steps, width), BF16)
        out_specs = pl.BlockSpec((block, steps, width), lambda i, *_: (0, 0, 0))
    else:
        out_shape = jax.ShapeDtypeStruct((steps, block, width), BF16)
        out_specs = per_t(block, width)
    return pl.pallas_call(
        functools.partial(finish_kernel, len(pieces), split),
        out_shape=out_shape,
        grid_spec=pltpu.PrefetchScalarGridSpec(
            num_scalar_prefetch=1,
            grid=(steps // tb,),
            in_specs=[per_t(p.shape[1], width) for p in pieces]
            + [
                full(incoming),
                full(live),
                per_t(block, width),
                per_t(width, block),
                per_t(1, H * block),
                per_t(1, H * block),
                full(gain),
                pl.BlockSpec((width, width), lambda i, *_: (0, 0)),
                full(wvt),
                full(wo),
                full(gain_ffn),
                full(w_in),
                full(w_out),
            ],
            out_specs=out_specs,
            scratch_shapes=[
                pltpu.VMEM((steps, remote, width), BF16),
                pltpu.VMEM((steps, remote, width), BF16),
                pltpu.VMEM((width, tb * block), BF16),
                pltpu.VMEM((steps, block, width), BF16),
                pltpu.VMEM((remote, steps, width), BF16),
            ],
        ),
        compiler_params=pltpu.CompilerParams(vmem_limit_bytes=VMEM_LIMIT),
        cost_estimate=pl.CostEstimate(
            flops=steps * block * width * width * 18, bytes_accessed=steps * block * width * 12, transcendentals=0
        ),
        name="remote_keys_and_feed_forward",
    )(own, *pieces, incoming, live, q, lctx, ltop, lsum, gain, wkv, wvt, wo, gain_ffn, w_in, w_out)


def local(
    tm,
    tokens,
    gain_time,
    wq_time,
    wkv_time,
    wo_time,
    gain_graph,
    wq_graph,
    wkv_graph,
    wo_graph,
    gain_ffn,
    w_in,
    w_out,
    neighbour_blocks,
    slot_used_mask,
    neighbour_rows,
):
    sensors_here, steps, width = tokens.shape
    block = sensors_here * tm
    group = steps // tm
    block_count, slots = neighbour_blocks.shape
    split = tm == 2 and group == 16 and sensors_here % 32 == 0
    gain_time, gain_graph, gain_ffn = (g.reshape(1, width) for g in (gain_time, gain_graph, gain_ffn))
    mine = lax.axis_index("tm").astype(jnp.int32)
    block_index = lax.axis_index("sensor")
    time = functools.partial(time_block, tokens, mine.reshape(1), gain_time, wq_time, wkv_time, wo_time)
    if split:
        chunks = 2
        size = sensors_here // chunks
        kept, got = [], []
        for c in range(chunks):
            keep, send = time(c * size, size, True)
            kept.append(keep)
            got.append(lax.ppermute(send, "tm", [(0, 1), (1, 0)]))
        pieces = kept + got
    else:
        whole = lax.all_to_all(time(0, sensors_here, False), "tm", split_axis=1, concat_axis=0, tiled=True)
        pieces = [whole.transpose(1, 0, 2)]
    matches = (neighbour_blocks == block_index).astype(jnp.int32)
    wanted = jnp.sum(matches[:, :, None] * neighbour_rows, axis=1).reshape(-1)
    own = lax.dynamic_index_in_dim(neighbour_blocks, block_index, 0, keepdims=False)
    live = jnp.broadcast_to(jnp.repeat(slot_used_mask[0], REMOTE_SENSORS)[:, None], (slots * REMOTE_SENSORS, H * block))
    if split:
        place = (jnp.arange(block) + mine * sensors_here) % block
        pick = (wanted[:, None] == place[None, :]).astype(BF16)
        outgoing = pick_rows(pick, pieces)
    else:
        outgoing = jnp.take(whole, wanted, axis=0)
    outgoing = outgoing.reshape(block_count, REMOTE_SENSORS, group, width)
    incoming = lax.all_to_all(outgoing, "sensor", split_axis=0, concat_axis=0, tiled=True)
    if not split:
        incoming = jnp.take(incoming, own, axis=0).reshape(-1, group, width).transpose(1, 0, 2)
    near = local_part(pieces, gain_graph, wq_graph, wkv_graph)
    numbers = jnp.concatenate([own.astype(jnp.int32), mine.reshape(1)])
    out = finish(numbers, pieces, incoming, live, near, gain_graph, wkv_graph, wo_graph, gain_ffn, w_in, w_out, split)
    return out if split else out.transpose(1, 0, 2)


def solution(mesh):
    in_specs = (
        P(("sensor", "tm"), None, None),
        P(),
        P(),
        P(),
        P(),
        P(),
        P(),
        P(),
        P(),
        P(),
        P(),
        P(),
        P(),
        P("sensor", None),
        P(),
    )
    out_specs = P("sensor", "tm", None)
    body = functools.partial(local, mesh.shape["tm"])
    return jax.shard_map(body, mesh=mesh, in_specs=in_specs, out_specs=out_specs, check_vma=False)
```

```python
import functools
import math

import jax
import jax.numpy as jnp
from jax import lax
from jax.experimental import pallas as pl
from jax.experimental.pallas import tpu as pltpu
from jax.sharding import PartitionSpec as P

H = 8
HEAD = 32
REMOTE_SENSORS = 4
EPSILON = 1e-06
NEG = -1e30
SCALE = math.log2(math.e) / math.sqrt(HEAD)
F32 = jnp.float32
BF16 = jnp.bfloat16
VMEM_LARGE = 60 * 1024 * 1024
VMEM_SMALL = 24 * 1024 * 1024


def dot(a, b):
    return jnp.dot(a, b, preferred_element_type=F32)


def dot_nt(a, b):
    return lax.dot_general(a, b, (((1,), (1,)), ((), ())), preferred_element_type=F32)


def dot_tn(a, b):
    return lax.dot_general(a, b, (((0,), (0,)), ((), ())), preferred_element_type=F32)


def rms(x, gain):
    inverse = lax.rsqrt(jnp.mean(x * x, axis=-1, keepdims=True) + EPSILON)
    return (x * inverse * gain).astype(BF16)


def swap16():
    row = lax.broadcasted_iota(jnp.int32, (256, 256), 0)
    col = lax.broadcasted_iota(jnp.int32, (256, 256), 1)
    return (col == ((row & 15) << 4) + (row >> 4)).astype(BF16)


def head_rows(rows, lanes, head_of_row, first_head):
    row = lax.broadcasted_iota(jnp.int32, (rows, lanes), 0)
    lane = lax.broadcasted_iota(jnp.int32, (rows, lanes), 1)
    return (lane // HEAD + first_head == row // head_of_row).astype(BF16)


def time_kernel(split, my_ref, x_ref, gain_ref, wq_ref, wkv_ref, wo_ref, *refs):
    if split:
        keep_ref, send_ref, q_s, k_s, v_s, a_s, c_s, after_s = refs
    else:
        out_ref, q_s, k_s, v_s, a_s, c_s = refs
    sensors, steps, width = x_ref.shape
    rows = sensors * steps
    x = x_ref[...].reshape(rows, width).astype(F32)
    normed = rms(x, gain_ref[...])
    q_s[...] = dot(normed, wq_ref[...]).astype(BF16)
    kv = dot(normed, wkv_ref[...]).astype(BF16)
    k_s[...] = kv[:, :width]
    v_s[...] = kv[:, width:]
    lanes = H * steps
    near = 128 // HEAD
    span = near * steps
    mask = head_rows(span, 128, steps, 0)
    none = jnp.zeros((span, 128), BF16)
    key_t = lax.broadcasted_iota(jnp.int32, (steps, lanes), 0)
    query_t = lax.broadcasted_iota(jnp.int32, (steps, lanes), 1) & (steps - 1)
    causal = key_t <= query_t
    for s in range(sensors):
        here = slice(s * steps, (s + 1) * steps)
        first, second = (jnp.concatenate([q_s[here, c : c + 128]] * near, axis=0) * mask for c in (0, 128))
        spread = jnp.concatenate(
            [jnp.concatenate([first, none], axis=1), jnp.concatenate([none, second], axis=1)], axis=0
        )
        scores = jnp.where(causal, dot_nt(k_s[here, :], spread), NEG)
        top = jnp.max(scores, axis=0, keepdims=True)
        e = jnp.exp2((scores - top) * SCALE)
        a_s[here, :] = (e * (1.0 / jnp.sum(e, axis=0, keepdims=True))).astype(BF16)
    lane_head = lax.broadcasted_iota(jnp.int32, (steps, 128), 1) // HEAD
    for g in range(rows // 128):
        turned = a_s[g * 128 : (g + 1) * 128, :].T
        for half in range(2):
            cols = slice(half * 128, (half + 1) * 128)
            for s in range(0, 128 // steps, 2):
                columns = []
                for r in (s, s + 1):
                    v = v_s[g * 128 + r * steps : g * 128 + (r + 1) * steps, cols]
                    parts = [jnp.zeros((r * steps, 128), BF16), v, jnp.zeros((128 - (r + 1) * steps, 128), BF16)]
                    columns.append(jnp.concatenate([p for p in parts if p.shape[0]], axis=0))
                wide = dot(turned[half * span : (half + 1) * span], jnp.concatenate(columns, axis=1))
                for i in range(2):
                    ctx = wide[:steps, i * 128 : (i + 1) * 128]
                    for h in range(1, near):
                        ctx = jnp.where(lane_head == h, wide[h * steps : (h + 1) * steps, i * 128 : (i + 1) * 128], ctx)
                    at = g * 128 + (s + i) * steps
                    c_s[at : at + steps, cols] = ctx.astype(BF16)
    after = (x + dot(c_s[...], wo_ref[...])).astype(BF16)
    if not split:
        out_ref[...] = after.reshape(sensors, steps, width)
        return
    after_s[...] = after.reshape(sensors, steps, width)
    order = swap16()
    mine = my_ref[0]
    for ref, part in ((keep_ref, mine), (send_ref, 1 - mine)):
        rows16 = after_s[:, pl.ds(pl.multiple_of(part * 16, 16), 16), :]
        for b in range(sensors // 16):
            block = rows16[b * 16 : (b + 1) * 16].reshape(256, width)
            ref[:, b * 16 : (b + 1) * 16, :] = dot(order, block).astype(BF16).reshape(16, 16, width)


def time_block(tokens, my, gain, wq, wkv, wo, first, count, split):
    steps, width = tokens.shape[1:]
    sb = min(16, count)
    rows = sb * steps
    full = lambda a: pl.BlockSpec(a.shape, lambda i, *_: (0,) * a.ndim)
    if split:
        out_shape = [jax.ShapeDtypeStruct((16, count, width), BF16)] * 2
        out_specs = [pl.BlockSpec((16, sb, width), lambda i, *_: (0, i, 0))] * 2
        extra = [pltpu.VMEM((sb, steps, width), BF16)]
    else:
        out_shape = jax.ShapeDtypeStruct((count, steps, width), BF16)
        out_specs = pl.BlockSpec((sb, steps, width), lambda i, *_: (i, 0, 0))
        extra = []
    return pl.pallas_call(
        functools.partial(time_kernel, split),
        out_shape=out_shape,
        grid_spec=pltpu.PrefetchScalarGridSpec(
            num_scalar_prefetch=1,
            grid=(count // sb,),
            in_specs=[
                pl.BlockSpec((sb, steps, width), lambda i, *_: (first // sb + i, 0, 0)),
                full(gain),
                full(wq),
                full(wkv),
                full(wo),
            ],
            out_specs=out_specs,
            scratch_shapes=[pltpu.VMEM((rows, width), BF16)] * 5 + extra,
        ),
        compiler_params=pltpu.CompilerParams(vmem_limit_bytes=VMEM_LARGE if first == 0 else VMEM_SMALL),
        cost_estimate=pl.CostEstimate(
            flops=count * steps * width * width * 12, bytes_accessed=count * steps * width * 4, transcendentals=0
        ),
        name="time_block",
    )(my, tokens, gain, wq, wkv, wo)


def pick_kernel(n, pick_ref, *refs):
    pieces, (out_ref, o_s) = refs[:n], refs[n:]
    steps = out_ref.shape[1]
    wanted = out_ref.shape[0]
    order = swap16()
    pick = pick_ref[...]
    for t in range(steps):
        rows = jnp.concatenate([p[t] for p in pieces], axis=0)
        o_s[t] = dot(pick, rows).astype(BF16)
    for b in range(wanted // 16):
        block = o_s[:, b * 16 : (b + 1) * 16, :].reshape(256, 256)
        out_ref[b * 16 : (b + 1) * 16] = dot(order, block).astype(BF16).reshape(16, 16, 256)


def pick_rows(pick, pieces):
    steps, _, width = pieces[0].shape
    wanted = pick.shape[0]
    return pl.pallas_call(
        functools.partial(pick_kernel, len(pieces)),
        out_shape=jax.ShapeDtypeStruct((wanted, steps, width), BF16),
        scratch_shapes=[pltpu.VMEM((steps, wanted, width), BF16)],
        compiler_params=pltpu.CompilerParams(vmem_limit_bytes=VMEM_SMALL),
        name="pick_rows",
    )(pick, *pieces)


def pair_scores(q, k, masks, pair):
    cols = slice(pair // 2 * 128, pair // 2 * 128 + 128)
    spread = jnp.concatenate([q[:, cols]] * 2, axis=0) * masks[pair % 2]
    return dot_nt(k[:, cols], spread)


def local_kernel(n, *refs):
    pieces = refs[:n]
    gain_ref, wq_ref, wkv_ref, qt_ref, ctx_ref, top_ref, sum_ref, wvt_ref, wqt_s = refs[n:]
    tb, width, block = qt_ref.shape

    @pl.when(pl.program_id(0) == 0)
    def _():
        wvt_ref[...] = wkv_ref[:, width:].T
        wqt_s[...] = wq_ref[...].T

    x = jnp.concatenate([p[t] for t in range(tb) for p in pieces], axis=0).astype(F32)
    normed = rms(x, gain_ref[...])
    q = dot(normed, wq_ref[...]).astype(BF16)
    k = dot(normed, wkv_ref[:, :width]).astype(BF16)
    masks = [head_rows(2 * block, 128, block, -2 * p) for p in range(2)]
    for t in range(tb):
        here = slice(t * block, (t + 1) * block)
        qt_ref[t] = dot_nt(wqt_s[...], normed[here]).astype(BF16)
        vt = dot_nt(wvt_ref[...], normed[here]).astype(BF16)
        scores = [pair_scores(q[here], k[here], masks, pair) for pair in range(H // 2)]
        tops = [jnp.max(x, axis=0, keepdims=True) for x in scores]
        es = [jnp.exp2((x - top) * SCALE) for x, top in zip(scores, tops)]
        for pair, e in enumerate(es):
            lo = pair * 2 * HEAD
            both = dot(vt[lo : lo + 2 * HEAD], e.astype(BF16))
            total = jnp.sum(e, axis=0, keepdims=True)
            for i in range(2):
                lanes = slice(i * block, (i + 1) * block)
                head = 2 * pair + i
                ctx_ref[t, lo + i * HEAD : lo + (i + 1) * HEAD, :] = both[i * HEAD : (i + 1) * HEAD, lanes].astype(BF16)
                top_ref[t, head : head + 1, :] = tops[pair][:, lanes]
                sum_ref[t, head : head + 1, :] = total[:, lanes]


def local_part(pieces, gain, wq, wkv):
    steps, _, width = pieces[0].shape
    block = sum(p.shape[1] for p in pieces)
    tb = 4
    full = lambda a: pl.BlockSpec(a.shape, lambda i: (0,) * a.ndim)
    per_t = lambda *shape: pl.BlockSpec((tb,) + shape, lambda i: (i, 0, 0))
    return pl.pallas_call(
        functools.partial(local_kernel, len(pieces)),
        out_shape=[
            jax.ShapeDtypeStruct((steps, width, block), BF16),
            jax.ShapeDtypeStruct((steps, width, block), BF16),
            jax.ShapeDtypeStruct((steps, H, block), F32),
            jax.ShapeDtypeStruct((steps, H, block), F32),
            jax.ShapeDtypeStruct((width, width), BF16),
        ],
        grid=(steps // tb,),
        in_specs=[per_t(p.shape[1], width) for p in pieces] + [full(gain), full(wq), full(wkv)],
        out_specs=[
            per_t(width, block),
            per_t(width, block),
            per_t(H, block),
            per_t(H, block),
            pl.BlockSpec((width, width), lambda i: (0, 0)),
        ],
        scratch_shapes=[pltpu.VMEM((width, width), BF16)],
        compiler_params=pltpu.CompilerParams(vmem_limit_bytes=VMEM_SMALL),
        cost_estimate=pl.CostEstimate(
            flops=steps * block * width * width * 12, bytes_accessed=steps * block * width * 10, transcendentals=0
        ),
        name="local_keys",
    )(*pieces, gain, wq, wkv)


def gelu(x):
    inner = x * (0.7978845608028654 + 0.035677408136300125 * (x * x))
    half = 0.5 * x
    return half + half * jnp.tanh(inner)


def finish_kernel(n, split, tb, numbers_ref, *refs):
    pieces = refs[:n]
    in_hbm, gain_ref, gain_ffn_ref, ltop_ref, lsum_ref = refs[n : n + 5]
    qt_hbm, lctx_hbm, wkv_hbm, wvt_hbm, wo_hbm, w_in_hbm, w_out_hbm, out_hbm = refs[n + 5 : n + 13]
    x_s, raw_s, rn_s, rk_s, ctx_s, y_s, out_s, qt_s, lctx_s, wk_s, wvt_s, wo_s, w_in_s, w_out_s, sems, out_sems = refs[n + 13 :]
    steps, width, block = qt_s.shape
    remote = rn_s.shape[1]
    slots = remote // REMOTE_SENSORS
    chunks = steps // tb
    count = [0]

    def fetch(src, dst):
        copy = pltpu.make_async_copy(src, dst, sems.at[count[0]])
        count[0] += 1
        copy.start()
        return copy

    if split:
        raw_in = [
            fetch(in_hbm.at[numbers_ref[1 + j]], raw_s.at[pl.ds(j * REMOTE_SENSORS, REMOTE_SENSORS)]) for j in range(slots)
        ]
    else:
        raw_in = [fetch(in_hbm, raw_s)]
    first_in = [fetch(wkv_hbm.at[:, pl.ds(0, width)], wk_s), fetch(wvt_hbm, wvt_s)]
    chunk = [pl.ds(c * tb, tb) for c in range(chunks)]
    qt_in = [fetch(qt_hbm.at[here], qt_s.at[here]) for here in chunk]

    order = swap16() if split else None
    lane_head = lax.broadcasted_iota(jnp.int32, (1, 128), 1) // HEAD
    heads = [(lane_head == h).astype(BF16) for h in range(128 // HEAD)]
    none = jnp.zeros((remote, 128), BF16)
    own_block = (
        lax.broadcasted_iota(jnp.int32, (width, H * remote), 0) // HEAD
        == lax.broadcasted_iota(jnp.int32, (width, H * remote), 1) // remote
    ).astype(BF16)
    slot = lax.broadcasted_iota(jnp.int32, (remote, block), 0) // REMOTE_SENSORS
    live = jnp.zeros((remote, block), jnp.int32)
    for j in range(slots):
        live = jnp.where(slot == j, numbers_ref[1 + slots + j], live)
    live = live > 0

    for copy in raw_in + first_in:
        copy.wait()
    lctx_in, x_in = [], []
    for here in chunk:
        lctx_in.append(fetch(lctx_hbm.at[here], lctx_s.at[here]))
        place, x_c = 0, []
        for p in pieces:
            x_c.append(fetch(p.at[here], x_s.at[here, pl.ds(place, p.shape[1])]))
            place += p.shape[1]
        x_in.append(x_c)
    wo_in = fetch(wo_hbm, wo_s)
    ffn_in = [fetch(w_in_hbm, w_in_s), fetch(w_out_hbm, w_out_s)]
    if split:
        for b in range(remote // 16):
            rows = raw_s[b * 16 : (b + 1) * 16].reshape(256, width)
            rn_s[:, b * 16 : (b + 1) * 16, :] = dot(order, rows).astype(BF16).reshape(16, 16, width)
        raw = rn_s[...]
    else:
        raw = raw_s[...]
    normed = rms(raw.reshape(steps * remote, width).astype(F32), gain_ref[...])
    rn_s[...] = normed.reshape(steps, remote, width)
    rk_s[...] = dot(normed, wk_s[...]).astype(BF16).reshape(steps, remote, width)

    for c in range(chunks):
        ts = range(c * tb, (c + 1) * tb)
        qt_in[c].wait()
        keys = []
        for t in ts:
            rk = rk_s[t]
            spread = []
            for h in range(H):
                half = h * HEAD // 128
                part = rk[:, half * 128 : (half + 1) * 128] * heads[h % (128 // HEAD)]
                spread.append(jnp.concatenate([part, none] if half == 0 else [none, part], axis=1))
            keys.append(jnp.concatenate(spread, axis=0))
        scores = [dot(k, qt_s[t]).reshape(H, remote, block) for k, t in zip(keys, ts)]
        values = []
        for t in ts:
            tiled = jnp.concatenate([rn_s[t]] * H, axis=0)
            values.append(dot_nt(wvt_s[...], tiled).astype(BF16) * own_block)
        weights, keeps = [], []
        for s, t in zip(scores, ts):
            masked = jnp.where(live[None], s, NEG)
            ltop = ltop_ref[t]
            top = jnp.maximum(jnp.max(masked, axis=1), ltop)
            e = jnp.exp2((masked - top[:, None, :]) * SCALE)
            keep = jnp.exp2((ltop - top) * SCALE)
            inverse = 1.0 / (jnp.sum(e, axis=1) + lsum_ref[t] * keep)
            keeps.append(keep * inverse)
            weights.append((e * inverse[:, None, :]).astype(BF16).reshape(H * remote, block))
        far = [dot(v, w).reshape(H, HEAD, block) for v, w in zip(values, weights)]
        lctx_in[c].wait()
        for i, t in enumerate(ts):
            merged = lctx_s[t].astype(F32).reshape(H, HEAD, block) * keeps[i][:, None, :] + far[i]
            ctx_s[:, i * block : (i + 1) * block] = merged.reshape(width, block).astype(BF16)
        if c == 0:
            wo_in.wait()
        for copy in x_in[c]:
            copy.wait()
        x = x_s[c * tb : (c + 1) * tb].reshape(tb * block, width)
        after = x.astype(F32) + dot(ctx_s[...].T, wo_s[...])
        normed = rms(after, gain_ffn_ref[...])
        if c == 0:
            for copy in ffn_in:
                copy.wait()
        hidden = gelu(dot(normed, w_in_s[...])).astype(BF16)
        y_s[c * tb : (c + 1) * tb] = (after + dot(hidden, w_out_s[...])).astype(BF16).reshape(tb, block, width)

    if not split:
        copy = pltpu.make_async_copy(y_s, out_hbm, out_sems.at[0])
        copy.start()
        copy.wait()
        return
    mine = numbers_ref[0]
    half = block // 2
    copies = []
    for b in range(block // 16):
        first = b * 16
        owner = mine if first < half else 1 - mine
        rows = y_s[:, first : first + 16, :].reshape(256, width)
        out_s[first : first + 16] = dot(order, rows).astype(BF16).reshape(16, 16, width)
        place = out_hbm.at[pl.ds(owner * half + first % half, 16)]
        copy = pltpu.make_async_copy(out_s.at[pl.ds(first, 16)], place, out_sems.at[b])
        copy.start()
        copies.append(copy)
    for copy in copies:
        copy.wait()


def finish(numbers, pieces, incoming, local, gain, wkv, wo, gain_ffn, w_in, w_out, split):
    qt, lctx, ltop, lsum, wvt = local
    steps, width, block = qt.shape
    remote = (numbers.shape[0] - 1) // 2 * REMOTE_SENSORS
    tb = min(16, steps)
    vmem = pl.BlockSpec(memory_space=pltpu.VMEM)
    hbm = pl.BlockSpec(memory_space=pl.ANY)
    chunks = steps // tb
    n_copies = (remote // REMOTE_SENSORS if split else 1) + 5 + chunks * (2 + len(pieces))
    buffer = lambda *shape: pltpu.VMEM(shape, BF16)
    return pl.pallas_call(
        functools.partial(finish_kernel, len(pieces), split, tb),
        out_shape=jax.ShapeDtypeStruct((block, steps, width) if split else (steps, block, width), BF16),
        in_specs=[pl.BlockSpec(memory_space=pltpu.SMEM)] + [hbm] * (len(pieces) + 1) + [vmem] * 4 + [hbm] * 7,
        out_specs=hbm,
        scratch_shapes=[
            buffer(steps, block, width),
            buffer(remote, steps, width) if split else buffer(steps, remote, width),
            buffer(steps, remote, width),
            buffer(steps, remote, width),
            buffer(width, tb * block),
            buffer(steps, block, width),
            buffer(block, steps, width) if split else buffer(8, 128),
            buffer(steps, width, block),
            buffer(steps, width, block),
            buffer(width, width),
            buffer(width, width),
            buffer(*wo.shape),
            buffer(*w_in.shape),
            buffer(*w_out.shape),
            pltpu.SemaphoreType.DMA((n_copies,)),
            pltpu.SemaphoreType.DMA((max(block // 16, 1),)),
        ],
        compiler_params=pltpu.CompilerParams(vmem_limit_bytes=VMEM_LARGE),
        cost_estimate=pl.CostEstimate(
            flops=steps * block * width * width * 18, bytes_accessed=steps * block * width * 12, transcendentals=0
        ),
        name="remote_keys_and_feed_forward",
    )(numbers, *pieces, incoming, gain, gain_ffn, ltop, lsum, qt, lctx, wkv, wvt, wo, w_in, w_out)


def local(
    tm,
    tokens,
    gain_time,
    wq_time,
    wkv_time,
    wo_time,
    gain_graph,
    wq_graph,
    wkv_graph,
    wo_graph,
    gain_ffn,
    w_in,
    w_out,
    neighbour_blocks,
    slot_used_mask,
    neighbour_rows,
):
    sensors_here, steps, width = tokens.shape
    block = sensors_here * tm
    group = steps // tm
    block_count, slots = neighbour_blocks.shape
    split = tm == 2 and group == 16 and sensors_here % 32 == 0
    gain_time, gain_graph, gain_ffn = (g.reshape(1, width) for g in (gain_time, gain_graph, gain_ffn))
    mine = lax.axis_index("tm").astype(jnp.int32)
    block_index = lax.axis_index("sensor")
    time = functools.partial(time_block, tokens, mine.reshape(1), gain_time, wq_time, wkv_time, wo_time)
    if split:
        chunks = 2
        size = sensors_here // chunks
        kept, got = [], []
        for c in range(chunks):
            keep, send = time(c * size, size, True)
            kept.append(keep)
            got.append(lax.ppermute(send, "tm", [(0, 1), (1, 0)]))
        pieces = kept + got
    else:
        whole = lax.all_to_all(time(0, sensors_here, False), "tm", split_axis=1, concat_axis=0, tiled=True)
        pieces = [whole.transpose(1, 0, 2)]
    matches = (neighbour_blocks == block_index).astype(jnp.int32)
    wanted = jnp.sum(matches[:, :, None] * neighbour_rows, axis=1).reshape(-1)
    own = lax.dynamic_index_in_dim(neighbour_blocks, block_index, 0, keepdims=False)
    numbers = jnp.concatenate([mine.reshape(1), own, slot_used_mask[0]])
    if split:
        place = (jnp.arange(block) + mine * sensors_here) % block
        pick = (wanted[:, None] == place[None, :]).astype(BF16)
        outgoing = pick_rows(pick, pieces)
    else:
        outgoing = jnp.take(whole, wanted, axis=0)
    outgoing = outgoing.reshape(block_count, REMOTE_SENSORS, group, width)
    incoming = lax.all_to_all(outgoing, "sensor", split_axis=0, concat_axis=0, tiled=True)
    if not split:
        incoming = jnp.take(incoming, own, axis=0).reshape(-1, group, width).transpose(1, 0, 2)
    near = local_part(pieces, gain_graph, wq_graph, wkv_graph)
    out = finish(numbers, pieces, incoming, near, gain_graph, wkv_graph, wo_graph, gain_ffn, w_in, w_out, split)
    return out if split else out.transpose(1, 0, 2)


def solution(mesh):
    in_specs = (
        P(("sensor", "tm"), None, None),
        P(),
        P(),
        P(),
        P(),
        P(),
        P(),
        P(),
        P(),
        P(),
        P(),
        P(),
        P(),
        P("sensor", None),
        P(),
    )
    out_specs = P("sensor", "tm", None)
    body = functools.partial(local, mesh.shape["tm"])
    return jax.shard_map(body, mesh=mesh, in_specs=in_specs, out_specs=out_specs, check_vma=False)
```

```python
import functools
import math

import jax
import jax.numpy as jnp
from jax import lax
from jax.experimental import pallas as pl
from jax.experimental.pallas import tpu as pltpu
from jax.sharding import PartitionSpec as P

H = 8
HEAD = 32
REMOTE_SENSORS = 4
EPSILON = 1e-06
NEG = -1e30
SCALE = math.log2(math.e) / math.sqrt(HEAD)
SHARES = (1, 1, 2)
F32 = jnp.float32
BF16 = jnp.bfloat16
VMEM_LIMIT = 28 * 1024 * 1024


def dot(a, b):
    return jnp.dot(a, b, preferred_element_type=F32)


def dot_nt(a, b):
    return lax.dot_general(a, b, (((1,), (1,)), ((), ())), preferred_element_type=F32)


def dot_tn(a, b):
    return lax.dot_general(a, b, (((0,), (0,)), ((), ())), preferred_element_type=F32)


def rms(x, gain):
    inverse = lax.rsqrt(jnp.mean(x * x, axis=-1, keepdims=True) + EPSILON)
    return (x * inverse * gain).astype(BF16)


def swap16():
    row = lax.broadcasted_iota(jnp.int32, (256, 256), 0)
    col = lax.broadcasted_iota(jnp.int32, (256, 256), 1)
    return (col == ((row & 15) << 4) + (row >> 4)).astype(BF16)


def head_rows(rows, lanes, head_of_row, first_head):
    row = lax.broadcasted_iota(jnp.int32, (rows, lanes), 0)
    lane = lax.broadcasted_iota(jnp.int32, (rows, lanes), 1)
    return (lane // HEAD + first_head == row // head_of_row).astype(BF16)


def time_kernel(split, my_ref, x_ref, gain_ref, wq_ref, wkv_ref, wo_ref, *refs):
    if split:
        keep_ref, send_ref, q_s, k_s, v_s, a_s, c_s, after_s = refs
    else:
        out_ref, q_s, k_s, v_s, a_s, c_s = refs
    sensors, steps, width = x_ref.shape
    rows = sensors * steps
    x = x_ref[...].reshape(rows, width).astype(F32)
    normed = rms(x, gain_ref[...])
    q_s[...] = dot(normed, wq_ref[...]).astype(BF16)
    kv = dot(normed, wkv_ref[...]).astype(BF16)
    k_s[...] = kv[:, :width]
    v_s[...] = kv[:, width:]
    lanes = H * steps
    near = 128 // HEAD
    span = near * steps
    mask = head_rows(span, 128, steps, 0)
    none = jnp.zeros((span, 128), BF16)
    key_t = lax.broadcasted_iota(jnp.int32, (steps, lanes), 0)
    query_t = lax.broadcasted_iota(jnp.int32, (steps, lanes), 1) & (steps - 1)
    causal = key_t <= query_t
    for s in range(sensors):
        here = slice(s * steps, (s + 1) * steps)
        first, second = (jnp.concatenate([q_s[here, c : c + 128]] * near, axis=0) * mask for c in (0, 128))
        spread = jnp.concatenate(
            [jnp.concatenate([first, none], axis=1), jnp.concatenate([none, second], axis=1)], axis=0
        )
        scores = jnp.where(causal, dot_nt(k_s[here, :], spread), NEG)
        top = jnp.max(scores, axis=0, keepdims=True)
        e = jnp.exp2((scores - top) * SCALE)
        a_s[here, :] = (e * (1.0 / jnp.sum(e, axis=0, keepdims=True))).astype(BF16)
    lane_head = lax.broadcasted_iota(jnp.int32, (steps, 128), 1) // HEAD
    for g in range(rows // 128):
        turned = a_s[g * 128 : (g + 1) * 128, :].T
        for half in range(2):
            cols = slice(half * 128, (half + 1) * 128)
            for s in range(0, 128 // steps, 2):
                columns = []
                for r in (s, s + 1):
                    v = v_s[g * 128 + r * steps : g * 128 + (r + 1) * steps, cols]
                    parts = [jnp.zeros((r * steps, 128), BF16), v, jnp.zeros((128 - (r + 1) * steps, 128), BF16)]
                    columns.append(jnp.concatenate([p for p in parts if p.shape[0]], axis=0))
                wide = dot(turned[half * span : (half + 1) * span], jnp.concatenate(columns, axis=1))
                for i in range(2):
                    ctx = wide[:steps, i * 128 : (i + 1) * 128]
                    for h in range(1, near):
                        ctx = jnp.where(lane_head == h, wide[h * steps : (h + 1) * steps, i * 128 : (i + 1) * 128], ctx)
                    at = g * 128 + (s + i) * steps
                    c_s[at : at + steps, cols] = ctx.astype(BF16)
    after = (x + dot(c_s[...], wo_ref[...])).astype(BF16)
    if not split:
        out_ref[...] = after.reshape(sensors, steps, width)
        return
    after_s[...] = after.reshape(sensors, steps, width)
    order = swap16()
    mine = my_ref[0]
    for ref, part in ((keep_ref, mine), (send_ref, 1 - mine)):
        rows16 = after_s[:, pl.ds(pl.multiple_of(part * 16, 16), 16), :]
        for b in range(sensors // 16):
            block = rows16[b * 16 : (b + 1) * 16].reshape(256, width)
            ref[:, b * 16 : (b + 1) * 16, :] = dot(order, block).astype(BF16).reshape(16, 16, width)


def time_block(tokens, my, gain, wq, wkv, wo, first, count, split):
    steps, width = tokens.shape[1:]
    if first == 0:
        tokens, gain, wq, wkv, wo = (pltpu.with_memory_space_constraint(a, pltpu.HBM) for a in (tokens, gain, wq, wkv, wo))
    sb = min(16, count)
    rows = sb * steps
    full = lambda a: pl.BlockSpec(a.shape, lambda i, *_: (0,) * a.ndim)
    if split:
        out_shape = [jax.ShapeDtypeStruct((16, count, width), BF16)] * 2
        out_specs = [pl.BlockSpec((16, sb, width), lambda i, *_: (0, i, 0))] * 2
        extra = [pltpu.VMEM((sb, steps, width), BF16)]
    else:
        out_shape = jax.ShapeDtypeStruct((count, steps, width), BF16)
        out_specs = pl.BlockSpec((sb, steps, width), lambda i, *_: (i, 0, 0))
        extra = []
    return pl.pallas_call(
        functools.partial(time_kernel, split),
        out_shape=out_shape,
        grid_spec=pltpu.PrefetchScalarGridSpec(
            num_scalar_prefetch=1,
            grid=(count // sb,),
            in_specs=[
                pl.BlockSpec((sb, steps, width), lambda i, *_: (first // sb + i, 0, 0)),
                full(gain),
                full(wq),
                full(wkv),
                full(wo),
            ],
            out_specs=out_specs,
            scratch_shapes=[pltpu.VMEM((rows, width), BF16)] * 5 + extra,
        ),
        compiler_params=pltpu.CompilerParams(vmem_limit_bytes=VMEM_LIMIT),
        cost_estimate=pl.CostEstimate(
            flops=count * steps * width * width * 12, bytes_accessed=count * steps * width * 4, transcendentals=0
        ),
        name="time_block",
    )(my, tokens, gain, wq, wkv, wo)


def pick_kernel(n, pick_ref, *refs):
    pieces, (out_ref, o_s) = refs[:n], refs[n:]
    steps = out_ref.shape[1]
    wanted = out_ref.shape[0]
    order = swap16()
    pick = pick_ref[...]
    for t in range(steps):
        rows = jnp.concatenate([p[t] for p in pieces], axis=0)
        o_s[t] = dot(pick, rows).astype(BF16)
    for b in range(wanted // 16):
        block = o_s[:, b * 16 : (b + 1) * 16, :].reshape(256, 256)
        out_ref[b * 16 : (b + 1) * 16] = dot(order, block).astype(BF16).reshape(16, 16, 256)


def pick_rows(pick, pieces):
    steps, _, width = pieces[0].shape
    wanted = pick.shape[0]
    return pl.pallas_call(
        functools.partial(pick_kernel, len(pieces)),
        out_shape=jax.ShapeDtypeStruct((wanted, steps, width), BF16),
        scratch_shapes=[pltpu.VMEM((steps, wanted, width), BF16)],
        compiler_params=pltpu.CompilerParams(vmem_limit_bytes=VMEM_LIMIT),
        name="pick_rows",
    )(pick, *pieces)


def pair_scores(q, k, masks, pair):
    cols = slice(pair // 2 * 128, pair // 2 * 128 + 128)
    spread = jnp.concatenate([q[:, cols]] * 2, axis=0) * masks[pair % 2]
    return dot_nt(k[:, cols], spread)


def local_kernel(n, *refs):
    pieces = refs[:n]
    gain_ref, wq_ref, wkv_ref, qt_ref, ctx_ref, top_ref, sum_ref, wvt_ref, wqt_s = refs[n:]
    tb, width, block = qt_ref.shape

    @pl.when(pl.program_id(0) == 0)
    def _():
        wvt_ref[...] = wkv_ref[:, width:].T
        wqt_s[...] = wq_ref[...].T

    x = jnp.concatenate([p[t] for t in range(tb) for p in pieces], axis=0).astype(F32)
    normed = rms(x, gain_ref[...])
    q = dot(normed, wq_ref[...]).astype(BF16)
    k = dot(normed, wkv_ref[:, :width]).astype(BF16)
    masks = [head_rows(2 * block, 128, block, -2 * p) for p in range(2)]
    for t in range(tb):
        here = slice(t * block, (t + 1) * block)
        qt_ref[t] = dot_nt(wqt_s[...], normed[here]).astype(BF16)
        vt = dot_nt(wvt_ref[...], normed[here]).astype(BF16)
        scores = [pair_scores(q[here], k[here], masks, pair) for pair in range(H // 2)]
        tops = [jnp.max(x, axis=0, keepdims=True) for x in scores]
        es = [jnp.exp2((x - top) * SCALE) for x, top in zip(scores, tops)]
        for pair, e in enumerate(es):
            lo = pair * 2 * HEAD
            both = dot(vt[lo : lo + 2 * HEAD], e.astype(BF16))
            total = jnp.sum(e, axis=0, keepdims=True)
            for i in range(2):
                lanes = slice(i * block, (i + 1) * block)
                head = 2 * pair + i
                ctx_ref[t, lo + i * HEAD : lo + (i + 1) * HEAD, :] = both[i * HEAD : (i + 1) * HEAD, lanes].astype(BF16)
                top_ref[t, head : head + 1, :] = tops[pair][:, lanes]
                sum_ref[t, head : head + 1, :] = total[:, lanes]


def local_part(pieces, gain, wq, wkv):
    steps, _, width = pieces[0].shape
    block = sum(p.shape[1] for p in pieces)
    tb = 4
    full = lambda a: pl.BlockSpec(a.shape, lambda i: (0,) * a.ndim)
    per_t = lambda *shape: pl.BlockSpec((tb,) + shape, lambda i: (i, 0, 0))
    return pl.pallas_call(
        functools.partial(local_kernel, len(pieces)),
        out_shape=[
            pltpu.HBM((steps, width, block), BF16),
            pltpu.HBM((steps, width, block), BF16),
            pltpu.HBM((steps, H, block), F32),
            pltpu.HBM((steps, H, block), F32),
            pltpu.HBM((width, width), BF16),
        ],
        grid=(steps // tb,),
        in_specs=[per_t(p.shape[1], width) for p in pieces] + [full(gain), full(wq), full(wkv)],
        out_specs=[
            per_t(width, block),
            per_t(width, block),
            per_t(H, block),
            per_t(H, block),
            pl.BlockSpec((width, width), lambda i: (0, 0)),
        ],
        scratch_shapes=[pltpu.VMEM((width, width), BF16)],
        compiler_params=pltpu.CompilerParams(vmem_limit_bytes=VMEM_LIMIT),
        cost_estimate=pl.CostEstimate(
            flops=steps * block * width * width * 12, bytes_accessed=steps * block * width * 10, transcendentals=0
        ),
        name="local_keys",
    )(*pieces, gain, wq, wkv)


def gelu(x):
    inner = x * (0.7978845608028654 + 0.035677408136300125 * (x * x))
    half = 0.5 * x
    return half + half * jnp.tanh(inner)


def finish_kernel(n, split, sb, numbers_ref, *refs):
    pieces = refs[:n]
    in_ref, gain_hbm, gain_ffn_hbm, ltop_hbm, lsum_hbm = refs[n : n + 5]
    qt_hbm, lctx_hbm, wkv_hbm, wvt_hbm, wo_hbm, w_in_hbm, w_out_hbm, out_hbm = refs[n + 5 : n + 13]
    (x_s, raw_s, rn_s, rk_s, ctx_s, out_s, qt_s, lctx_s, wk_s, wvt_s, wo_s, w_in_s, w_out_s, gain_ref, gain_ffn_ref,
     ltop_ref, lsum_ref, sems, out_sems) = refs[n + 13 :]
    steps, width, block = qt_s.shape
    remote = rn_s.shape[1]
    slots = remote // REMOTE_SENSORS
    count = [0]

    def fetch(src, dst):
        copy = pltpu.make_async_copy(src, dst, sems.at[count[0]])
        count[0] += 1
        copy.start()
        return copy

    first_in = [fetch(gain_hbm, gain_ref), fetch(wkv_hbm.at[:, pl.ds(0, width)], wk_s), fetch(wvt_hbm, wvt_s)]
    score_in = [fetch(qt_hbm, qt_s), fetch(ltop_hbm, ltop_ref), fetch(lsum_hbm, lsum_ref)]

    order = swap16() if split else None
    lane_head = lax.broadcasted_iota(jnp.int32, (1, 128), 1) // HEAD
    heads = [(lane_head == h).astype(BF16) for h in range(128 // HEAD)]
    none = jnp.zeros((remote, 128), BF16)
    own_block = (
        lax.broadcasted_iota(jnp.int32, (width, H * remote), 0) // HEAD
        == lax.broadcasted_iota(jnp.int32, (width, H * remote), 1) // remote
    ).astype(BF16)
    slot = lax.broadcasted_iota(jnp.int32, (remote, block), 0) // REMOTE_SENSORS
    live = jnp.zeros((remote, block), jnp.int32)
    for j in range(slots):
        live = jnp.where(slot == j, numbers_ref[1 + slots + j], live)
    live = live > 0

    for copy in first_in:
        copy.wait()
    merge_in = [fetch(lctx_hbm, lctx_s)]
    x_in, place = [fetch(wo_hbm, wo_s)], 0
    for p in pieces:
        x_in.append(fetch(p, x_s.at[:, pl.ds(place, p.shape[1])]))
        place += p.shape[1]
    ffn_in = [fetch(gain_ffn_hbm, gain_ffn_ref), fetch(w_in_hbm, w_in_s), fetch(w_out_hbm, w_out_s)]
    if split:
        for j in range(slots):
            raw_s[j * REMOTE_SENSORS : (j + 1) * REMOTE_SENSORS] = in_ref[numbers_ref[1 + j]]
        for b in range(remote // 16):
            rows = raw_s[b * 16 : (b + 1) * 16].reshape(256, width)
            rn_s[:, b * 16 : (b + 1) * 16, :] = dot(order, rows).astype(BF16).reshape(16, 16, width)
        raw = rn_s[...]
    else:
        raw = in_ref[...]
    normed = rms(raw.reshape(steps * remote, width).astype(F32), gain_ref[...])
    rn_s[...] = normed.reshape(steps, remote, width)
    rk_s[...] = dot(normed, wk_s[...]).astype(BF16).reshape(steps, remote, width)

    for copy in score_in:
        copy.wait()
    keys = []
    for t in range(steps):
        rk = rk_s[t]
        spread = []
        for h in range(H):
            half = h * HEAD // 128
            part = rk[:, half * 128 : (half + 1) * 128] * heads[h % (128 // HEAD)]
            spread.append(jnp.concatenate([part, none] if half == 0 else [none, part], axis=1))
        keys.append(jnp.concatenate(spread, axis=0))
    scores = [dot(keys[t], qt_s[t]).reshape(H, remote, block) for t in range(steps)]
    values = []
    for t in range(steps):
        tiled = jnp.concatenate([rn_s[t]] * H, axis=0)
        values.append(dot_nt(wvt_s[...], tiled).astype(BF16) * own_block)
    weights, keeps = [], []
    for t in range(steps):
        masked = jnp.where(live[None], scores[t], NEG)
        ltop = ltop_ref[t]
        top = jnp.maximum(jnp.max(masked, axis=1), ltop)
        e = jnp.exp2((masked - top[:, None, :]) * SCALE)
        keep = jnp.exp2((ltop - top) * SCALE)
        inverse = 1.0 / (jnp.sum(e, axis=1) + lsum_ref[t] * keep)
        keeps.append(keep * inverse)
        weights.append((e * inverse[:, None, :]).astype(BF16).reshape(H * remote, block))
    far = [dot(values[t], weights[t]).reshape(H, HEAD, block) for t in range(steps)]
    for copy in merge_in:
        copy.wait()
    for t in range(steps):
        merged = lctx_s[t].astype(F32).reshape(H, HEAD, block) * keeps[t][:, None, :] + far[t]
        ctx_s[t] = merged.reshape(width, block).astype(BF16).T

    for copy in x_in + ffn_in:
        copy.wait()
    tile = width
    tiles = w_in_s.shape[1] // tile
    work = [(first, n) for first in range(0, block, sb) for n in range(tiles)]
    ready, total, copies = {}, {}, []

    def open_rows(first):
        rows = lambda ref: ref[:, first : first + sb, :].reshape(steps * sb, width)
        after = rows(x_s).astype(F32) + dot(rows(ctx_s), wo_s[...])
        total[first] = after
        ready[first] = rms(after, gain_ffn_ref[...])

    def up(first, n):
        return dot(ready[first], w_in_s[:, n * tile : (n + 1) * tile])

    open_rows(0)
    upper = up(*work[0])
    for k, (first, n) in enumerate(work):
        if n == 0 and first + sb < block:
            open_rows(first + sb)
        later = up(*work[k + 1]) if k + 1 < len(work) else None
        total[first] = total[first] + dot(gelu(upper).astype(BF16), w_out_s[n * tile : (n + 1) * tile, :])
        upper = later
        if n < tiles - 1:
            continue
        y = total[first].astype(BF16).reshape(steps, sb, width)
        if not split:
            out_s[:, first : first + sb, :] = y
            continue
        for b in range(sb // 16):
            turned = dot(order, y[:, b * 16 : (b + 1) * 16].reshape(256, width)).astype(BF16)
            out_s[first + b * 16 : first + (b + 1) * 16] = turned.reshape(16, steps, width)
        half = block // 2
        owner = numbers_ref[0] if first < half else 1 - numbers_ref[0]
        place = out_hbm.at[pl.ds(owner * half + first % half, sb)]
        copies.append(pltpu.make_async_copy(out_s.at[pl.ds(first, sb)], place, out_sems.at[first // sb]))
        copies[-1].start()
    if not split:
        copies.append(pltpu.make_async_copy(out_s, out_hbm, out_sems.at[0]))
        copies[-1].start()
    for copy in copies:
        copy.wait()


def finish(numbers, pieces, incoming, local, gain, wkv, wo, gain_ffn, w_in, w_out, split):
    qt, lctx, ltop, lsum, wvt = local
    steps, width, block = qt.shape
    remote = (numbers.shape[0] - 1) // 2 * REMOTE_SENSORS
    sb = 32
    hbm = pl.BlockSpec(memory_space=pl.ANY)
    n_copies = 12 + len(pieces)
    far = (*pieces, incoming, gain, gain_ffn, ltop, lsum, qt, lctx, wkv, wvt, wo, w_in, w_out)
    far = [a if a is incoming else pltpu.with_memory_space_constraint(a, pltpu.HBM) for a in far]
    buffer = lambda *shape: pltpu.VMEM(shape, BF16)
    return pl.pallas_call(
        functools.partial(finish_kernel, len(pieces), split, sb),
        out_shape=jax.ShapeDtypeStruct((block, steps, width) if split else (steps, block, width), BF16),
        in_specs=[pl.BlockSpec(memory_space=pltpu.SMEM)] + [pl.BlockSpec(memory_space=pltpu.VMEM) if a is incoming else hbm for a in far],
        out_specs=hbm,
        scratch_shapes=[
            buffer(steps, block, width),
            buffer(remote, steps, width),
            buffer(steps, remote, width),
            buffer(steps, remote, width),
            buffer(steps, block, width),
            buffer(block, steps, width) if split else buffer(steps, block, width),
            buffer(steps, width, block),
            buffer(steps, width, block),
            buffer(width, width),
            buffer(width, width),
            buffer(*wo.shape),
            buffer(*w_in.shape),
            buffer(*w_out.shape),
            pltpu.VMEM(gain.shape, F32),
            pltpu.VMEM(gain_ffn.shape, F32),
            pltpu.VMEM(ltop.shape, F32),
            pltpu.VMEM(lsum.shape, F32),
            pltpu.SemaphoreType.DMA((n_copies,)),
            pltpu.SemaphoreType.DMA((block // sb,)),
        ],
        compiler_params=pltpu.CompilerParams(vmem_limit_bytes=VMEM_LIMIT),
        cost_estimate=pl.CostEstimate(
            flops=steps * block * width * width * 18, bytes_accessed=steps * block * width * 12, transcendentals=0
        ),
        name="remote_keys_and_feed_forward",
    )(numbers, *far)


def local(
    tm,
    tokens,
    gain_time,
    wq_time,
    wkv_time,
    wo_time,
    gain_graph,
    wq_graph,
    wkv_graph,
    wo_graph,
    gain_ffn,
    w_in,
    w_out,
    neighbour_blocks,
    slot_used_mask,
    neighbour_rows,
):
    sensors_here, steps, width = tokens.shape
    block = sensors_here * tm
    group = steps // tm
    block_count, slots = neighbour_blocks.shape
    split = tm == 2 and group == 16 and sensors_here % 32 == 0
    gain_time, gain_graph, gain_ffn = (g.reshape(1, width) for g in (gain_time, gain_graph, gain_ffn))
    mine = lax.axis_index("tm").astype(jnp.int32)
    block_index = lax.axis_index("sensor")
    time = lambda x, *where: time_block(x, mine.reshape(1), gain_time, wq_time, wkv_time, wo_time, *where)
    if split:
        kept, got = [], []
        first = 0
        for share in SHARES:
            size = sensors_here * share // sum(SHARES)
            keep, send = time(tokens, first, size, True)
            tokens, send = lax.optimization_barrier((tokens, send))
            kept.append(keep)
            got.append(lax.ppermute(send, "tm", [(0, 1), (1, 0)]))
            first += size
        pieces = kept + got
    else:
        whole = lax.all_to_all(time(tokens, 0, sensors_here, False), "tm", split_axis=1, concat_axis=0, tiled=True)
        pieces = [whole.transpose(1, 0, 2)]
    matches = (neighbour_blocks == block_index).astype(jnp.int32)
    wanted = jnp.sum(matches[:, :, None] * neighbour_rows, axis=1).reshape(-1)
    own = lax.dynamic_index_in_dim(neighbour_blocks, block_index, 0, keepdims=False)
    numbers = jnp.concatenate([mine.reshape(1), own, slot_used_mask[0]])
    if split:
        place = (jnp.arange(block) + mine * sensors_here) % block
        pick = (wanted[:, None] == place[None, :]).astype(BF16)
        outgoing = pick_rows(pick, pieces)
    else:
        outgoing = jnp.take(whole, wanted, axis=0)
    outgoing = outgoing.reshape(block_count, REMOTE_SENSORS, group, width)
    incoming = lax.all_to_all(outgoing, "sensor", split_axis=0, concat_axis=0, tiled=True)
    if not split:
        incoming = jnp.take(incoming, own, axis=0).reshape(-1, group, width).transpose(1, 0, 2)
    near = local_part(pieces, gain_graph, wq_graph, wkv_graph)
    out = finish(numbers, pieces, incoming, near, gain_graph, wkv_graph, wo_graph, gain_ffn, w_in, w_out, split)
    return out if split else out.transpose(1, 0, 2)


def solution(mesh):
    in_specs = (
        P(("sensor", "tm"), None, None),
        P(),
        P(),
        P(),
        P(),
        P(),
        P(),
        P(),
        P(),
        P(),
        P(),
        P(),
        P(),
        P("sensor", None),
        P(),
    )
    out_specs = P("sensor", "tm", None)
    body = functools.partial(local, mesh.shape["tm"])
    return jax.shard_map(body, mesh=mesh, in_specs=in_specs, out_specs=out_specs, check_vma=False)
```

```python
import functools
import math

import jax
import jax.numpy as jnp
from jax import lax
from jax.experimental import pallas as pl
from jax.experimental.pallas import tpu as pltpu
from jax.sharding import PartitionSpec as P

H = 8
HEAD = 32
REMOTE_SENSORS = 4
EPSILON = 1e-06
NEG = -1e30
SCALE = math.log2(math.e) / math.sqrt(HEAD)
SHARES = (1, 1, 1, 1)
F32 = jnp.float32
BF16 = jnp.bfloat16
VMEM_LIMIT = 28 * 1024 * 1024


def dot(a, b):
    return jnp.dot(a, b, preferred_element_type=F32)


def dot_nt(a, b):
    return lax.dot_general(a, b, (((1,), (1,)), ((), ())), preferred_element_type=F32)


def dot_tn(a, b):
    return lax.dot_general(a, b, (((0,), (0,)), ((), ())), preferred_element_type=F32)


def rms(x, gain):
    inverse = lax.rsqrt(jnp.mean(x * x, axis=-1, keepdims=True) + EPSILON)
    return (x * inverse * gain).astype(BF16)


def swap16():
    row = lax.broadcasted_iota(jnp.int32, (256, 256), 0)
    col = lax.broadcasted_iota(jnp.int32, (256, 256), 1)
    return (col == ((row & 15) << 4) + (row >> 4)).astype(BF16)


def head_rows(rows, lanes, head_of_row, first_head):
    row = lax.broadcasted_iota(jnp.int32, (rows, lanes), 0)
    lane = lax.broadcasted_iota(jnp.int32, (rows, lanes), 1)
    return (lane // HEAD + first_head == row // head_of_row).astype(BF16)


def time_kernel(split, my_ref, x_ref, gain_ref, wq_ref, wkv_ref, wo_ref, *refs):
    if split:
        keep_ref, send_ref, q_s, k_s, v_s, a_s, c_s, after_s = refs
    else:
        out_ref, q_s, k_s, v_s, a_s, c_s = refs
    sensors, steps, width = x_ref.shape
    rows = sensors * steps
    x = x_ref[...].reshape(rows, width).astype(F32)
    normed = rms(x, gain_ref[...])
    q_s[...] = dot(normed, wq_ref[...]).astype(BF16)
    kv = dot(normed, wkv_ref[...]).astype(BF16)
    k_s[...] = kv[:, :width]
    v_s[...] = kv[:, width:]
    lanes = H * steps
    near = 128 // HEAD
    span = near * steps
    mask = head_rows(span, 128, steps, 0)
    none = jnp.zeros((span, 128), BF16)
    key_t = lax.broadcasted_iota(jnp.int32, (steps, lanes), 0)
    query_t = lax.broadcasted_iota(jnp.int32, (steps, lanes), 1) & (steps - 1)
    causal = key_t <= query_t
    for s in range(sensors):
        here = slice(s * steps, (s + 1) * steps)
        first, second = (jnp.concatenate([q_s[here, c : c + 128]] * near, axis=0) * mask for c in (0, 128))
        spread = jnp.concatenate(
            [jnp.concatenate([first, none], axis=1), jnp.concatenate([none, second], axis=1)], axis=0
        )
        scores = jnp.where(causal, dot_nt(k_s[here, :], spread), NEG)
        top = jnp.max(scores, axis=0, keepdims=True)
        e = jnp.exp2((scores - top) * SCALE)
        a_s[here, :] = (e * (1.0 / jnp.sum(e, axis=0, keepdims=True))).astype(BF16)
    lane_head = lax.broadcasted_iota(jnp.int32, (steps, 128), 1) // HEAD
    for g in range(rows // 128):
        turned = a_s[g * 128 : (g + 1) * 128, :].T
        for half in range(2):
            cols = slice(half * 128, (half + 1) * 128)
            for s in range(0, 128 // steps, 2):
                columns = []
                for r in (s, s + 1):
                    v = v_s[g * 128 + r * steps : g * 128 + (r + 1) * steps, cols]
                    parts = [jnp.zeros((r * steps, 128), BF16), v, jnp.zeros((128 - (r + 1) * steps, 128), BF16)]
                    columns.append(jnp.concatenate([p for p in parts if p.shape[0]], axis=0))
                wide = dot(turned[half * span : (half + 1) * span], jnp.concatenate(columns, axis=1))
                for i in range(2):
                    ctx = wide[:steps, i * 128 : (i + 1) * 128]
                    for h in range(1, near):
                        ctx = jnp.where(lane_head == h, wide[h * steps : (h + 1) * steps, i * 128 : (i + 1) * 128], ctx)
                    at = g * 128 + (s + i) * steps
                    c_s[at : at + steps, cols] = ctx.astype(BF16)
    after = (x + dot(c_s[...], wo_ref[...])).astype(BF16)
    if not split:
        out_ref[...] = after.reshape(sensors, steps, width)
        return
    after_s[...] = after.reshape(sensors, steps, width)
    order = swap16()
    mine = my_ref[0]
    for ref, part in ((keep_ref, mine), (send_ref, 1 - mine)):
        rows16 = after_s[:, pl.ds(pl.multiple_of(part * 16, 16), 16), :]
        for b in range(sensors // 16):
            block = rows16[b * 16 : (b + 1) * 16].reshape(256, width)
            ref[:, b * 16 : (b + 1) * 16, :] = dot(order, block).astype(BF16).reshape(16, 16, width)


def time_block(tokens, my, gain, wq, wkv, wo, first, count, split):
    steps, width = tokens.shape[1:]
    if first == 0:
        tokens, gain, wq, wkv, wo = (pltpu.with_memory_space_constraint(a, pltpu.HBM) for a in (tokens, gain, wq, wkv, wo))
    sb = min(16, count)
    rows = sb * steps
    full = lambda a: pl.BlockSpec(a.shape, lambda i, *_: (0,) * a.ndim)
    if split:
        out_shape = [jax.ShapeDtypeStruct((16, count, width), BF16)] * 2
        out_specs = [pl.BlockSpec((16, sb, width), lambda i, *_: (0, i, 0))] * 2
        extra = [pltpu.VMEM((sb, steps, width), BF16)]
    else:
        out_shape = jax.ShapeDtypeStruct((count, steps, width), BF16)
        out_specs = pl.BlockSpec((sb, steps, width), lambda i, *_: (i, 0, 0))
        extra = []
    return pl.pallas_call(
        functools.partial(time_kernel, split),
        out_shape=out_shape,
        grid_spec=pltpu.PrefetchScalarGridSpec(
            num_scalar_prefetch=1,
            grid=(count // sb,),
            in_specs=[
                pl.BlockSpec((sb, steps, width), lambda i, *_: (first // sb + i, 0, 0)),
                full(gain),
                full(wq),
                full(wkv),
                full(wo),
            ],
            out_specs=out_specs,
            scratch_shapes=[pltpu.VMEM((rows, width), BF16)] * 5 + extra,
        ),
        compiler_params=pltpu.CompilerParams(vmem_limit_bytes=VMEM_LIMIT),
        cost_estimate=pl.CostEstimate(
            flops=count * steps * width * width * 12, bytes_accessed=count * steps * width * 4, transcendentals=0
        ),
        name="time_block",
    )(my, tokens, gain, wq, wkv, wo)


def pick_kernel(n, pick_ref, *refs):
    pieces, (out_ref, o_s) = refs[:n], refs[n:]
    steps = out_ref.shape[1]
    wanted = out_ref.shape[0]
    order = swap16()
    pick = pick_ref[...]
    for t in range(steps):
        rows = jnp.concatenate([p[t] for p in pieces], axis=0)
        o_s[t] = dot(pick, rows).astype(BF16)
    for b in range(wanted // 16):
        block = o_s[:, b * 16 : (b + 1) * 16, :].reshape(256, 256)
        out_ref[b * 16 : (b + 1) * 16] = dot(order, block).astype(BF16).reshape(16, 16, 256)


def pick_rows(pick, pieces):
    steps, _, width = pieces[0].shape
    wanted = pick.shape[0]
    return pl.pallas_call(
        functools.partial(pick_kernel, len(pieces)),
        out_shape=jax.ShapeDtypeStruct((wanted, steps, width), BF16),
        scratch_shapes=[pltpu.VMEM((steps, wanted, width), BF16)],
        compiler_params=pltpu.CompilerParams(vmem_limit_bytes=VMEM_LIMIT),
        name="pick_rows",
    )(pick, *pieces)


def pair_scores(q, k, masks, pair):
    cols = slice(pair // 2 * 128, pair // 2 * 128 + 128)
    spread = jnp.concatenate([q[:, cols]] * 2, axis=0) * masks[pair % 2]
    return dot_nt(k[:, cols], spread)


def local_kernel(n, *refs):
    pieces = refs[:n]
    gain_ref, wq_ref, wkv_ref, qt_ref, ctx_ref, top_ref, sum_ref, wvt_ref, wqt_s = refs[n:]
    tb, width, block = qt_ref.shape

    @pl.when(pl.program_id(0) == 0)
    def _():
        wvt_ref[...] = wkv_ref[:, width:].T
        wqt_s[...] = wq_ref[...].T

    x = jnp.concatenate([p[t] for t in range(tb) for p in pieces], axis=0).astype(F32)
    normed = rms(x, gain_ref[...])
    q = dot(normed, wq_ref[...]).astype(BF16)
    k = dot(normed, wkv_ref[:, :width]).astype(BF16)
    masks = [head_rows(2 * block, 128, block, -2 * p) for p in range(2)]
    for t in range(tb):
        here = slice(t * block, (t + 1) * block)
        qt_ref[t] = dot_nt(wqt_s[...], normed[here]).astype(BF16)
        vt = dot_nt(wvt_ref[...], normed[here]).astype(BF16)
        scores = [pair_scores(q[here], k[here], masks, pair) for pair in range(H // 2)]
        tops = [jnp.max(x, axis=0, keepdims=True) for x in scores]
        es = [jnp.exp2((x - top) * SCALE) for x, top in zip(scores, tops)]
        for pair, e in enumerate(es):
            lo = pair * 2 * HEAD
            both = dot(vt[lo : lo + 2 * HEAD], e.astype(BF16))
            total = jnp.sum(e, axis=0, keepdims=True)
            for i in range(2):
                lanes = slice(i * block, (i + 1) * block)
                head = 2 * pair + i
                ctx_ref[t, lo + i * HEAD : lo + (i + 1) * HEAD, :] = both[i * HEAD : (i + 1) * HEAD, lanes].astype(BF16)
                top_ref[t, head : head + 1, :] = tops[pair][:, lanes]
                sum_ref[t, head : head + 1, :] = total[:, lanes]


def local_part(pieces, gain, wq, wkv):
    steps, _, width = pieces[0].shape
    block = sum(p.shape[1] for p in pieces)
    tb = 4
    full = lambda a: pl.BlockSpec(a.shape, lambda i: (0,) * a.ndim)
    per_t = lambda *shape: pl.BlockSpec((tb,) + shape, lambda i: (i, 0, 0))
    return pl.pallas_call(
        functools.partial(local_kernel, len(pieces)),
        out_shape=[
            pltpu.HBM((steps, width, block), BF16),
            pltpu.HBM((steps, width, block), BF16),
            pltpu.HBM((steps, H, block), F32),
            pltpu.HBM((steps, H, block), F32),
            pltpu.HBM((width, width), BF16),
        ],
        grid=(steps // tb,),
        in_specs=[per_t(p.shape[1], width) for p in pieces] + [full(gain), full(wq), full(wkv)],
        out_specs=[
            per_t(width, block),
            per_t(width, block),
            per_t(H, block),
            per_t(H, block),
            pl.BlockSpec((width, width), lambda i: (0, 0)),
        ],
        scratch_shapes=[pltpu.VMEM((width, width), BF16)],
        compiler_params=pltpu.CompilerParams(vmem_limit_bytes=VMEM_LIMIT),
        cost_estimate=pl.CostEstimate(
            flops=steps * block * width * width * 12, bytes_accessed=steps * block * width * 10, transcendentals=0
        ),
        name="local_keys",
    )(*pieces, gain, wq, wkv)


def gelu(x):
    inner = x * (0.7978845608028654 + 0.035677408136300125 * (x * x))
    half = 0.5 * x
    return half + half * jnp.tanh(inner)


def finish_kernel(n, split, sb, numbers_ref, *refs):
    pieces = refs[:n]
    in_ref, gain_hbm, gain_ffn_hbm, ltop_hbm, lsum_hbm = refs[n : n + 5]
    qt_hbm, lctx_hbm, wkv_hbm, wvt_hbm, wo_hbm, w_in_hbm, w_out_hbm, out_hbm = refs[n + 5 : n + 13]
    (x_s, raw_s, rn_s, rk_s, ctx_s, out_s, qt_s, lctx_s, wk_s, wvt_s, wo_s, w_in_s, w_out_s, gain_ref, gain_ffn_ref,
     ltop_ref, lsum_ref, sems, out_sems) = refs[n + 13 :]
    steps, width, block = qt_s.shape
    remote = rn_s.shape[1]
    slots = remote // REMOTE_SENSORS
    count = [0]

    def fetch(src, dst):
        copy = pltpu.make_async_copy(src, dst, sems.at[count[0]])
        count[0] += 1
        copy.start()
        return copy

    first_in = [fetch(gain_hbm, gain_ref), fetch(wkv_hbm.at[:, pl.ds(0, width)], wk_s), fetch(wvt_hbm, wvt_s)]
    score_in = [fetch(qt_hbm, qt_s), fetch(ltop_hbm, ltop_ref), fetch(lsum_hbm, lsum_ref)]

    order = swap16() if split else None
    lane_head = lax.broadcasted_iota(jnp.int32, (1, 128), 1) // HEAD
    heads = [(lane_head == h).astype(BF16) for h in range(128 // HEAD)]
    none = jnp.zeros((remote, 128), BF16)
    own_block = (
        lax.broadcasted_iota(jnp.int32, (width, H * remote), 0) // HEAD
        == lax.broadcasted_iota(jnp.int32, (width, H * remote), 1) // remote
    ).astype(BF16)
    slot = lax.broadcasted_iota(jnp.int32, (remote, block), 0) // REMOTE_SENSORS
    live = jnp.zeros((remote, block), jnp.int32)
    for j in range(slots):
        live = jnp.where(slot == j, numbers_ref[1 + slots + j], live)
    live = live > 0

    for copy in first_in:
        copy.wait()
    merge_in = [fetch(lctx_hbm, lctx_s)]
    x_in, place = [fetch(wo_hbm, wo_s)], 0
    for p in pieces:
        x_in.append(fetch(p, x_s.at[:, pl.ds(place, p.shape[1])]))
        place += p.shape[1]
    ffn_in = [fetch(gain_ffn_hbm, gain_ffn_ref), fetch(w_in_hbm, w_in_s), fetch(w_out_hbm, w_out_s)]
    if split:
        for j in range(slots):
            raw_s[j * REMOTE_SENSORS : (j + 1) * REMOTE_SENSORS] = in_ref[numbers_ref[1 + j]]
        for b in range(remote // 16):
            rows = raw_s[b * 16 : (b + 1) * 16].reshape(256, width)
            rn_s[:, b * 16 : (b + 1) * 16, :] = dot(order, rows).astype(BF16).reshape(16, 16, width)
        raw = rn_s[...]
    else:
        raw = in_ref[...]
    normed = rms(raw.reshape(steps * remote, width).astype(F32), gain_ref[...])
    rn_s[...] = normed.reshape(steps, remote, width)
    rk_s[...] = dot(normed, wk_s[...]).astype(BF16).reshape(steps, remote, width)

    for copy in score_in:
        copy.wait()
    keys = []
    for t in range(steps):
        rk = rk_s[t]
        spread = []
        for h in range(H):
            half = h * HEAD // 128
            part = rk[:, half * 128 : (half + 1) * 128] * heads[h % (128 // HEAD)]
            spread.append(jnp.concatenate([part, none] if half == 0 else [none, part], axis=1))
        keys.append(jnp.concatenate(spread, axis=0))
    scores = [dot(keys[t], qt_s[t]).reshape(H, remote, block) for t in range(steps)]
    values = []
    for t in range(steps):
        tiled = jnp.concatenate([rn_s[t]] * H, axis=0)
        values.append(dot_nt(wvt_s[...], tiled).astype(BF16) * own_block)
    weights, keeps = [], []
    for t in range(steps):
        masked = jnp.where(live[None], scores[t], NEG)
        ltop = ltop_ref[t]
        top = jnp.maximum(jnp.max(masked, axis=1), ltop)
        e = jnp.exp2((masked - top[:, None, :]) * SCALE)
        keep = jnp.exp2((ltop - top) * SCALE)
        inverse = 1.0 / (jnp.sum(e, axis=1) + lsum_ref[t] * keep)
        keeps.append(keep * inverse)
        weights.append((e * inverse[:, None, :]).astype(BF16).reshape(H * remote, block))
    far = [dot(values[t], weights[t]).reshape(H, HEAD, block) for t in range(steps)]
    for copy in merge_in:
        copy.wait()
    for t in range(steps):
        merged = lctx_s[t].astype(F32).reshape(H, HEAD, block) * keeps[t][:, None, :] + far[t]
        ctx_s[t] = merged.reshape(width, block).astype(BF16).T

    for copy in x_in + ffn_in:
        copy.wait()
    tile = width
    tiles = w_in_s.shape[1] // tile
    work = [(first, n) for first in range(0, block, sb) for n in range(tiles)]
    ready, total, copies = {}, {}, []

    def open_rows(first):
        rows = lambda ref: ref[:, first : first + sb, :].reshape(steps * sb, width)
        after = rows(x_s).astype(F32) + dot(rows(ctx_s), wo_s[...])
        total[first] = after
        ready[first] = rms(after, gain_ffn_ref[...])

    def up(first, n):
        return dot(ready[first], w_in_s[:, n * tile : (n + 1) * tile])

    open_rows(0)
    upper = up(*work[0])
    for k, (first, n) in enumerate(work):
        if n == 0 and first + sb < block:
            open_rows(first + sb)
        later = up(*work[k + 1]) if k + 1 < len(work) else None
        total[first] = total[first] + dot(gelu(upper).astype(BF16), w_out_s[n * tile : (n + 1) * tile, :])
        upper = later
        if n < tiles - 1:
            continue
        y = total[first].astype(BF16).reshape(steps, sb, width)
        if not split:
            out_s[:, first : first + sb, :] = y
            continue
        for b in range(sb // 16):
            turned = dot(order, y[:, b * 16 : (b + 1) * 16].reshape(256, width)).astype(BF16)
            out_s[first + b * 16 : first + (b + 1) * 16] = turned.reshape(16, steps, width)
        half = block // 2
        owner = numbers_ref[0] if first < half else 1 - numbers_ref[0]
        place = out_hbm.at[pl.ds(owner * half + first % half, sb)]
        copies.append(pltpu.make_async_copy(out_s.at[pl.ds(first, sb)], place, out_sems.at[first // sb]))
        copies[-1].start()
    if not split:
        copies.append(pltpu.make_async_copy(out_s, out_hbm, out_sems.at[0]))
        copies[-1].start()
    for copy in copies:
        copy.wait()


def finish(numbers, pieces, incoming, local, gain, wkv, wo, gain_ffn, w_in, w_out, split):
    qt, lctx, ltop, lsum, wvt = local
    steps, width, block = qt.shape
    remote = (numbers.shape[0] - 1) // 2 * REMOTE_SENSORS
    sb = 32
    hbm = pl.BlockSpec(memory_space=pl.ANY)
    n_copies = 12 + len(pieces)
    far = (*pieces, incoming, gain, gain_ffn, ltop, lsum, qt, lctx, wkv, wvt, wo, w_in, w_out)
    far = [a if a is incoming else pltpu.with_memory_space_constraint(a, pltpu.HBM) for a in far]
    buffer = lambda *shape: pltpu.VMEM(shape, BF16)
    return pl.pallas_call(
        functools.partial(finish_kernel, len(pieces), split, sb),
        out_shape=jax.ShapeDtypeStruct((block, steps, width) if split else (steps, block, width), BF16),
        in_specs=[pl.BlockSpec(memory_space=pltpu.SMEM)] + [pl.BlockSpec(memory_space=pltpu.VMEM) if a is incoming else hbm for a in far],
        out_specs=hbm,
        scratch_shapes=[
            buffer(steps, block, width),
            buffer(remote, steps, width),
            buffer(steps, remote, width),
            buffer(steps, remote, width),
            buffer(steps, block, width),
            buffer(block, steps, width) if split else buffer(steps, block, width),
            buffer(steps, width, block),
            buffer(steps, width, block),
            buffer(width, width),
            buffer(width, width),
            buffer(*wo.shape),
            buffer(*w_in.shape),
            buffer(*w_out.shape),
            pltpu.VMEM(gain.shape, F32),
            pltpu.VMEM(gain_ffn.shape, F32),
            pltpu.VMEM(ltop.shape, F32),
            pltpu.VMEM(lsum.shape, F32),
            pltpu.SemaphoreType.DMA((n_copies,)),
            pltpu.SemaphoreType.DMA((block // sb,)),
        ],
        compiler_params=pltpu.CompilerParams(vmem_limit_bytes=VMEM_LIMIT),
        cost_estimate=pl.CostEstimate(
            flops=steps * block * width * width * 18, bytes_accessed=steps * block * width * 12, transcendentals=0
        ),
        name="remote_keys_and_feed_forward",
    )(numbers, *far)


def local(
    tm,
    tokens,
    gain_time,
    wq_time,
    wkv_time,
    wo_time,
    gain_graph,
    wq_graph,
    wkv_graph,
    wo_graph,
    gain_ffn,
    w_in,
    w_out,
    neighbour_blocks,
    slot_used_mask,
    neighbour_rows,
):
    sensors_here, steps, width = tokens.shape
    block = sensors_here * tm
    group = steps // tm
    block_count, slots = neighbour_blocks.shape
    split = tm == 2 and group == 16 and sensors_here % 32 == 0
    gain_time, gain_graph, gain_ffn = (g.reshape(1, width) for g in (gain_time, gain_graph, gain_ffn))
    mine = lax.axis_index("tm").astype(jnp.int32)
    block_index = lax.axis_index("sensor")
    time = lambda x, *where: time_block(x, mine.reshape(1), gain_time, wq_time, wkv_time, wo_time, *where)
    if split:
        kept, got = [], []
        first = 0
        for share in SHARES:
            size = sensors_here * share // sum(SHARES)
            keep, send = time(tokens, first, size, True)
            tokens, send = lax.optimization_barrier((tokens, send))
            kept.append(keep)
            got.append(lax.ppermute(send, "tm", [(0, 1), (1, 0)]))
            first += size
        pieces = kept + got
    else:
        whole = lax.all_to_all(time(tokens, 0, sensors_here, False), "tm", split_axis=1, concat_axis=0, tiled=True)
        pieces = [whole.transpose(1, 0, 2)]
    matches = (neighbour_blocks == block_index).astype(jnp.int32)
    wanted = jnp.sum(matches[:, :, None] * neighbour_rows, axis=1).reshape(-1)
    own = lax.dynamic_index_in_dim(neighbour_blocks, block_index, 0, keepdims=False)
    numbers = jnp.concatenate([mine.reshape(1), own, slot_used_mask[0]])
    if split:
        place = (jnp.arange(block) + mine * sensors_here) % block
        pick = (wanted[:, None] == place[None, :]).astype(BF16)
        outgoing = pick_rows(pick, pieces)
    else:
        outgoing = jnp.take(whole, wanted, axis=0)
    outgoing = outgoing.reshape(block_count, REMOTE_SENSORS, group, width)
    incoming = lax.all_to_all(outgoing, "sensor", split_axis=0, concat_axis=0, tiled=True)
    if not split:
        incoming = jnp.take(incoming, own, axis=0).reshape(-1, group, width).transpose(1, 0, 2)
    near = local_part(pieces, gain_graph, wq_graph, wkv_graph)
    out = finish(numbers, pieces, incoming, near, gain_graph, wkv_graph, wo_graph, gain_ffn, w_in, w_out, split)
    return out if split else out.transpose(1, 0, 2)


def solution(mesh):
    in_specs = (
        P(("sensor", "tm"), None, None),
        P(),
        P(),
        P(),
        P(),
        P(),
        P(),
        P(),
        P(),
        P(),
        P(),
        P(),
        P(),
        P("sensor", None),
        P(),
    )
    out_specs = P("sensor", "tm", None)
    body = functools.partial(local, mesh.shape["tm"])
    return jax.shard_map(body, mesh=mesh, in_specs=in_specs, out_specs=out_specs, check_vma=False)
```

```python
import functools
import math

import jax
import jax.numpy as jnp
from jax import lax
from jax.experimental import pallas as pl
from jax.experimental.pallas import tpu as pltpu
from jax.sharding import PartitionSpec as P

H = 8
HEAD = 32
REMOTE_SENSORS = 4
EPSILON = 1e-06
NEG = -1e30
SCALE = math.log2(math.e) / math.sqrt(HEAD)
SHARES = (1, 1, 1, 1)
F32 = jnp.float32
BF16 = jnp.bfloat16
VMEM_LIMIT = 28 * 1024 * 1024


def dot(a, b):
    return jnp.dot(a, b, preferred_element_type=F32)


def dot_nt(a, b):
    return lax.dot_general(a, b, (((1,), (1,)), ((), ())), preferred_element_type=F32)


def dot_tn(a, b):
    return lax.dot_general(a, b, (((0,), (0,)), ((), ())), preferred_element_type=F32)


def rms(x, gain):
    inverse = lax.rsqrt(jnp.mean(x * x, axis=-1, keepdims=True) + EPSILON)
    return (x * inverse * gain).astype(BF16)


def swap16():
    row = lax.broadcasted_iota(jnp.int32, (256, 256), 0)
    col = lax.broadcasted_iota(jnp.int32, (256, 256), 1)
    return (col == ((row & 15) << 4) + (row >> 4)).astype(BF16)


def head_rows(rows, lanes, head_of_row, first_head):
    row = lax.broadcasted_iota(jnp.int32, (rows, lanes), 0)
    lane = lax.broadcasted_iota(jnp.int32, (rows, lanes), 1)
    return (lane // HEAD + first_head == row // head_of_row).astype(BF16)


def time_kernel(split, my_ref, x_ref, gain_ref, wq_ref, wkv_ref, wo_ref, *refs):
    if split:
        keep_ref, send_ref, q_s, k_s, v_s, a_s, c_s, after_s = refs
    else:
        out_ref, q_s, k_s, v_s, a_s, c_s = refs
    sensors, steps, width = x_ref.shape
    rows = sensors * steps
    x = x_ref[...].reshape(rows, width).astype(F32)
    normed = rms(x, gain_ref[...])
    q_s[...] = dot(normed, wq_ref[...]).astype(BF16)
    kv = dot(normed, wkv_ref[...]).astype(BF16)
    k_s[...] = kv[:, :width]
    v_s[...] = kv[:, width:]
    lanes = H * steps
    near = 128 // HEAD
    span = near * steps
    mask = head_rows(span, 128, steps, 0)
    none = jnp.zeros((span, 128), BF16)
    key_t = lax.broadcasted_iota(jnp.int32, (steps, lanes), 0)
    query_t = lax.broadcasted_iota(jnp.int32, (steps, lanes), 1) & (steps - 1)
    causal = key_t <= query_t
    for s in range(sensors):
        here = slice(s * steps, (s + 1) * steps)
        first, second = (jnp.concatenate([q_s[here, c : c + 128]] * near, axis=0) * mask for c in (0, 128))
        spread = jnp.concatenate(
            [jnp.concatenate([first, none], axis=1), jnp.concatenate([none, second], axis=1)], axis=0
        )
        scores = jnp.where(causal, dot_nt(k_s[here, :], spread), NEG)
        top = jnp.max(scores, axis=0, keepdims=True)
        e = jnp.exp2((scores - top) * SCALE)
        a_s[here, :] = (e * (1.0 / jnp.sum(e, axis=0, keepdims=True))).astype(BF16)
    lane_head = lax.broadcasted_iota(jnp.int32, (steps, 128), 1) // HEAD
    for g in range(rows // 128):
        turned = a_s[g * 128 : (g + 1) * 128, :].T
        for half in range(2):
            cols = slice(half * 128, (half + 1) * 128)
            for s in range(0, 128 // steps, 2):
                columns = []
                for r in (s, s + 1):
                    v = v_s[g * 128 + r * steps : g * 128 + (r + 1) * steps, cols]
                    parts = [jnp.zeros((r * steps, 128), BF16), v, jnp.zeros((128 - (r + 1) * steps, 128), BF16)]
                    columns.append(jnp.concatenate([p for p in parts if p.shape[0]], axis=0))
                wide = dot(turned[half * span : (half + 1) * span], jnp.concatenate(columns, axis=1))
                for i in range(2):
                    ctx = wide[:steps, i * 128 : (i + 1) * 128]
                    for h in range(1, near):
                        ctx = jnp.where(lane_head == h, wide[h * steps : (h + 1) * steps, i * 128 : (i + 1) * 128], ctx)
                    at = g * 128 + (s + i) * steps
                    c_s[at : at + steps, cols] = ctx.astype(BF16)
    after = (x + dot(c_s[...], wo_ref[...])).astype(BF16)
    if not split:
        out_ref[...] = after.reshape(sensors, steps, width)
        return
    after_s[...] = after.reshape(sensors, steps, width)
    order = swap16()
    mine = my_ref[0]
    for ref, part in ((keep_ref, mine), (send_ref, 1 - mine)):
        rows16 = after_s[:, pl.ds(pl.multiple_of(part * 16, 16), 16), :]
        for b in range(sensors // 16):
            block = rows16[b * 16 : (b + 1) * 16].reshape(256, width)
            ref[:, b * 16 : (b + 1) * 16, :] = dot(order, block).astype(BF16).reshape(16, 16, width)


def time_block(tokens, my, gain, wq, wkv, wo, first, count, split):
    steps, width = tokens.shape[1:]
    if first == 0:
        tokens, gain, wq, wkv, wo = (pltpu.with_memory_space_constraint(a, pltpu.HBM) for a in (tokens, gain, wq, wkv, wo))
    sb = min(16, count)
    rows = sb * steps
    full = lambda a: pl.BlockSpec(a.shape, lambda i, *_: (0,) * a.ndim)
    if split:
        out_shape = [jax.ShapeDtypeStruct((16, count, width), BF16)] * 2
        out_specs = [pl.BlockSpec((16, sb, width), lambda i, *_: (0, i, 0))] * 2
        extra = [pltpu.VMEM((sb, steps, width), BF16)]
    else:
        out_shape = jax.ShapeDtypeStruct((count, steps, width), BF16)
        out_specs = pl.BlockSpec((sb, steps, width), lambda i, *_: (i, 0, 0))
        extra = []
    return pl.pallas_call(
        functools.partial(time_kernel, split),
        out_shape=out_shape,
        grid_spec=pltpu.PrefetchScalarGridSpec(
            num_scalar_prefetch=1,
            grid=(count // sb,),
            in_specs=[
                pl.BlockSpec((sb, steps, width), lambda i, *_: (first // sb + i, 0, 0)),
                full(gain),
                full(wq),
                full(wkv),
                full(wo),
            ],
            out_specs=out_specs,
            scratch_shapes=[pltpu.VMEM((rows, width), BF16)] * 5 + extra,
        ),
        compiler_params=pltpu.CompilerParams(vmem_limit_bytes=VMEM_LIMIT),
        cost_estimate=pl.CostEstimate(
            flops=count * steps * width * width * 12, bytes_accessed=count * steps * width * 4, transcendentals=0
        ),
        name="time_block",
    )(my, tokens, gain, wq, wkv, wo)


def pick_kernel(n, pick_ref, *refs):
    pieces, (out_ref, o_s) = refs[:n], refs[n:]
    steps = out_ref.shape[1]
    wanted = out_ref.shape[0]
    order = swap16()
    pick = pick_ref[...]
    for t in range(steps):
        rows = jnp.concatenate([p[t] for p in pieces], axis=0)
        o_s[t] = dot(pick, rows).astype(BF16)
    for b in range(wanted // 16):
        block = o_s[:, b * 16 : (b + 1) * 16, :].reshape(256, 256)
        out_ref[b * 16 : (b + 1) * 16] = dot(order, block).astype(BF16).reshape(16, 16, 256)


def pick_rows(pick, pieces):
    steps, _, width = pieces[0].shape
    wanted = pick.shape[0]
    return pl.pallas_call(
        functools.partial(pick_kernel, len(pieces)),
        out_shape=jax.ShapeDtypeStruct((wanted, steps, width), BF16),
        scratch_shapes=[pltpu.VMEM((steps, wanted, width), BF16)],
        compiler_params=pltpu.CompilerParams(vmem_limit_bytes=VMEM_LIMIT),
        name="pick_rows",
    )(pick, *pieces)


def pair_scores(q, k, masks, pair):
    cols = slice(pair // 2 * 128, pair // 2 * 128 + 128)
    spread = jnp.concatenate([q[:, cols]] * 2, axis=0) * masks[pair % 2]
    return dot_nt(k[:, cols], spread)


def local_kernel(n, *refs):
    pieces = refs[:n]
    gain_ref, wq_ref, wkv_ref, qt_ref, ctx_ref, stat_ref, wqt_s, wvt_s = refs[n:]
    tb, width, block = qt_ref.shape

    @pl.when(pl.program_id(0) == 0)
    def _():
        wvt_s[...] = wkv_ref[:, width:].T
        wqt_s[...] = wq_ref[...].T

    x = jnp.concatenate([p[t] for t in range(tb) for p in pieces], axis=0).astype(F32)
    normed = rms(x, gain_ref[...])
    q = dot(normed, wq_ref[...]).astype(BF16)
    k = dot(normed, wkv_ref[:, :width]).astype(BF16)
    masks = [head_rows(2 * block, 128, block, -2 * p) for p in range(2)]
    for t in range(tb):
        here = slice(t * block, (t + 1) * block)
        qt_ref[t] = dot_nt(wqt_s[...], normed[here]).astype(BF16)
        vt = dot_nt(wvt_s[...], normed[here]).astype(BF16)
        scores = [pair_scores(q[here], k[here], masks, pair) for pair in range(H // 2)]
        tops = [jnp.max(x, axis=0, keepdims=True) for x in scores]
        es = [jnp.exp2((x - top) * SCALE) for x, top in zip(scores, tops)]
        context = []
        for pair, e in enumerate(es):
            lo = pair * 2 * HEAD
            both = dot(vt[lo : lo + 2 * HEAD], e.astype(BF16))
            total = jnp.sum(e, axis=0, keepdims=True)
            for i in range(2):
                lanes = slice(i * block, (i + 1) * block)
                head = 2 * pair + i
                context.append(both[i * HEAD : (i + 1) * HEAD, lanes].astype(BF16))
                stat_ref[t, head : head + 1, :] = tops[pair][:, lanes]
                stat_ref[t, H + head : H + head + 1, :] = total[:, lanes]
        ctx_ref[t] = jnp.concatenate(context, axis=0).T


def local_part(pieces, gain, wq, wkv):
    steps, _, width = pieces[0].shape
    block = sum(p.shape[1] for p in pieces)
    tb = 4
    full = lambda a: pl.BlockSpec(a.shape, lambda i: (0,) * a.ndim)
    per_t = lambda *shape: pl.BlockSpec((tb,) + shape, lambda i: (i, 0, 0))
    return pl.pallas_call(
        functools.partial(local_kernel, len(pieces)),
        out_shape=[
            pltpu.HBM((steps, width, block), BF16),
            pltpu.HBM((steps, block, width), BF16),
            jax.ShapeDtypeStruct((steps, 2 * H, block), F32),
        ],
        grid=(steps // tb,),
        in_specs=[per_t(p.shape[1], width) for p in pieces] + [full(gain), full(wq), full(wkv)],
        out_specs=[
            per_t(width, block),
            per_t(block, width),
            per_t(2 * H, block),
        ],
        scratch_shapes=[pltpu.VMEM((width, width), BF16)] * 2,
        compiler_params=pltpu.CompilerParams(vmem_limit_bytes=VMEM_LIMIT),
        cost_estimate=pl.CostEstimate(
            flops=steps * block * width * width * 12, bytes_accessed=steps * block * width * 10, transcendentals=0
        ),
        name="local_keys",
    )(*pieces, gain, wq, wkv)


def gelu(x):
    inner = x * (0.7978845608028654 + 0.035677408136300125 * (x * x))
    half = 0.5 * x
    return half + half * jnp.tanh(inner)


def rows_of(pieces, first, count):
    parts, start = [], 0
    for p in pieces:
        low, high = max(first, start), min(first + count, start + p.shape[1])
        if low < high:
            parts.append(p[:, low - start : high - start, :])
        start += p.shape[1]
    return jnp.concatenate(parts, axis=1)


def finish_kernel(n, split, sb, numbers_ref, *refs):
    pieces = refs[:n]
    in_ref, gain_ref, wkv_ref, stat_ref, wo_s, w_in_s, w_out_s = refs[n : n + 7]
    gain_ffn_hbm, qt_hbm, lctx_hbm, out_hbm = refs[n + 7 : n + 11]
    raw_s, rn_s, rk_s, rv_s, ctx_s, out_s, qt_s, lctx_s, gain_ffn_ref, sems, out_sems = refs[n + 11 :]
    steps, width, block = qt_s.shape
    remote = rn_s.shape[1]
    slots = remote // REMOTE_SENSORS
    count = [0]

    def fetch(src, dst):
        copy = pltpu.make_async_copy(src, dst, sems.at[count[0]])
        count[0] += 1
        copy.start()
        return copy

    score_in = [fetch(qt_hbm, qt_s)]
    merge_in = [fetch(lctx_hbm, lctx_s)]
    ffn_in = [fetch(gain_ffn_hbm, gain_ffn_ref)]

    order = swap16() if split else None
    lane_head = lax.broadcasted_iota(jnp.int32, (1, 128), 1) // HEAD
    heads = [(lane_head == h).astype(BF16) for h in range(128 // HEAD)]
    none = jnp.zeros((remote, 128), BF16)
    to_lanes = (
        lax.broadcasted_iota(jnp.int32, (2 * H, width), 1) // HEAD
        == lax.broadcasted_iota(jnp.int32, (2 * H, width), 0) % H
    ).astype(BF16)
    slot = lax.broadcasted_iota(jnp.int32, (remote, block), 0) // REMOTE_SENSORS
    live = jnp.zeros((remote, block), jnp.int32)
    for j in range(slots):
        live = jnp.where(slot == j, numbers_ref[1 + slots + j], live)
    live = live > 0

    if split:
        for j in range(slots):
            raw_s[j * REMOTE_SENSORS : (j + 1) * REMOTE_SENSORS] = in_ref[numbers_ref[1 + j]]
        for b in range(remote // 16):
            rows = raw_s[b * 16 : (b + 1) * 16].reshape(256, width)
            rn_s[:, b * 16 : (b + 1) * 16, :] = dot(order, rows).astype(BF16).reshape(16, 16, width)
        raw = rn_s[...]
    else:
        raw = in_ref[...]
    normed = rms(raw.reshape(steps * remote, width).astype(F32), gain_ref[...])
    kv = dot(normed, wkv_ref[...]).astype(BF16)
    rk_s[...] = kv[:, :width].reshape(steps, remote, width)
    rv_s[...] = kv[:, width:].reshape(steps, remote, width)

    def by_head(rows):
        spread = []
        for h in range(H):
            half = h * HEAD // 128
            part = rows[:, half * 128 : (half + 1) * 128] * heads[h % (128 // HEAD)]
            spread.append(jnp.concatenate([part, none] if half == 0 else [none, part], axis=1))
        return jnp.concatenate(spread, axis=0)

    for copy in score_in:
        copy.wait()
    def score(t):
        return dot(by_head(rk_s[t]), qt_s[t]).reshape(H, remote, block)

    def weigh(t, scores):
        masked = jnp.where(live[None], scores, NEG)
        ltop = stat_ref[t, :H]
        top = jnp.maximum(jnp.max(masked, axis=1), ltop)
        e = jnp.exp2((masked - top[:, None, :]) * SCALE)
        keep = jnp.exp2((ltop - top) * SCALE)
        inverse = 1.0 / (jnp.sum(e, axis=1) + stat_ref[t, H:] * keep)
        keep = keep * inverse
        high = keep.astype(BF16).astype(F32)
        factors = jnp.concatenate([high, keep - high], axis=0).astype(BF16).T
        return factors, (e * inverse[:, None, :]).astype(BF16).reshape(H * remote, block).T

    def merge(t, factors, weights):
        far = dot(weights, by_head(rv_s[t]))
        ctx_s[t] = (lctx_s[t].astype(F32) * dot(factors, to_lanes) + far).astype(BF16)

    for copy in merge_in:
        copy.wait()
    upcoming, waiting = score(0), None
    for t in range(steps):
        scores, upcoming = upcoming, score(t + 1) if t + 1 < steps else None
        weighed = (t, *weigh(t, scores))
        if waiting:
            merge(*waiting)
        waiting = weighed
    merge(*waiting)

    for copy in ffn_in:
        copy.wait()
    tile = width
    tiles = w_in_s.shape[1] // tile
    work = [(first, n) for first in range(0, block, sb) for n in range(tiles)]
    ready, total, copies = {}, {}, []

    def open_rows(first):
        x = rows_of(pieces, first, sb).reshape(steps * sb, width)
        context = ctx_s[:, first : first + sb, :].reshape(steps * sb, width)
        after = x.astype(F32) + dot(context, wo_s[...])
        total[first] = after
        ready[first] = rms(after, gain_ffn_ref[...])

    def up(first, n):
        return dot(ready[first], w_in_s[:, n * tile : (n + 1) * tile])

    open_rows(0)
    upper = up(*work[0])
    for k, (first, n) in enumerate(work):
        if n == 0 and first + sb < block:
            open_rows(first + sb)
        later = up(*work[k + 1]) if k + 1 < len(work) else None
        total[first] = total[first] + dot(gelu(upper).astype(BF16), w_out_s[n * tile : (n + 1) * tile, :])
        upper = later
        if n < tiles - 1:
            continue
        y = total[first].astype(BF16).reshape(steps, sb, width)
        if not split:
            out_s[:, first : first + sb, :] = y
            continue
        for b in range(sb // 16):
            turned = dot(order, y[:, b * 16 : (b + 1) * 16].reshape(256, width)).astype(BF16)
            out_s[first + b * 16 : first + (b + 1) * 16] = turned.reshape(16, steps, width)
        half = block // 2
        owner = numbers_ref[0] if first < half else 1 - numbers_ref[0]
        place = out_hbm.at[pl.ds(owner * half + first % half, sb)]
        copies.append(pltpu.make_async_copy(out_s.at[pl.ds(first, sb)], place, out_sems.at[first // sb]))
        copies[-1].start()
    if not split:
        copies.append(pltpu.make_async_copy(out_s, out_hbm, out_sems.at[0]))
        copies[-1].start()
    for copy in copies:
        copy.wait()


def finish(numbers, pieces, incoming, local, gain, wkv, wo, gain_ffn, w_in, w_out, split):
    qt, lctx, stat = local
    steps, width, block = qt.shape
    remote = (numbers.shape[0] - 1) // 2 * REMOTE_SENSORS
    sb = 32
    hbm = pl.BlockSpec(memory_space=pl.ANY)
    near = [*pieces, incoming, gain, wkv, stat, wo, w_in, w_out]
    pin = lambda arrays: [pltpu.with_memory_space_constraint(a, pltpu.HBM) for a in arrays]
    vmem = pl.BlockSpec(memory_space=pltpu.VMEM)
    buffer = lambda *shape: pltpu.VMEM(shape, BF16)
    return pl.pallas_call(
        functools.partial(finish_kernel, len(pieces), split, sb),
        out_shape=jax.ShapeDtypeStruct((block, steps, width) if split else (steps, block, width), BF16),
        in_specs=[pl.BlockSpec(memory_space=pltpu.SMEM)] + [vmem] * len(near) + [hbm] * 3,
        out_specs=hbm,
        scratch_shapes=[
            buffer(remote, steps, width),
            buffer(steps, remote, width),
            buffer(steps, remote, width),
            buffer(steps, remote, width),
            buffer(steps, block, width),
            buffer(block, steps, width) if split else buffer(steps, block, width),
            buffer(steps, width, block),
            buffer(steps, block, width),
            pltpu.VMEM(gain_ffn.shape, F32),
            pltpu.SemaphoreType.DMA((3,)),
            pltpu.SemaphoreType.DMA((block // sb,)),
        ],
        compiler_params=pltpu.CompilerParams(vmem_limit_bytes=VMEM_LIMIT),
        cost_estimate=pl.CostEstimate(
            flops=steps * block * width * width * 18, bytes_accessed=steps * block * width * 12, transcendentals=0
        ),
        name="remote_keys_and_feed_forward",
    )(numbers, *near, *pin([gain_ffn, qt, lctx]))


def local(
    tm,
    tokens,
    gain_time,
    wq_time,
    wkv_time,
    wo_time,
    gain_graph,
    wq_graph,
    wkv_graph,
    wo_graph,
    gain_ffn,
    w_in,
    w_out,
    neighbour_blocks,
    slot_used_mask,
    neighbour_rows,
):
    sensors_here, steps, width = tokens.shape
    block = sensors_here * tm
    group = steps // tm
    block_count, slots = neighbour_blocks.shape
    split = tm == 2 and group == 16 and sensors_here % 32 == 0
    gain_time, gain_graph, gain_ffn = (g.reshape(1, width) for g in (gain_time, gain_graph, gain_ffn))
    mine = lax.axis_index("tm").astype(jnp.int32)
    block_index = lax.axis_index("sensor")
    time = lambda x, *where: time_block(x, mine.reshape(1), gain_time, wq_time, wkv_time, wo_time, *where)
    if split:
        kept, got = [], []
        first = 0
        for share in SHARES:
            size = sensors_here * share // sum(SHARES)
            keep, send = time(tokens, first, size, True)
            tokens, send = lax.optimization_barrier((tokens, send))
            kept.append(keep)
            got.append(lax.ppermute(send, "tm", [(0, 1), (1, 0)]))
            first += size
        pieces = kept + got
    else:
        whole = lax.all_to_all(time(tokens, 0, sensors_here, False), "tm", split_axis=1, concat_axis=0, tiled=True)
        pieces = [whole.transpose(1, 0, 2)]
    matches = (neighbour_blocks == block_index).astype(jnp.int32)
    wanted = jnp.sum(matches[:, :, None] * neighbour_rows, axis=1).reshape(-1)
    own = lax.dynamic_index_in_dim(neighbour_blocks, block_index, 0, keepdims=False)
    numbers = jnp.concatenate([mine.reshape(1), own, slot_used_mask[0]])
    if split:
        place = (jnp.arange(block) + mine * sensors_here) % block
        pick = (wanted[:, None] == place[None, :]).astype(BF16)
        outgoing = pick_rows(pick, pieces)
    else:
        outgoing = jnp.take(whole, wanted, axis=0)
    outgoing = outgoing.reshape(block_count, REMOTE_SENSORS, group, width)
    incoming = lax.all_to_all(outgoing, "sensor", split_axis=0, concat_axis=0, tiled=True)
    if not split:
        incoming = jnp.take(incoming, own, axis=0).reshape(-1, group, width).transpose(1, 0, 2)
    near = local_part(pieces, gain_graph, wq_graph, wkv_graph)
    out = finish(numbers, pieces, incoming, near, gain_graph, wkv_graph, wo_graph, gain_ffn, w_in, w_out, split)
    return out if split else out.transpose(1, 0, 2)


def solution(mesh):
    in_specs = (
        P(("sensor", "tm"), None, None),
        P(),
        P(),
        P(),
        P(),
        P(),
        P(),
        P(),
        P(),
        P(),
        P(),
        P(),
        P(),
        P("sensor", None),
        P(),
    )
    out_specs = P("sensor", "tm", None)
    body = functools.partial(local, mesh.shape["tm"])
    return jax.shard_map(body, mesh=mesh, in_specs=in_specs, out_specs=out_specs, check_vma=False)
```

```python
import functools
import math

import jax
import jax.numpy as jnp
from jax import lax
from jax.experimental import pallas as pl
from jax.experimental.pallas import tpu as pltpu
from jax.sharding import PartitionSpec as P

H = 8
HEAD = 32
REMOTE_SENSORS = 4
EPSILON = 1e-06
NEG = -1e30
SCALE = math.log2(math.e) / math.sqrt(HEAD)
SHARES = (1, 1, 1, 1)
F32 = jnp.float32
BF16 = jnp.bfloat16
VMEM_LIMIT = 28 * 1024 * 1024


def dot(a, b):
    return jnp.dot(a, b, preferred_element_type=F32)


def dot_nt(a, b):
    return lax.dot_general(a, b, (((1,), (1,)), ((), ())), preferred_element_type=F32)


def dot_tn(a, b):
    return lax.dot_general(a, b, (((0,), (0,)), ((), ())), preferred_element_type=F32)


def rms(x, gain):
    inverse = lax.rsqrt(jnp.mean(x * x, axis=-1, keepdims=True) + EPSILON)
    return (x * inverse * gain).astype(BF16)


def swap16():
    row = lax.broadcasted_iota(jnp.int32, (256, 256), 0)
    col = lax.broadcasted_iota(jnp.int32, (256, 256), 1)
    return (col == ((row & 15) << 4) + (row >> 4)).astype(BF16)


def head_rows(rows, lanes, head_of_row, first_head):
    row = lax.broadcasted_iota(jnp.int32, (rows, lanes), 0)
    lane = lax.broadcasted_iota(jnp.int32, (rows, lanes), 1)
    return (lane // HEAD + first_head == row // head_of_row).astype(BF16)


def time_kernel(split, my_ref, x_ref, gain_ref, wq_ref, wkv_ref, wo_ref, *refs):
    if split:
        keep_ref, send_ref, q_s, k_s, v_s, a_s, c_s, after_s = refs
    else:
        out_ref, q_s, k_s, v_s, a_s, c_s = refs
    sensors, steps, width = x_ref.shape
    rows = sensors * steps
    x = x_ref[...].reshape(rows, width).astype(F32)
    normed = rms(x, gain_ref[...])
    q_s[...] = dot(normed, wq_ref[...]).astype(BF16)
    kv = dot(normed, wkv_ref[...]).astype(BF16)
    k_s[...] = kv[:, :width]
    v_s[...] = kv[:, width:]
    lanes = H * steps
    near = 128 // HEAD
    span = near * steps
    mask = head_rows(span, 128, steps, 0)
    none = jnp.zeros((span, 128), BF16)
    key_t = lax.broadcasted_iota(jnp.int32, (steps, lanes), 0)
    query_t = lax.broadcasted_iota(jnp.int32, (steps, lanes), 1) & (steps - 1)
    causal = key_t <= query_t
    for s in range(sensors):
        here = slice(s * steps, (s + 1) * steps)
        first, second = (jnp.concatenate([q_s[here, c : c + 128]] * near, axis=0) * mask for c in (0, 128))
        spread = jnp.concatenate(
            [jnp.concatenate([first, none], axis=1), jnp.concatenate([none, second], axis=1)], axis=0
        )
        scores = jnp.where(causal, dot_nt(k_s[here, :], spread), NEG)
        top = jnp.max(scores, axis=0, keepdims=True)
        e = jnp.exp2((scores - top) * SCALE)
        a_s[here, :] = (e * (1.0 / jnp.sum(e, axis=0, keepdims=True))).astype(BF16)
    lane_head = lax.broadcasted_iota(jnp.int32, (steps, 128), 1) // HEAD
    for g in range(rows // 128):
        turned = a_s[g * 128 : (g + 1) * 128, :].T
        for half in range(2):
            cols = slice(half * 128, (half + 1) * 128)
            for s in range(0, 128 // steps, 2):
                columns = []
                for r in (s, s + 1):
                    v = v_s[g * 128 + r * steps : g * 128 + (r + 1) * steps, cols]
                    parts = [jnp.zeros((r * steps, 128), BF16), v, jnp.zeros((128 - (r + 1) * steps, 128), BF16)]
                    columns.append(jnp.concatenate([p for p in parts if p.shape[0]], axis=0))
                wide = dot(turned[half * span : (half + 1) * span], jnp.concatenate(columns, axis=1))
                for i in range(2):
                    ctx = wide[:steps, i * 128 : (i + 1) * 128]
                    for h in range(1, near):
                        ctx = jnp.where(lane_head == h, wide[h * steps : (h + 1) * steps, i * 128 : (i + 1) * 128], ctx)
                    at = g * 128 + (s + i) * steps
                    c_s[at : at + steps, cols] = ctx.astype(BF16)
    after = (x + dot(c_s[...], wo_ref[...])).astype(BF16)
    if not split:
        out_ref[...] = after.reshape(sensors, steps, width)
        return
    after_s[...] = after.reshape(sensors, steps, width)
    order = swap16()
    mine = my_ref[0]
    for ref, part in ((keep_ref, mine), (send_ref, 1 - mine)):
        rows16 = after_s[:, pl.ds(pl.multiple_of(part * 16, 16), 16), :]
        for b in range(sensors // 16):
            block = rows16[b * 16 : (b + 1) * 16].reshape(256, width)
            ref[:, b * 16 : (b + 1) * 16, :] = dot(order, block).astype(BF16).reshape(16, 16, width)


def time_block(tokens, my, gain, wq, wkv, wo, first, count, split):
    steps, width = tokens.shape[1:]
    if first == 0:
        tokens, gain, wq, wkv, wo = (pltpu.with_memory_space_constraint(a, pltpu.HBM) for a in (tokens, gain, wq, wkv, wo))
    sb = min(16, count)
    rows = sb * steps
    full = lambda a: pl.BlockSpec(a.shape, lambda i, *_: (0,) * a.ndim)
    if split:
        out_shape = [jax.ShapeDtypeStruct((16, count, width), BF16)] * 2
        out_specs = [pl.BlockSpec((16, sb, width), lambda i, *_: (0, i, 0))] * 2
        extra = [pltpu.VMEM((sb, steps, width), BF16)]
    else:
        out_shape = jax.ShapeDtypeStruct((count, steps, width), BF16)
        out_specs = pl.BlockSpec((sb, steps, width), lambda i, *_: (i, 0, 0))
        extra = []
    return pl.pallas_call(
        functools.partial(time_kernel, split),
        out_shape=out_shape,
        grid_spec=pltpu.PrefetchScalarGridSpec(
            num_scalar_prefetch=1,
            grid=(count // sb,),
            in_specs=[
                pl.BlockSpec((sb, steps, width), lambda i, *_: (first // sb + i, 0, 0)),
                full(gain),
                full(wq),
                full(wkv),
                full(wo),
            ],
            out_specs=out_specs,
            scratch_shapes=[pltpu.VMEM((rows, width), BF16)] * 5 + extra,
        ),
        compiler_params=pltpu.CompilerParams(vmem_limit_bytes=VMEM_LIMIT),
        cost_estimate=pl.CostEstimate(
            flops=count * steps * width * width * 12, bytes_accessed=count * steps * width * 4, transcendentals=0
        ),
        name="time_block",
    )(my, tokens, gain, wq, wkv, wo)


def pick_kernel(n, pick_ref, *refs):
    pieces, (out_hbm, o_s, out_s, sems) = refs[:n], refs[n:]
    steps, wanted, width = o_s.shape
    order = swap16()
    pick = pick_ref[...]
    for t in range(steps):
        rows = jnp.concatenate([p[t] for p in pieces], axis=0)
        o_s[t] = dot(pick, rows).astype(BF16)
    copies = []
    for b in range(wanted // 16):
        here = pl.ds(b * 16, 16)
        block = o_s[:, b * 16 : (b + 1) * 16, :].reshape(256, width)
        out_s[b * 16 : (b + 1) * 16] = dot(order, block).astype(BF16).reshape(16, 16, width)
        copies.append(pltpu.make_async_copy(out_s.at[here], out_hbm.at[here], sems.at[b]))
        copies[-1].start()
    for copy in copies:
        copy.wait()


def pick_rows(pick, pieces):
    steps, _, width = pieces[0].shape
    wanted = pick.shape[0]
    vmem = pl.BlockSpec(memory_space=pltpu.VMEM)
    return pl.pallas_call(
        functools.partial(pick_kernel, len(pieces)),
        out_shape=pltpu.HBM((wanted, steps, width), BF16),
        in_specs=[vmem] * (1 + len(pieces)),
        out_specs=pl.BlockSpec(memory_space=pl.ANY),
        scratch_shapes=[
            pltpu.VMEM((steps, wanted, width), BF16),
            pltpu.VMEM((wanted, steps, width), BF16),
            pltpu.SemaphoreType.DMA((wanted // 16,)),
        ],
        compiler_params=pltpu.CompilerParams(vmem_limit_bytes=VMEM_LIMIT),
        name="pick_rows",
    )(pick, *pieces)


def pair_scores(q, k, masks, pair):
    cols = slice(pair // 2 * 128, pair // 2 * 128 + 128)
    spread = jnp.concatenate([q[:, cols]] * 2, axis=0) * masks[pair % 2]
    return dot_nt(k[:, cols], spread)


def local_kernel(n, *refs):
    pieces = refs[:n]
    gain_ref, wq_ref, wkv_ref, qt_ref, ctx_ref, stat_ref, wqt_s, wvt_s = refs[n:]
    tb, width, block = qt_ref.shape

    @pl.when(pl.program_id(0) == 0)
    def _():
        wvt_s[...] = wkv_ref[:, width:].T
        wqt_s[...] = wq_ref[...].T

    x = jnp.concatenate([p[t] for t in range(tb) for p in pieces], axis=0).astype(F32)
    normed = rms(x, gain_ref[...])
    q = dot(normed, wq_ref[...]).astype(BF16)
    k = dot(normed, wkv_ref[:, :width]).astype(BF16)
    masks = [head_rows(2 * block, 128, block, -2 * p) for p in range(2)]
    for t in range(tb):
        here = slice(t * block, (t + 1) * block)
        qt_ref[t] = dot_nt(wqt_s[...], normed[here]).astype(BF16)
        vt = dot_nt(wvt_s[...], normed[here]).astype(BF16)
        scores = [pair_scores(q[here], k[here], masks, pair) for pair in range(H // 2)]
        tops = [jnp.max(x, axis=0, keepdims=True) for x in scores]
        es = [jnp.exp2((x - top) * SCALE) for x, top in zip(scores, tops)]
        context = []
        for pair, e in enumerate(es):
            lo = pair * 2 * HEAD
            both = dot(vt[lo : lo + 2 * HEAD], e.astype(BF16))
            total = jnp.sum(e, axis=0, keepdims=True)
            for i in range(2):
                lanes = slice(i * block, (i + 1) * block)
                head = 2 * pair + i
                context.append(both[i * HEAD : (i + 1) * HEAD, lanes].astype(BF16))
                stat_ref[t, head : head + 1, :] = tops[pair][:, lanes]
                stat_ref[t, H + head : H + head + 1, :] = total[:, lanes]
        ctx_ref[t] = jnp.concatenate(context, axis=0).T


def local_part(pieces, gain, wq, wkv):
    steps, _, width = pieces[0].shape
    block = sum(p.shape[1] for p in pieces)
    tb = 4
    full = lambda a: pl.BlockSpec(a.shape, lambda i: (0,) * a.ndim)
    per_t = lambda *shape: pl.BlockSpec((tb,) + shape, lambda i: (i, 0, 0))
    return pl.pallas_call(
        functools.partial(local_kernel, len(pieces)),
        out_shape=[
            pltpu.HBM((steps, width, block), BF16),
            pltpu.HBM((steps, block, width), BF16),
            jax.ShapeDtypeStruct((steps, 2 * H, block), F32),
        ],
        grid=(steps // tb,),
        in_specs=[per_t(p.shape[1], width) for p in pieces] + [full(gain), full(wq), full(wkv)],
        out_specs=[
            per_t(width, block),
            per_t(block, width),
            per_t(2 * H, block),
        ],
        scratch_shapes=[pltpu.VMEM((width, width), BF16)] * 2,
        compiler_params=pltpu.CompilerParams(vmem_limit_bytes=VMEM_LIMIT),
        cost_estimate=pl.CostEstimate(
            flops=steps * block * width * width * 12, bytes_accessed=steps * block * width * 10, transcendentals=0
        ),
        name="local_keys",
    )(*pieces, gain, wq, wkv)


def gelu_of_half(x):
    inner = x * (1.5957691216057308 + 0.28541926509040096 * (x * x))
    return x + x * jnp.tanh(inner)


def rows_of(pieces, first, count):
    parts, start = [], 0
    for p in pieces:
        low, high = max(first, start), min(first + count, start + p.shape[1])
        if low < high:
            parts.append(p[:, low - start : high - start, :])
        start += p.shape[1]
    return jnp.concatenate(parts, axis=1)


def finish_kernel(n, split, sb, numbers_ref, *refs):
    pieces = refs[:n]
    in_ref, gain_ref, wkv_ref, stat_ref, wo_s, w_in_s, w_out_s = refs[n : n + 7]
    gain_ffn_hbm, qt_hbm, lctx_hbm, out_hbm = refs[n + 7 : n + 11]
    raw_s, rn_s, rk_s, rv_s, ctx_s, out_s, qt_s, lctx_s, gain_ffn_ref, sems, out_sems = refs[n + 11 :]
    steps, width, block = qt_s.shape
    remote = rn_s.shape[1]
    slots = remote // REMOTE_SENSORS
    count = [0]

    def fetch(src, dst):
        copy = pltpu.make_async_copy(src, dst, sems.at[count[0]])
        count[0] += 1
        copy.start()
        return copy

    score_in = [fetch(qt_hbm, qt_s)]
    merge_in = [fetch(lctx_hbm, lctx_s)]
    ffn_in = [fetch(gain_ffn_hbm, gain_ffn_ref)]

    order = swap16() if split else None
    lane_head = lax.broadcasted_iota(jnp.int32, (1, 128), 1) // HEAD
    heads = [(lane_head == h).astype(BF16) for h in range(128 // HEAD)]
    none = jnp.zeros((remote, 128), BF16)
    to_lanes = (
        lax.broadcasted_iota(jnp.int32, (2 * H, width), 1) // HEAD
        == lax.broadcasted_iota(jnp.int32, (2 * H, width), 0) % H
    ).astype(BF16)
    slot = lax.broadcasted_iota(jnp.int32, (remote, block), 0) // REMOTE_SENSORS
    live = jnp.zeros((remote, block), jnp.int32)
    for j in range(slots):
        live = jnp.where(slot == j, numbers_ref[1 + slots + j], live)
    live = live > 0

    if split:
        for j in range(slots):
            raw_s[j * REMOTE_SENSORS : (j + 1) * REMOTE_SENSORS] = in_ref[numbers_ref[1 + j]]
        for b in range(remote // 16):
            rows = raw_s[b * 16 : (b + 1) * 16].reshape(256, width)
            rn_s[:, b * 16 : (b + 1) * 16, :] = dot(order, rows).astype(BF16).reshape(16, 16, width)
        raw = rn_s[...]
    else:
        raw = in_ref[...]
    normed = rms(raw.reshape(steps * remote, width).astype(F32), gain_ref[...])
    kv = dot(normed, wkv_ref[...]).astype(BF16)
    rk_s[...] = kv[:, :width].reshape(steps, remote, width)
    rv_s[...] = kv[:, width:].reshape(steps, remote, width)

    def by_head(rows):
        spread = []
        for h in range(H):
            half = h * HEAD // 128
            part = rows[:, half * 128 : (half + 1) * 128] * heads[h % (128 // HEAD)]
            spread.append(jnp.concatenate([part, none] if half == 0 else [none, part], axis=1))
        return jnp.concatenate(spread, axis=0)

    for copy in score_in:
        copy.wait()
    def score(t):
        return dot(by_head(rk_s[t]), qt_s[t]).reshape(H, remote, block)

    def weigh(t, scores):
        masked = jnp.where(live[None], scores, NEG)
        ltop = stat_ref[t, :H]
        top = jnp.maximum(jnp.max(masked, axis=1), ltop)
        e = jnp.exp2((masked - top[:, None, :]) * SCALE)
        keep = jnp.exp2((ltop - top) * SCALE)
        inverse = 1.0 / (jnp.sum(e, axis=1) + stat_ref[t, H:] * keep)
        keep = keep * inverse
        high = keep.astype(BF16).astype(F32)
        factors = jnp.concatenate([high, keep - high], axis=0).astype(BF16).T
        return factors, (e * inverse[:, None, :]).astype(BF16).reshape(H * remote, block).T

    def merge(t, factors, weights):
        if t == 0:
            for copy in merge_in:
                copy.wait()
        far = dot(weights, by_head(rv_s[t]))
        ctx_s[t] = (lctx_s[t].astype(F32) * dot(factors, to_lanes) + far).astype(BF16)

    upcoming, waiting = score(0), None
    for t in range(steps):
        scores, upcoming = upcoming, score(t + 1) if t + 1 < steps else None
        weighed = (t, *weigh(t, scores))
        if waiting:
            merge(*waiting)
        waiting = weighed
    merge(*waiting)

    for copy in ffn_in:
        copy.wait()
    tile = width
    tiles = w_in_s.shape[1] // tile
    work = [(first, n) for first in range(0, block, sb) for n in range(tiles)]
    ready, total, copies = {}, {}, []

    def open_rows(first):
        x = rows_of(pieces, first, sb).reshape(steps * sb, width)
        context = ctx_s[:, first : first + sb, :].reshape(steps * sb, width)
        after = x.astype(F32) + dot(context, wo_s[...])
        total[first] = after
        ready[first] = rms(after, 0.5 * gain_ffn_ref[...])

    def up(first, n):
        return dot(ready[first], w_in_s[:, n * tile : (n + 1) * tile])

    open_rows(0)
    upper = up(*work[0])
    for k, (first, n) in enumerate(work):
        if n == 0 and first + sb < block:
            open_rows(first + sb)
        later = up(*work[k + 1]) if k + 1 < len(work) else None
        total[first] = total[first] + dot(gelu_of_half(upper).astype(BF16), w_out_s[n * tile : (n + 1) * tile, :])
        upper = later
        if n < tiles - 1:
            continue
        y = total[first].astype(BF16).reshape(steps, sb, width)
        if not split:
            out_s[:, first : first + sb, :] = y
            continue
        for b in range(sb // 16):
            turned = dot(order, y[:, b * 16 : (b + 1) * 16].reshape(256, width)).astype(BF16)
            out_s[first + b * 16 : first + (b + 1) * 16] = turned.reshape(16, steps, width)
        half = block // 2
        owner = numbers_ref[0] if first < half else 1 - numbers_ref[0]
        place = out_hbm.at[pl.ds(owner * half + first % half, sb)]
        copies.append(pltpu.make_async_copy(out_s.at[pl.ds(first, sb)], place, out_sems.at[first // sb]))
        copies[-1].start()
    if not split:
        copies.append(pltpu.make_async_copy(out_s, out_hbm, out_sems.at[0]))
        copies[-1].start()
    for copy in copies:
        copy.wait()


def finish(numbers, pieces, incoming, local, gain, wkv, wo, gain_ffn, w_in, w_out, split):
    qt, lctx, stat = local
    steps, width, block = qt.shape
    remote = (numbers.shape[0] - 1) // 2 * REMOTE_SENSORS
    sb = 32
    hbm = pl.BlockSpec(memory_space=pl.ANY)
    near = [*pieces, incoming, gain, wkv, stat, wo, w_in, w_out]
    pin = lambda arrays: [pltpu.with_memory_space_constraint(a, pltpu.HBM) for a in arrays]
    vmem = pl.BlockSpec(memory_space=pltpu.VMEM)
    buffer = lambda *shape: pltpu.VMEM(shape, BF16)
    return pl.pallas_call(
        functools.partial(finish_kernel, len(pieces), split, sb),
        out_shape=jax.ShapeDtypeStruct((block, steps, width) if split else (steps, block, width), BF16),
        in_specs=[pl.BlockSpec(memory_space=pltpu.SMEM)] + [vmem] * len(near) + [hbm] * 3,
        out_specs=hbm,
        scratch_shapes=[
            buffer(remote, steps, width),
            buffer(steps, remote, width),
            buffer(steps, remote, width),
            buffer(steps, remote, width),
            buffer(steps, block, width),
            buffer(block, steps, width) if split else buffer(steps, block, width),
            buffer(steps, width, block),
            buffer(steps, block, width),
            pltpu.VMEM(gain_ffn.shape, F32),
            pltpu.SemaphoreType.DMA((3,)),
            pltpu.SemaphoreType.DMA((block // sb,)),
        ],
        compiler_params=pltpu.CompilerParams(vmem_limit_bytes=VMEM_LIMIT),
        cost_estimate=pl.CostEstimate(
            flops=steps * block * width * width * 18, bytes_accessed=steps * block * width * 12, transcendentals=0
        ),
        name="remote_keys_and_feed_forward",
    )(numbers, *near, *pin([gain_ffn, qt, lctx]))


def local(
    tm,
    tokens,
    gain_time,
    wq_time,
    wkv_time,
    wo_time,
    gain_graph,
    wq_graph,
    wkv_graph,
    wo_graph,
    gain_ffn,
    w_in,
    w_out,
    neighbour_blocks,
    slot_used_mask,
    neighbour_rows,
):
    sensors_here, steps, width = tokens.shape
    block = sensors_here * tm
    group = steps // tm
    block_count, slots = neighbour_blocks.shape
    split = tm == 2 and group == 16 and sensors_here % 32 == 0
    gain_time, gain_graph, gain_ffn = (g.reshape(1, width) for g in (gain_time, gain_graph, gain_ffn))
    mine = lax.axis_index("tm").astype(jnp.int32)
    block_index = lax.axis_index("sensor")
    time = lambda x, *where: time_block(x, mine.reshape(1), gain_time, wq_time, wkv_time, wo_time, *where)
    if split:
        kept, got = [], []
        first = 0
        for share in SHARES:
            size = sensors_here * share // sum(SHARES)
            keep, send = time(tokens, first, size, True)
            tokens, send = lax.optimization_barrier((tokens, send))
            kept.append(keep)
            got.append(lax.ppermute(send, "tm", [(0, 1), (1, 0)]))
            first += size
        pieces = kept + got
    else:
        whole = lax.all_to_all(time(tokens, 0, sensors_here, False), "tm", split_axis=1, concat_axis=0, tiled=True)
        pieces = [whole.transpose(1, 0, 2)]
    matches = (neighbour_blocks == block_index).astype(jnp.int32)
    wanted = jnp.sum(matches[:, :, None] * neighbour_rows, axis=1).reshape(-1)
    own = lax.dynamic_index_in_dim(neighbour_blocks, block_index, 0, keepdims=False)
    numbers = jnp.concatenate([mine.reshape(1), own, slot_used_mask[0]])
    if split:
        place = (jnp.arange(block) + mine * sensors_here) % block
        pick = (wanted[:, None] == place[None, :]).astype(BF16)
        outgoing = pick_rows(pick, pieces)
    else:
        outgoing = jnp.take(whole, wanted, axis=0)
    outgoing = outgoing.reshape(block_count, REMOTE_SENSORS, group, width)
    incoming = lax.all_to_all(outgoing, "sensor", split_axis=0, concat_axis=0, tiled=True)
    if not split:
        incoming = jnp.take(incoming, own, axis=0).reshape(-1, group, width).transpose(1, 0, 2)
    near = local_part(pieces, gain_graph, wq_graph, wkv_graph)
    out = finish(numbers, pieces, incoming, near, gain_graph, wkv_graph, wo_graph, gain_ffn, w_in, w_out, split)
    return out if split else out.transpose(1, 0, 2)


def solution(mesh):
    in_specs = (
        P(("sensor", "tm"), None, None),
        P(),
        P(),
        P(),
        P(),
        P(),
        P(),
        P(),
        P(),
        P(),
        P(),
        P(),
        P(),
        P("sensor", None),
        P(),
    )
    out_specs = P("sensor", "tm", None)
    body = functools.partial(local, mesh.shape["tm"])
    return jax.shard_map(body, mesh=mesh, in_specs=in_specs, out_specs=out_specs, check_vma=False)
```

```python
import functools
import math

import jax
import jax.numpy as jnp
from jax import lax
from jax.experimental import pallas as pl
from jax.experimental.pallas import tpu as pltpu
from jax.sharding import PartitionSpec as P

H = 8
HEAD = 32
REMOTE_SENSORS = 4
EPSILON = 1e-06
NEG = -1e30
SCALE = math.log2(math.e) / math.sqrt(HEAD)
SHARES = (1, 1, 1, 1)
F32 = jnp.float32
BF16 = jnp.bfloat16
VMEM_LIMIT = 28 * 1024 * 1024


def dot(a, b):
    return jnp.dot(a, b, preferred_element_type=F32)


def dot_nt(a, b):
    return lax.dot_general(a, b, (((1,), (1,)), ((), ())), preferred_element_type=F32)


def dot_tn(a, b):
    return lax.dot_general(a, b, (((0,), (0,)), ((), ())), preferred_element_type=F32)


def rms(x, gain):
    inverse = lax.rsqrt(jnp.mean(x * x, axis=-1, keepdims=True) + EPSILON)
    return (x * inverse * gain).astype(BF16)


def swap16():
    row = lax.broadcasted_iota(jnp.int32, (256, 256), 0)
    col = lax.broadcasted_iota(jnp.int32, (256, 256), 1)
    return (col == ((row & 15) << 4) + (row >> 4)).astype(BF16)


def head_rows(rows, lanes, head_of_row, first_head):
    row = lax.broadcasted_iota(jnp.int32, (rows, lanes), 0)
    lane = lax.broadcasted_iota(jnp.int32, (rows, lanes), 1)
    return (lane // HEAD + first_head == row // head_of_row).astype(BF16)


def time_kernel(split, my_ref, x_ref, gain_ref, wq_ref, wkv_ref, wo_ref, *refs):
    if split:
        keep_ref, send_ref, q_s, k_s, v_s, a_s, c_s, after_s = refs
    else:
        out_ref, q_s, k_s, v_s, a_s, c_s = refs
    sensors, steps, width = x_ref.shape
    rows = sensors * steps
    x = x_ref[...].reshape(rows, width).astype(F32)
    normed = rms(x, gain_ref[...])
    q_s[...] = dot(normed, wq_ref[...]).astype(BF16)
    kv = dot(normed, wkv_ref[...]).astype(BF16)
    k_s[...] = kv[:, :width]
    v_s[...] = kv[:, width:]
    lanes = H * steps
    near = 128 // HEAD
    span = near * steps
    mask = head_rows(span, 128, steps, 0)
    none = jnp.zeros((span, 128), BF16)
    key_t = lax.broadcasted_iota(jnp.int32, (steps, lanes), 0)
    query_t = lax.broadcasted_iota(jnp.int32, (steps, lanes), 1) & (steps - 1)
    causal = key_t <= query_t
    for s in range(sensors):
        here = slice(s * steps, (s + 1) * steps)
        first, second = (jnp.concatenate([q_s[here, c : c + 128]] * near, axis=0) * mask for c in (0, 128))
        spread = jnp.concatenate(
            [jnp.concatenate([first, none], axis=1), jnp.concatenate([none, second], axis=1)], axis=0
        )
        scores = jnp.where(causal, dot_nt(k_s[here, :], spread), NEG)
        top = jnp.max(scores, axis=0, keepdims=True)
        e = jnp.exp2((scores - top) * SCALE)
        a_s[here, :] = (e * (1.0 / jnp.sum(e, axis=0, keepdims=True))).astype(BF16)
    lane_head = lax.broadcasted_iota(jnp.int32, (steps, 128), 1) // HEAD
    for g in range(rows // 128):
        turned = a_s[g * 128 : (g + 1) * 128, :].T
        for half in range(2):
            cols = slice(half * 128, (half + 1) * 128)
            for s in range(0, 128 // steps, 2):
                columns = []
                for r in (s, s + 1):
                    v = v_s[g * 128 + r * steps : g * 128 + (r + 1) * steps, cols]
                    parts = [jnp.zeros((r * steps, 128), BF16), v, jnp.zeros((128 - (r + 1) * steps, 128), BF16)]
                    columns.append(jnp.concatenate([p for p in parts if p.shape[0]], axis=0))
                wide = dot(turned[half * span : (half + 1) * span], jnp.concatenate(columns, axis=1))
                for i in range(2):
                    ctx = wide[:steps, i * 128 : (i + 1) * 128]
                    for h in range(1, near):
                        ctx = jnp.where(lane_head == h, wide[h * steps : (h + 1) * steps, i * 128 : (i + 1) * 128], ctx)
                    at = g * 128 + (s + i) * steps
                    c_s[at : at + steps, cols] = ctx.astype(BF16)
    after = (x + dot(c_s[...], wo_ref[...])).astype(BF16)
    if not split:
        out_ref[...] = after.reshape(sensors, steps, width)
        return
    after_s[...] = after.reshape(sensors, steps, width)
    mine = my_ref[0]
    for ref, part in ((keep_ref, mine), (send_ref, 1 - mine)):
        ref[...] = after_s[:, pl.ds(pl.multiple_of(part * 16, 16), 16), :]


def time_block(tokens, my, gain, wq, wkv, wo, first, count, split):
    steps, width = tokens.shape[1:]
    if first == 0:
        tokens, gain, wq, wkv, wo = (pltpu.with_memory_space_constraint(a, pltpu.HBM) for a in (tokens, gain, wq, wkv, wo))
    sb = min(16, count)
    rows = sb * steps
    full = lambda a: pl.BlockSpec(a.shape, lambda i, *_: (0,) * a.ndim)
    if split:
        out_shape = [jax.ShapeDtypeStruct((count, 16, width), BF16)] * 2
        out_specs = [pl.BlockSpec((sb, 16, width), lambda i, *_: (i, 0, 0))] * 2
        extra = [pltpu.VMEM((sb, steps, width), BF16)]
    else:
        out_shape = jax.ShapeDtypeStruct((count, steps, width), BF16)
        out_specs = pl.BlockSpec((sb, steps, width), lambda i, *_: (i, 0, 0))
        extra = []
    return pl.pallas_call(
        functools.partial(time_kernel, split),
        out_shape=out_shape,
        grid_spec=pltpu.PrefetchScalarGridSpec(
            num_scalar_prefetch=1,
            grid=(count // sb,),
            in_specs=[
                pl.BlockSpec((sb, steps, width), lambda i, *_: (first // sb + i, 0, 0)),
                full(gain),
                full(wq),
                full(wkv),
                full(wo),
            ],
            out_specs=out_specs,
            scratch_shapes=[pltpu.VMEM((rows, width), BF16)] * 5 + extra,
        ),
        compiler_params=pltpu.CompilerParams(vmem_limit_bytes=VMEM_LIMIT),
        cost_estimate=pl.CostEstimate(
            flops=count * steps * width * width * 12, bytes_accessed=count * steps * width * 4, transcendentals=0
        ),
        name="time_block",
    )(my, tokens, gain, wq, wkv, wo)


def pick_kernel(n, wanted_ref, *refs):
    pieces, (out_hbm, x_s, out_s, sems) = refs[:n], refs[n:]
    place = 0
    for p in pieces:
        x_s[place : place + p.shape[0]] = p[...]
        place += p.shape[0]
    copies = []
    for b in range(out_s.shape[0] // 16):
        for j in range(b * 16, (b + 1) * 16):
            out_s[j] = x_s[wanted_ref[j]]
        here = pl.ds(b * 16, 16)
        copies.append(pltpu.make_async_copy(out_s.at[here], out_hbm.at[here], sems.at[b]))
        copies[-1].start()
    for copy in copies:
        copy.wait()


def pick_rows(wanted, pieces):
    _, steps, width = pieces[0].shape
    count = wanted.shape[0]
    block = sum(p.shape[0] for p in pieces)
    return pl.pallas_call(
        functools.partial(pick_kernel, len(pieces)),
        out_shape=pltpu.HBM((count, steps, width), BF16),
        in_specs=[pl.BlockSpec(memory_space=pltpu.SMEM)] + [pl.BlockSpec(memory_space=pltpu.VMEM)] * len(pieces),
        out_specs=pl.BlockSpec(memory_space=pl.ANY),
        scratch_shapes=[
            pltpu.VMEM((block, steps, width), BF16),
            pltpu.VMEM((count, steps, width), BF16),
            pltpu.SemaphoreType.DMA((count // 16,)),
        ],
        compiler_params=pltpu.CompilerParams(vmem_limit_bytes=VMEM_LIMIT),
        name="pick_rows",
    )(wanted, *pieces)


def pair_scores(q, k, masks, pair):
    cols = slice(pair // 2 * 128, pair // 2 * 128 + 128)
    spread = jnp.concatenate([q[:, cols]] * 2, axis=0) * masks[pair % 2]
    return dot_nt(k[:, cols], spread)


def local_kernel(n, split, *refs):
    pieces = refs[:n]
    gain_ref, wq_ref, wkv_ref, x_ref, qt_ref, ctx_ref, stat_ref, wqt_s, wvt_s = refs[n:]
    tb, width, block = qt_ref.shape

    @pl.when(pl.program_id(0) == 0)
    def _():
        wvt_s[...] = wkv_ref[:, width:].T
        place = 0
        if not split:
            x_ref[...] = pieces[0][...]
        for p in pieces if split else []:
            for b in range(0, p.shape[0], 16):
                turned = dot(swap16(), p[b : b + 16].reshape(256, width)).astype(BF16)
                x_ref[:, place + b : place + b + 16, :] = turned.reshape(16, 16, width)
            place += p.shape[0]
        wqt_s[...] = wq_ref[...].T

    x = x_ref[pl.ds(pl.program_id(0) * tb, tb)].reshape(tb * block, width).astype(F32)
    normed = rms(x, gain_ref[...])
    q = dot(normed, wq_ref[...]).astype(BF16)
    k = dot(normed, wkv_ref[:, :width]).astype(BF16)
    masks = [head_rows(2 * block, 128, block, -2 * p) for p in range(2)]
    for t in range(tb):
        here = slice(t * block, (t + 1) * block)
        qt_ref[t] = dot_nt(wqt_s[...], normed[here]).astype(BF16)
        vt = dot_nt(wvt_s[...], normed[here]).astype(BF16)
        scores = [pair_scores(q[here], k[here], masks, pair) for pair in range(H // 2)]
        tops = [jnp.max(x, axis=0, keepdims=True) for x in scores]
        es = [jnp.exp2((x - top) * SCALE) for x, top in zip(scores, tops)]
        context = []
        for pair, e in enumerate(es):
            lo = pair * 2 * HEAD
            both = dot(vt[lo : lo + 2 * HEAD], e.astype(BF16))
            total = jnp.sum(e, axis=0, keepdims=True)
            for i in range(2):
                lanes = slice(i * block, (i + 1) * block)
                head = 2 * pair + i
                context.append(both[i * HEAD : (i + 1) * HEAD, lanes].astype(BF16))
                stat_ref[t, head : head + 1, :] = tops[pair][:, lanes]
                stat_ref[t, H + head : H + head + 1, :] = total[:, lanes]
        ctx_ref[t] = jnp.concatenate(context, axis=0).T


def local_part(pieces, gain, wq, wkv, split):
    sensors, steps = (0, 1) if split else (1, 0)
    steps, width = pieces[0].shape[steps], pieces[0].shape[2]
    block = sum(p.shape[sensors] for p in pieces)
    tb = 4
    full = lambda a: pl.BlockSpec(a.shape, lambda i: (0,) * a.ndim)
    per_t = lambda *shape: pl.BlockSpec((tb,) + shape, lambda i: (i, 0, 0))
    return pl.pallas_call(
        functools.partial(local_kernel, len(pieces), split),
        out_shape=[
            pltpu.HBM((steps, block, width), BF16),
            pltpu.HBM((steps, width, block), BF16),
            pltpu.HBM((steps, block, width), BF16),
            jax.ShapeDtypeStruct((steps, 2 * H, block), F32),
        ],
        grid=(steps // tb,),
        in_specs=[full(p) for p in pieces] + [full(gain), full(wq), full(wkv)],
        out_specs=[
            pl.BlockSpec((steps, block, width), lambda i: (0, 0, 0)),
            per_t(width, block),
            per_t(block, width),
            per_t(2 * H, block),
        ],
        scratch_shapes=[pltpu.VMEM((width, width), BF16)] * 2,
        compiler_params=pltpu.CompilerParams(vmem_limit_bytes=VMEM_LIMIT),
        cost_estimate=pl.CostEstimate(
            flops=steps * block * width * width * 12, bytes_accessed=steps * block * width * 10, transcendentals=0
        ),
        name="local_keys",
    )(*pieces, gain, wq, wkv)


def gelu_of_half(x):
    inner = x * (1.5957691216057308 + 0.28541926509040096 * (x * x))
    return x + x * jnp.tanh(inner)


def finish_kernel(split, sb, numbers_ref, *refs):
    in_ref, gain_ref, wkv_ref, stat_ref, wo_s, w_in_s, w_out_s = refs[:7]
    gain_ffn_hbm, qt_hbm, lctx_hbm, x_hbm, out_hbm = refs[7:12]
    raw_s, rn_s, rk_s, rv_s, ctx_s, out_s, qt_s, lctx_s, x_s, gain_ffn_ref, sems, out_sems = refs[12:]
    steps, width, block = qt_s.shape
    remote = rn_s.shape[1]
    slots = remote // REMOTE_SENSORS
    count = [0]

    def fetch(src, dst):
        copy = pltpu.make_async_copy(src, dst, sems.at[count[0]])
        count[0] += 1
        copy.start()
        return copy

    score_in = [fetch(qt_hbm, qt_s)]
    merge_in = [fetch(lctx_hbm, lctx_s)]
    ffn_in = [fetch(x_hbm, x_s), fetch(gain_ffn_hbm, gain_ffn_ref)]

    order = swap16() if split else None
    lane_head = lax.broadcasted_iota(jnp.int32, (1, 128), 1) // HEAD
    heads = [(lane_head == h).astype(BF16) for h in range(128 // HEAD)]
    none = jnp.zeros((remote, 128), BF16)
    to_lanes = (
        lax.broadcasted_iota(jnp.int32, (2 * H, width), 1) // HEAD
        == lax.broadcasted_iota(jnp.int32, (2 * H, width), 0) % H
    ).astype(BF16)
    slot = lax.broadcasted_iota(jnp.int32, (remote, block), 0) // REMOTE_SENSORS
    live = jnp.zeros((remote, block), jnp.int32)
    for j in range(slots):
        live = jnp.where(slot == j, numbers_ref[1 + slots + j], live)
    live = live > 0

    if split:
        for j in range(slots):
            raw_s[j * REMOTE_SENSORS : (j + 1) * REMOTE_SENSORS] = in_ref[numbers_ref[1 + j]]
        for b in range(remote // 16):
            rows = raw_s[b * 16 : (b + 1) * 16].reshape(256, width)
            rn_s[:, b * 16 : (b + 1) * 16, :] = dot(order, rows).astype(BF16).reshape(16, 16, width)
        raw = rn_s[...]
    else:
        raw = in_ref[...]
    normed = rms(raw.reshape(steps * remote, width).astype(F32), gain_ref[...])
    kv = dot(normed, wkv_ref[...]).astype(BF16)
    rk_s[...] = kv[:, :width].reshape(steps, remote, width)
    rv_s[...] = kv[:, width:].reshape(steps, remote, width)

    def by_head(rows):
        spread = []
        for h in range(H):
            half = h * HEAD // 128
            part = rows[:, half * 128 : (half + 1) * 128] * heads[h % (128 // HEAD)]
            spread.append(jnp.concatenate([part, none] if half == 0 else [none, part], axis=1))
        return jnp.concatenate(spread, axis=0)

    for copy in score_in:
        copy.wait()
    def score(t):
        return dot(by_head(rk_s[t]), qt_s[t]).reshape(H, remote, block)

    def weigh(t, scores):
        masked = jnp.where(live[None], scores, NEG)
        ltop = stat_ref[t, :H]
        top = jnp.maximum(jnp.max(masked, axis=1), ltop)
        e = jnp.exp2((masked - top[:, None, :]) * SCALE)
        keep = jnp.exp2((ltop - top) * SCALE)
        inverse = 1.0 / (jnp.sum(e, axis=1) + stat_ref[t, H:] * keep)
        keep = keep * inverse
        high = keep.astype(BF16).astype(F32)
        factors = jnp.concatenate([high, keep - high], axis=0).astype(BF16).T
        return factors, (e * inverse[:, None, :]).astype(BF16).reshape(H * remote, block).T

    def merge(t, factors, weights):
        if t == 0:
            for copy in merge_in:
                copy.wait()
        far = dot(weights, by_head(rv_s[t]))
        ctx_s[t] = (lctx_s[t].astype(F32) * dot(factors, to_lanes) + far).astype(BF16)

    upcoming, waiting = score(0), None
    for t in range(steps):
        scores, upcoming = upcoming, score(t + 1) if t + 1 < steps else None
        weighed = (t, *weigh(t, scores))
        if waiting:
            merge(*waiting)
        waiting = weighed
    merge(*waiting)

    for copy in ffn_in:
        copy.wait()
    tile = width
    tiles = w_in_s.shape[1] // tile
    work = [(first, n) for first in range(0, block, sb) for n in range(tiles)]
    ready, total, copies = {}, {}, []

    def open_rows(first):
        x = x_s[:, first : first + sb, :].reshape(steps * sb, width)
        context = ctx_s[:, first : first + sb, :].reshape(steps * sb, width)
        after = x.astype(F32) + dot(context, wo_s[...])
        total[first] = after
        ready[first] = rms(after, 0.5 * gain_ffn_ref[...])

    def up(first, n):
        return dot(ready[first], w_in_s[:, n * tile : (n + 1) * tile])

    open_rows(0)
    upper = up(*work[0])
    for k, (first, n) in enumerate(work):
        if n == 0 and first + sb < block:
            open_rows(first + sb)
        later = up(*work[k + 1]) if k + 1 < len(work) else None
        total[first] = total[first] + dot(gelu_of_half(upper).astype(BF16), w_out_s[n * tile : (n + 1) * tile, :])
        upper = later
        if n < tiles - 1:
            continue
        y = total[first].astype(BF16).reshape(steps, sb, width)
        if not split:
            out_s[:, first : first + sb, :] = y
            continue
        for b in range(sb // 16):
            turned = dot(order, y[:, b * 16 : (b + 1) * 16].reshape(256, width)).astype(BF16)
            out_s[first + b * 16 : first + (b + 1) * 16] = turned.reshape(16, steps, width)
        half = block // 2
        owner = numbers_ref[0] if first < half else 1 - numbers_ref[0]
        place = out_hbm.at[pl.ds(owner * half + first % half, sb)]
        copies.append(pltpu.make_async_copy(out_s.at[pl.ds(first, sb)], place, out_sems.at[first // sb]))
        copies[-1].start()
    if not split:
        copies.append(pltpu.make_async_copy(out_s, out_hbm, out_sems.at[0]))
        copies[-1].start()
    for copy in copies:
        copy.wait()


def finish(numbers, incoming, local, gain, wkv, wo, gain_ffn, w_in, w_out, split):
    x, qt, lctx, stat = local
    steps, width, block = qt.shape
    remote = (numbers.shape[0] - 1) // 2 * REMOTE_SENSORS
    sb = 32
    hbm = pl.BlockSpec(memory_space=pl.ANY)
    near = [incoming, gain, wkv, stat, wo, w_in, w_out]
    pin = lambda arrays: [pltpu.with_memory_space_constraint(a, pltpu.HBM) for a in arrays]
    vmem = pl.BlockSpec(memory_space=pltpu.VMEM)
    buffer = lambda *shape: pltpu.VMEM(shape, BF16)
    return pl.pallas_call(
        functools.partial(finish_kernel, split, sb),
        out_shape=jax.ShapeDtypeStruct((block, steps, width) if split else (steps, block, width), BF16),
        in_specs=[pl.BlockSpec(memory_space=pltpu.SMEM)] + [vmem] * len(near) + [hbm] * 4,
        out_specs=hbm,
        scratch_shapes=[
            buffer(remote, steps, width),
            buffer(steps, remote, width),
            buffer(steps, remote, width),
            buffer(steps, remote, width),
            buffer(steps, block, width),
            buffer(block, steps, width) if split else buffer(steps, block, width),
            buffer(steps, width, block),
            buffer(steps, block, width),
            buffer(steps, block, width),
            pltpu.VMEM(gain_ffn.shape, F32),
            pltpu.SemaphoreType.DMA((4,)),
            pltpu.SemaphoreType.DMA((block // sb,)),
        ],
        compiler_params=pltpu.CompilerParams(vmem_limit_bytes=VMEM_LIMIT),
        cost_estimate=pl.CostEstimate(
            flops=steps * block * width * width * 18, bytes_accessed=steps * block * width * 12, transcendentals=0
        ),
        name="remote_keys_and_feed_forward",
    )(numbers, *near, *pin([gain_ffn, qt, lctx, x]))


def local(
    tm,
    tokens,
    gain_time,
    wq_time,
    wkv_time,
    wo_time,
    gain_graph,
    wq_graph,
    wkv_graph,
    wo_graph,
    gain_ffn,
    w_in,
    w_out,
    neighbour_blocks,
    slot_used_mask,
    neighbour_rows,
):
    sensors_here, steps, width = tokens.shape
    block = sensors_here * tm
    group = steps // tm
    block_count, slots = neighbour_blocks.shape
    split = tm == 2 and group == 16 and sensors_here % 32 == 0
    gain_time, gain_graph, gain_ffn = (g.reshape(1, width) for g in (gain_time, gain_graph, gain_ffn))
    mine = lax.axis_index("tm").astype(jnp.int32)
    block_index = lax.axis_index("sensor")
    time = lambda x, *where: time_block(x, mine.reshape(1), gain_time, wq_time, wkv_time, wo_time, *where)
    if split:
        kept, got = [], []
        first = 0
        for share in SHARES:
            size = sensors_here * share // sum(SHARES)
            keep, send = time(tokens, first, size, True)
            tokens, send = lax.optimization_barrier((tokens, send))
            kept.append(keep)
            got.append(lax.ppermute(send, "tm", [(0, 1), (1, 0)]))
            first += size
        pieces = kept + got
    else:
        whole = lax.all_to_all(time(tokens, 0, sensors_here, False), "tm", split_axis=1, concat_axis=0, tiled=True)
        pieces = [whole.transpose(1, 0, 2)]
    matches = (neighbour_blocks == block_index).astype(jnp.int32)
    wanted = jnp.sum(matches[:, :, None] * neighbour_rows, axis=1).reshape(-1)
    own = lax.dynamic_index_in_dim(neighbour_blocks, block_index, 0, keepdims=False)
    numbers = jnp.concatenate([mine.reshape(1), own, slot_used_mask[0]])
    if split:
        outgoing = pick_rows((wanted + (tm - mine) * sensors_here) % block, pieces)
    else:
        outgoing = jnp.take(whole, wanted, axis=0)
    outgoing = outgoing.reshape(block_count, REMOTE_SENSORS, group, width)
    incoming = lax.all_to_all(outgoing, "sensor", split_axis=0, concat_axis=0, tiled=True)
    if not split:
        incoming = jnp.take(incoming, own, axis=0).reshape(-1, group, width).transpose(1, 0, 2)
    near = local_part(pieces, gain_graph, wq_graph, wkv_graph, split)
    out = finish(numbers, incoming, near, gain_graph, wkv_graph, wo_graph, gain_ffn, w_in, w_out, split)
    return out if split else out.transpose(1, 0, 2)


def solution(mesh):
    in_specs = (
        P(("sensor", "tm"), None, None),
        P(),
        P(),
        P(),
        P(),
        P(),
        P(),
        P(),
        P(),
        P(),
        P(),
        P(),
        P(),
        P("sensor", None),
        P(),
    )
    out_specs = P("sensor", "tm", None)
    body = functools.partial(local, mesh.shape["tm"])
    return jax.shard_map(body, mesh=mesh, in_specs=in_specs, out_specs=out_specs, check_vma=False)
```

```python
import functools
import math

import jax
import jax.numpy as jnp
from jax import lax
from jax.experimental import pallas as pl
from jax.experimental.pallas import tpu as pltpu
from jax.sharding import PartitionSpec as P

H = 8
HEAD = 32
REMOTE_SENSORS = 4
EPSILON = 1e-06
NEG = -1e30
SCALE = math.log2(math.e) / math.sqrt(HEAD)
SHARES = (1, 1, 1, 1)
F32 = jnp.float32
BF16 = jnp.bfloat16
VMEM_LIMIT = 28 * 1024 * 1024


def dot(a, b):
    return jnp.dot(a, b, preferred_element_type=F32)


def dot_nt(a, b):
    return lax.dot_general(a, b, (((1,), (1,)), ((), ())), preferred_element_type=F32)


def dot_tn(a, b):
    return lax.dot_general(a, b, (((0,), (0,)), ((), ())), preferred_element_type=F32)


def rms(x, gain):
    inverse = lax.rsqrt(jnp.mean(x * x, axis=-1, keepdims=True) + EPSILON)
    return (x * inverse * gain).astype(BF16)


def swap16():
    row = lax.broadcasted_iota(jnp.int32, (256, 256), 0)
    col = lax.broadcasted_iota(jnp.int32, (256, 256), 1)
    return (col == ((row & 15) << 4) + (row >> 4)).astype(BF16)


def head_rows(rows, lanes, head_of_row, first_head):
    row = lax.broadcasted_iota(jnp.int32, (rows, lanes), 0)
    lane = lax.broadcasted_iota(jnp.int32, (rows, lanes), 1)
    return (lane // HEAD + first_head == row // head_of_row).astype(BF16)


def time_kernel(split, my_ref, x_ref, gain_ref, wq_ref, wkv_ref, wo_ref, *refs):
    if split:
        keep_ref, send_ref, q_s, k_s, v_s, a_s, c_s, after_s = refs
    else:
        out_ref, q_s, k_s, v_s, a_s, c_s = refs
    sensors, steps, width = x_ref.shape
    rows = sensors * steps
    x = x_ref[...].reshape(rows, width).astype(F32)
    normed = rms(x, gain_ref[...])
    q_s[...] = dot(normed, wq_ref[...]).astype(BF16)
    kv = dot(normed, wkv_ref[...]).astype(BF16)
    k_s[...] = kv[:, :width]
    v_s[...] = kv[:, width:]
    lanes = H * steps
    near = 128 // HEAD
    span = near * steps
    mask = head_rows(span, 128, steps, 0)
    none = jnp.zeros((span, 128), BF16)
    key_t = lax.broadcasted_iota(jnp.int32, (steps, lanes), 0)
    query_t = lax.broadcasted_iota(jnp.int32, (steps, lanes), 1) & (steps - 1)
    causal = key_t <= query_t
    for s in range(sensors):
        here = slice(s * steps, (s + 1) * steps)
        first, second = (jnp.concatenate([q_s[here, c : c + 128]] * near, axis=0) * mask for c in (0, 128))
        spread = jnp.concatenate(
            [jnp.concatenate([first, none], axis=1), jnp.concatenate([none, second], axis=1)], axis=0
        )
        scores = jnp.where(causal, dot_nt(k_s[here, :], spread), NEG)
        top = jnp.max(scores, axis=0, keepdims=True)
        e = jnp.exp2((scores - top) * SCALE)
        a_s[here, :] = (e * (1.0 / jnp.sum(e, axis=0, keepdims=True))).astype(BF16)
    lane_head = lax.broadcasted_iota(jnp.int32, (steps, 128), 1) // HEAD
    for g in range(rows // 128):
        turned = a_s[g * 128 : (g + 1) * 128, :].T
        for half in range(2):
            cols = slice(half * 128, (half + 1) * 128)
            for s in range(0, 128 // steps, 2):
                columns = []
                for r in (s, s + 1):
                    v = v_s[g * 128 + r * steps : g * 128 + (r + 1) * steps, cols]
                    parts = [jnp.zeros((r * steps, 128), BF16), v, jnp.zeros((128 - (r + 1) * steps, 128), BF16)]
                    columns.append(jnp.concatenate([p for p in parts if p.shape[0]], axis=0))
                wide = dot(turned[half * span : (half + 1) * span], jnp.concatenate(columns, axis=1))
                for i in range(2):
                    ctx = wide[:steps, i * 128 : (i + 1) * 128]
                    for h in range(1, near):
                        ctx = jnp.where(lane_head == h, wide[h * steps : (h + 1) * steps, i * 128 : (i + 1) * 128], ctx)
                    at = g * 128 + (s + i) * steps
                    c_s[at : at + steps, cols] = ctx.astype(BF16)
    after = (x + dot(c_s[...], wo_ref[...])).astype(BF16)
    if not split:
        out_ref[...] = after.reshape(sensors, steps, width)
        return
    after_s[...] = after.reshape(sensors, steps, width)
    mine = my_ref[0]
    for ref, part in ((keep_ref, mine), (send_ref, 1 - mine)):
        ref[...] = after_s[:, pl.ds(pl.multiple_of(part * 16, 16), 16), :]


def time_block(tokens, my, gain, wq, wkv, wo, first, count, split):
    steps, width = tokens.shape[1:]
    if first == 0:
        tokens, gain, wq, wkv, wo = (pltpu.with_memory_space_constraint(a, pltpu.HBM) for a in (tokens, gain, wq, wkv, wo))
    sb = min(16, count)
    rows = sb * steps
    full = lambda a: pl.BlockSpec(a.shape, lambda i, *_: (0,) * a.ndim)
    if split:
        out_shape = [jax.ShapeDtypeStruct((count, 16, width), BF16)] * 2
        out_specs = [pl.BlockSpec((sb, 16, width), lambda i, *_: (i, 0, 0))] * 2
        extra = [pltpu.VMEM((sb, steps, width), BF16)]
    else:
        out_shape = jax.ShapeDtypeStruct((count, steps, width), BF16)
        out_specs = pl.BlockSpec((sb, steps, width), lambda i, *_: (i, 0, 0))
        extra = []
    return pl.pallas_call(
        functools.partial(time_kernel, split),
        out_shape=out_shape,
        grid_spec=pltpu.PrefetchScalarGridSpec(
            num_scalar_prefetch=1,
            grid=(count // sb,),
            in_specs=[
                pl.BlockSpec((sb, steps, width), lambda i, *_: (first // sb + i, 0, 0)),
                full(gain),
                full(wq),
                full(wkv),
                full(wo),
            ],
            out_specs=out_specs,
            scratch_shapes=[pltpu.VMEM((rows, width), BF16)] * 5 + extra,
        ),
        compiler_params=pltpu.CompilerParams(vmem_limit_bytes=VMEM_LIMIT),
        cost_estimate=pl.CostEstimate(
            flops=count * steps * width * width * 12, bytes_accessed=count * steps * width * 4, transcendentals=0
        ),
        name="time_block",
    )(my, tokens, gain, wq, wkv, wo)


def pick_kernel(n, wanted_ref, *refs):
    pieces, (out_hbm, x_s, out_s, sems) = refs[:n], refs[n:]
    place = 0
    for p in pieces:
        x_s[place : place + p.shape[0]] = p[...]
        place += p.shape[0]
    copies = []
    for b in range(out_s.shape[0] // 16):
        for j in range(b * 16, (b + 1) * 16):
            out_s[j] = x_s[wanted_ref[j]]
        here = pl.ds(b * 16, 16)
        copies.append(pltpu.make_async_copy(out_s.at[here], out_hbm.at[here], sems.at[b]))
        copies[-1].start()
    for copy in copies:
        copy.wait()


def pick_rows(wanted, pieces):
    _, steps, width = pieces[0].shape
    count = wanted.shape[0]
    block = sum(p.shape[0] for p in pieces)
    return pl.pallas_call(
        functools.partial(pick_kernel, len(pieces)),
        out_shape=pltpu.HBM((count, steps, width), BF16),
        in_specs=[pl.BlockSpec(memory_space=pltpu.SMEM)] + [pl.BlockSpec(memory_space=pltpu.VMEM)] * len(pieces),
        out_specs=pl.BlockSpec(memory_space=pl.ANY),
        scratch_shapes=[
            pltpu.VMEM((block, steps, width), BF16),
            pltpu.VMEM((count, steps, width), BF16),
            pltpu.SemaphoreType.DMA((count // 16,)),
        ],
        compiler_params=pltpu.CompilerParams(vmem_limit_bytes=VMEM_LIMIT),
        name="pick_rows",
    )(wanted, *pieces)


def pair_scores(q, k, masks, pair):
    cols = slice(pair // 2 * 128, pair // 2 * 128 + 128)
    spread = jnp.concatenate([q[:, cols]] * 2, axis=0) * masks[pair % 2]
    return dot_nt(k[:, cols], spread)


def local_kernel(n, split, *refs):
    pieces = refs[:n]
    gain_ref, wq_ref, wkv_ref, x_ref, qt_ref, ctx_ref, stat_ref, wqt_s, wvt_s = refs[n:]
    tb, width, block = qt_ref.shape

    @pl.when(pl.program_id(0) == 0)
    def _():
        wvt_s[...] = wkv_ref[:, width:].T
        place = 0
        if not split:
            x_ref[...] = pieces[0][...]
        for p in pieces if split else []:
            for b in range(0, p.shape[0], 16):
                turned = dot(swap16(), p[b : b + 16].reshape(256, width)).astype(BF16)
                x_ref[:, place + b : place + b + 16, :] = turned.reshape(16, 16, width)
            place += p.shape[0]
        wqt_s[...] = wq_ref[...].T

    x = x_ref[pl.ds(pl.program_id(0) * tb, tb)].reshape(tb * block, width).astype(F32)
    normed = rms(x, gain_ref[...])
    q = dot(normed, wq_ref[...]).astype(BF16)
    k = dot(normed, wkv_ref[:, :width]).astype(BF16)
    masks = [head_rows(2 * block, 128, block, -2 * p) for p in range(2)]
    for t in range(tb):
        here = slice(t * block, (t + 1) * block)
        qt_ref[t] = dot_nt(wqt_s[...], normed[here]).astype(BF16)
        vt = dot_nt(wvt_s[...], normed[here]).astype(BF16)
        scores = [pair_scores(q[here], k[here], masks, pair) for pair in range(H // 2)]
        tops = [jnp.max(x, axis=0, keepdims=True) for x in scores]
        es = [jnp.exp2((x - top) * SCALE) for x, top in zip(scores, tops)]
        context = []
        for pair, e in enumerate(es):
            lo = pair * 2 * HEAD
            both = dot(vt[lo : lo + 2 * HEAD], e.astype(BF16))
            total = jnp.sum(e, axis=0, keepdims=True)
            for i in range(2):
                lanes = slice(i * block, (i + 1) * block)
                head = 2 * pair + i
                context.append(both[i * HEAD : (i + 1) * HEAD, lanes].astype(BF16))
                stat_ref[t, head : head + 1, :] = tops[pair][:, lanes]
                stat_ref[t, H + head : H + head + 1, :] = total[:, lanes]
        ctx_ref[t] = jnp.concatenate(context, axis=0).T


def local_part(pieces, gain, wq, wkv, split):
    sensors, steps = (0, 1) if split else (1, 0)
    steps, width = pieces[0].shape[steps], pieces[0].shape[2]
    block = sum(p.shape[sensors] for p in pieces)
    tb = 4
    full = lambda a: pl.BlockSpec(a.shape, lambda i: (0,) * a.ndim)
    per_t = lambda *shape: pl.BlockSpec((tb,) + shape, lambda i: (i, 0, 0))
    return pl.pallas_call(
        functools.partial(local_kernel, len(pieces), split),
        out_shape=[
            pltpu.HBM((steps, block, width), BF16),
            pltpu.HBM((steps, width, block), BF16),
            pltpu.HBM((steps, block, width), BF16),
            jax.ShapeDtypeStruct((steps, 2 * H, block), F32),
        ],
        grid=(steps // tb,),
        in_specs=[full(p) for p in pieces] + [full(gain), full(wq), full(wkv)],
        out_specs=[
            pl.BlockSpec((steps, block, width), lambda i: (0, 0, 0)),
            per_t(width, block),
            per_t(block, width),
            per_t(2 * H, block),
        ],
        scratch_shapes=[pltpu.VMEM((width, width), BF16)] * 2,
        compiler_params=pltpu.CompilerParams(vmem_limit_bytes=VMEM_LIMIT),
        cost_estimate=pl.CostEstimate(
            flops=steps * block * width * width * 12, bytes_accessed=steps * block * width * 10, transcendentals=0
        ),
        name="local_keys",
    )(*pieces, gain, wq, wkv)


def gelu_of_half(x):
    inner = x * (1.5957691216057308 + 0.28541926509040096 * (x * x))
    return x + x * jnp.tanh(inner)


def finish_kernel(split, sb, numbers_ref, *refs):
    in_ref, gain_ref, wkv_ref, stat_ref, wo_s, w_in_s, w_out_s = refs[:7]
    gain_ffn_hbm, qt_hbm, lctx_hbm, x_hbm, out_hbm = refs[7:12]
    raw_s, rn_s, rk_s, rv_s, ctx_s, out_s, qt_s, lctx_s, x_s, gain_ffn_ref, sems, out_sems = refs[12:]
    steps, width, block = qt_s.shape
    remote = rn_s.shape[1]
    slots = remote // REMOTE_SENSORS
    count = [0]

    def fetch(src, dst):
        copy = pltpu.make_async_copy(src, dst, sems.at[count[0]])
        count[0] += 1
        copy.start()
        return copy

    score_in = [fetch(qt_hbm, qt_s)]
    merge_in = [fetch(lctx_hbm, lctx_s)]
    ffn_in = [fetch(x_hbm, x_s), fetch(gain_ffn_hbm, gain_ffn_ref)]

    order = swap16() if split else None
    lane_head = lax.broadcasted_iota(jnp.int32, (1, 128), 1) // HEAD
    heads = [(lane_head == h).astype(BF16) for h in range(128 // HEAD)]
    none = jnp.zeros((remote, 128), BF16)
    to_lanes = (
        lax.broadcasted_iota(jnp.int32, (2 * H, width), 1) // HEAD
        == lax.broadcasted_iota(jnp.int32, (2 * H, width), 0) % H
    ).astype(BF16)
    slot = lax.broadcasted_iota(jnp.int32, (remote, block), 0) // REMOTE_SENSORS
    live = jnp.zeros((remote, block), jnp.int32)
    for j in range(slots):
        live = jnp.where(slot == j, numbers_ref[1 + slots + j], live)
    live = live > 0

    if split:
        for j in range(slots):
            raw_s[j * REMOTE_SENSORS : (j + 1) * REMOTE_SENSORS] = in_ref[numbers_ref[1 + j]]
        for b in range(remote // 16):
            rows = raw_s[b * 16 : (b + 1) * 16].reshape(256, width)
            rn_s[:, b * 16 : (b + 1) * 16, :] = dot(order, rows).astype(BF16).reshape(16, 16, width)
        raw = rn_s[...]
    else:
        raw = in_ref[...]
    normed = rms(raw.reshape(steps * remote, width).astype(F32), gain_ref[...])
    kv = dot(normed, wkv_ref[...]).astype(BF16)
    rk_s[...] = kv[:, :width].reshape(steps, remote, width)
    rv_s[...] = kv[:, width:].reshape(steps, remote, width)

    def by_head(rows):
        spread = []
        for h in range(H):
            half = h * HEAD // 128
            part = rows[:, half * 128 : (half + 1) * 128] * heads[h % (128 // HEAD)]
            spread.append(jnp.concatenate([part, none] if half == 0 else [none, part], axis=1))
        return jnp.concatenate(spread, axis=0)

    for copy in score_in:
        copy.wait()
    def score(t):
        return dot(by_head(rk_s[t]), qt_s[t]).reshape(H, remote, block)

    def weigh(t, scores):
        masked = jnp.where(live[None], scores, NEG)
        ltop = stat_ref[t, :H]
        top = jnp.maximum(jnp.max(masked, axis=1), ltop)
        e = jnp.exp2(masked * SCALE - (top * SCALE)[:, None, :])
        keep = jnp.exp2((ltop - top) * SCALE)
        inverse = 1.0 / (jnp.sum(e, axis=1) + stat_ref[t, H:] * keep)
        keep = keep * inverse
        high = keep.astype(BF16).astype(F32)
        factors = jnp.concatenate([high, keep - high], axis=0).astype(BF16).T
        return factors, (e * inverse[:, None, :]).astype(BF16).reshape(H * remote, block).T

    def merge(t, factors, weights):
        if t == 0:
            for copy in merge_in:
                copy.wait()
        far = dot(weights, by_head(rv_s[t]))
        ctx_s[t] = (lctx_s[t].astype(F32) * dot(factors, to_lanes) + far).astype(BF16)

    upcoming, waiting = score(0), None
    for t in range(steps):
        scores, upcoming = upcoming, score(t + 1) if t + 1 < steps else None
        weighed = (t, *weigh(t, scores))
        if waiting:
            merge(*waiting)
        waiting = weighed
    merge(*waiting)

    for copy in ffn_in:
        copy.wait()
    tile = width
    tiles = w_in_s.shape[1] // tile
    work = [(first, n) for first in range(0, block, sb) for n in range(tiles)]
    ready, total, copies = {}, {}, []

    def open_rows(first):
        x = x_s[:, first : first + sb, :].reshape(steps * sb, width)
        context = ctx_s[:, first : first + sb, :].reshape(steps * sb, width)
        after = x.astype(F32) + dot(context, wo_s[...])
        total[first] = after
        ready[first] = rms(after, 0.5 * gain_ffn_ref[...])

    def up(first, n):
        return dot(ready[first], w_in_s[:, n * tile : (n + 1) * tile])

    open_rows(0)
    upper = up(*work[0])
    for k, (first, n) in enumerate(work):
        if n == 0 and first + sb < block:
            open_rows(first + sb)
        later = up(*work[k + 1]) if k + 1 < len(work) else None
        total[first] = total[first] + dot(gelu_of_half(upper).astype(BF16), w_out_s[n * tile : (n + 1) * tile, :])
        upper = later
        if n < tiles - 1:
            continue
        y = total[first].astype(BF16).reshape(steps, sb, width)
        if not split:
            out_s[:, first : first + sb, :] = y
            continue
        for b in range(sb // 16):
            turned = dot(order, y[:, b * 16 : (b + 1) * 16].reshape(256, width)).astype(BF16)
            out_s[first + b * 16 : first + (b + 1) * 16] = turned.reshape(16, steps, width)
        half = block // 2
        owner = numbers_ref[0] if first < half else 1 - numbers_ref[0]
        place = out_hbm.at[pl.ds(owner * half + first % half, sb)]
        copies.append(pltpu.make_async_copy(out_s.at[pl.ds(first, sb)], place, out_sems.at[first // sb]))
        copies[-1].start()
    if not split:
        copies.append(pltpu.make_async_copy(out_s, out_hbm, out_sems.at[0]))
        copies[-1].start()
    for copy in copies:
        copy.wait()


def finish(numbers, incoming, local, gain, wkv, wo, gain_ffn, w_in, w_out, split):
    x, qt, lctx, stat = local
    steps, width, block = qt.shape
    remote = (numbers.shape[0] - 1) // 2 * REMOTE_SENSORS
    sb = 32
    hbm = pl.BlockSpec(memory_space=pl.ANY)
    near = [incoming, gain, wkv, stat, wo, w_in, w_out]
    pin = lambda arrays: [pltpu.with_memory_space_constraint(a, pltpu.HBM) for a in arrays]
    vmem = pl.BlockSpec(memory_space=pltpu.VMEM)
    buffer = lambda *shape: pltpu.VMEM(shape, BF16)
    return pl.pallas_call(
        functools.partial(finish_kernel, split, sb),
        out_shape=jax.ShapeDtypeStruct((block, steps, width) if split else (steps, block, width), BF16),
        in_specs=[pl.BlockSpec(memory_space=pltpu.SMEM)] + [vmem] * len(near) + [hbm] * 4,
        out_specs=hbm,
        scratch_shapes=[
            buffer(remote, steps, width),
            buffer(steps, remote, width),
            buffer(steps, remote, width),
            buffer(steps, remote, width),
            buffer(steps, block, width),
            buffer(block, steps, width) if split else buffer(steps, block, width),
            buffer(steps, width, block),
            buffer(steps, block, width),
            buffer(steps, block, width),
            pltpu.VMEM(gain_ffn.shape, F32),
            pltpu.SemaphoreType.DMA((4,)),
            pltpu.SemaphoreType.DMA((block // sb,)),
        ],
        compiler_params=pltpu.CompilerParams(vmem_limit_bytes=VMEM_LIMIT),
        cost_estimate=pl.CostEstimate(
            flops=steps * block * width * width * 18, bytes_accessed=steps * block * width * 12, transcendentals=0
        ),
        name="remote_keys_and_feed_forward",
    )(numbers, *near, *pin([gain_ffn, qt, lctx, x]))


def local(
    tm,
    tokens,
    gain_time,
    wq_time,
    wkv_time,
    wo_time,
    gain_graph,
    wq_graph,
    wkv_graph,
    wo_graph,
    gain_ffn,
    w_in,
    w_out,
    neighbour_blocks,
    slot_used_mask,
    neighbour_rows,
):
    sensors_here, steps, width = tokens.shape
    block = sensors_here * tm
    group = steps // tm
    block_count, slots = neighbour_blocks.shape
    split = tm == 2 and group == 16 and sensors_here % 32 == 0
    gain_time, gain_graph, gain_ffn = (g.reshape(1, width) for g in (gain_time, gain_graph, gain_ffn))
    mine = lax.axis_index("tm").astype(jnp.int32)
    block_index = lax.axis_index("sensor")
    time = lambda x, *where: time_block(x, mine.reshape(1), gain_time, wq_time, wkv_time, wo_time, *where)
    if split:
        kept, got = [], []
        first = 0
        for share in SHARES:
            size = sensors_here * share // sum(SHARES)
            keep, send = time(tokens, first, size, True)
            tokens, send = lax.optimization_barrier((tokens, send))
            kept.append(keep)
            got.append(lax.ppermute(send, "tm", [(0, 1), (1, 0)]))
            first += size
        pieces = kept + got
    else:
        whole = lax.all_to_all(time(tokens, 0, sensors_here, False), "tm", split_axis=1, concat_axis=0, tiled=True)
        pieces = [whole.transpose(1, 0, 2)]
    matches = (neighbour_blocks == block_index).astype(jnp.int32)
    wanted = jnp.sum(matches[:, :, None] * neighbour_rows, axis=1).reshape(-1)
    own = lax.dynamic_index_in_dim(neighbour_blocks, block_index, 0, keepdims=False)
    numbers = jnp.concatenate([mine.reshape(1), own, slot_used_mask[0]])
    if split:
        outgoing = pick_rows((wanted + (tm - mine) * sensors_here) % block, pieces)
    else:
        outgoing = jnp.take(whole, wanted, axis=0)
    outgoing = outgoing.reshape(block_count, REMOTE_SENSORS, group, width)
    incoming = lax.all_to_all(outgoing, "sensor", split_axis=0, concat_axis=0, tiled=True)
    if not split:
        incoming = jnp.take(incoming, own, axis=0).reshape(-1, group, width).transpose(1, 0, 2)
    near = local_part(pieces, gain_graph, wq_graph, wkv_graph, split)
    out = finish(numbers, incoming, near, gain_graph, wkv_graph, wo_graph, gain_ffn, w_in, w_out, split)
    return out if split else out.transpose(1, 0, 2)


def solution(mesh):
    in_specs = (
        P(("sensor", "tm"), None, None),
        P(),
        P(),
        P(),
        P(),
        P(),
        P(),
        P(),
        P(),
        P(),
        P(),
        P(),
        P(),
        P("sensor", None),
        P(),
    )
    out_specs = P("sensor", "tm", None)
    body = functools.partial(local, mesh.shape["tm"])
    return jax.shard_map(body, mesh=mesh, in_specs=in_specs, out_specs=out_specs, check_vma=False)
```
